32 devices in a mesh: groups: 2 (over x), seq: 16 (over z, y, core).
Axes of the slice: x: 2, y: 2, z: 4, core: 2. Of those that a mesh axis runs over, the one named last changes fastest.
Arguments:
- frames: bfloat16 [4096, 1024], P(('groups', 'seq')), parts along dimension 0, may hold values from -6 to 6
- conv_kernel: bfloat16 [31, 1024], replicated, may hold values from -1 to 1
- norm_gain: bfloat16 [1024], replicated, may hold values from 0.25 to 1.75
- router: bfloat16 [1024, 8], replicated, may hold values from -0.1875 to 0.1875
- expert_in: bfloat16 [16, 1024, 1024], P('seq'), may hold values from -0.1875 to 0.1875
- expert_out: bfloat16 [16, 1024, 1024], P('seq'), may hold values from -0.125 to 0.125
- expert_ids: int32 [4096, 2], P(('groups', 'seq')), parts along dimension 0, may hold values from 0 to 7, all different within a row; in each aligned block of 128 rows (0 to 127, 128 to 255, ...) at most 64 rows name the same one
- out_grad: bfloat16 [4096, 1024], P(('groups', 'seq')), parts along dimension 0, may hold values from -6 to 6
Outputs:
- block_out: bfloat16 [4096, 1024], P(('groups', 'seq')), parts along dimension 0
- frames_grad: bfloat16 [4096, 1024], P(('groups', 'seq')), parts along dimension 0
- kernel_grad: float32 [62, 1024], P('groups'), parts along dimension 0
- gain_grad: float32 [2048], P('groups'), parts along dimension 0
- router_grad: float32 [2048, 8], P('groups'), parts along dimension 0
- expert_in_grad: bfloat16 [32, 1024, 1024], P(('groups', 'seq')), parts along dimension 0
- expert_out_grad: bfloat16 [32, 1024, 1024], P(('groups', 'seq')), parts along dimension 0
The draws below stay inside these ranges and needn't reach their ends.
There are 2 independent parts, one for each index of `groups`. The reference program is written for one: setup_inputs(seed, part) draws one part's arguments, and reference() takes and returns one part's arrays. A program takes and returns all parts, laid end to end along the dimension named above; an argument that names none is the same for every part. Nothing has to cross between parts.
Inputs may be any that keep to these rules, and one draw needn't show every extreme that they name: `expert_ids`: within the rows of one device (128 frames), no expert is named more than 64 times, a bound that some block reaches; a frame's two experts differ.
All inputs are finite; a program needn't handle non-finite values.
Results may differ from the reference program's by a relative error of at most 0.0079.
Values may be sent and summed in bfloat16 or wider, within the bound.
No kernel may reach another device: no remote copies, remote signals or barrier semaphores. Data moves between devices by JAX's collectives and lax.ppermute only.
A program may use at most 128 MiB of HBM per device.

```python
import math
import jax
import jax.numpy as jnp
import numpy as np
from jax import lax

D = 1024
HIDDEN_SIZE = 2048
KSIZE = 31
TOK_DEV = 128
FRAMES = 2048
EXPERTS = 8
SLOTS = 16
HALF = 1024
CAP = 64
N_SEQ = 16


def level_of(stream_key, extent, shards, least, top_value):
    def one(position, parts):
        draws = jax.random.uniform(jax.random.fold_in(jax.random.fold_in(stream_key, 6), position), (parts,), jnp.float32, least / len(shards), top_value / len(shards))
        return jnp.repeat(jnp.exp(draws), extent[position] // parts).reshape((-1,) + (1,) * (len(extent) - position - 1))

    factor_of = one(*shards[0])
    for cut in shards[1:]:
        factor_of = factor_of * one(*cut)
    return factor_of


def shared_out(own_key, own, number, rows, count, top, most, skew):
    ranking = jax.random.permutation(own_key, count)
    packed, usual = load_shares(count, rows * top, most, skew, True), load_shares(count, rows * top, most, skew, False)
    places = jnp.arange(count)

    def named(tallies, turn):
        used = int((tallies > 0).sum())
        fixed = max(1, used // 4)
        moved = fixed + (places - fixed + turn * (used - fixed)) % max(1, count - fixed)
        return jnp.zeros((count,), jnp.int32).at[ranking[jnp.where(places < fixed, places, moved)]].set(jnp.asarray(tallies, jnp.int32))

    tallies = jnp.where(number % 4 == 0, named(packed, number // 4), named(usual, number - number // 4 - 1))
    mixed = jax.random.permutation(jax.random.fold_in(own, 3), count)
    donor, receiver = mixed[0:count // 2 * 2:2], mixed[1:count // 2 * 2:2]
    margin = jnp.minimum(tallies[donor] - 1, most - tallies[receiver]) // 2
    margin = jnp.where((donor == ranking[0]) | (receiver == ranking[0]) | (tallies[receiver] == 0), 0, jnp.maximum(margin, 0))
    moved = jax.random.randint(jax.random.fold_in(own, 4), (count // 2,), 0, 1 << 20) % (margin + 1)
    tallies = tallies.at[donor].add(-moved).at[receiver].add(moved)
    members = jnp.searchsorted(jnp.cumsum(tallies), jnp.arange(rows * top), side="right").astype(jnp.int32)
    table = members.reshape(top, rows).T
    table = table[jax.random.permutation(jax.random.fold_in(own, 1), rows)]
    turn = jax.random.randint(jax.random.fold_in(own, 2), (rows, 1), 0, top)
    return jnp.take_along_axis(table, (jnp.arange(top)[None, :] + turn) % top, axis=1)


def load_shares(count, total, most, slope, full):
    weights = [(1 << 20) // math.isqrt(grade ** slope) + 1 for grade in range(1, count + 1)]
    largest = most if full else min(most, max(-(-total // count), total * weights[0] // sum(weights)))
    least = 1 if total - largest >= count - 1 else 0
    holding, surplus = [largest] + [least] * (count - 1), total - largest - least * (count - 1)
    while surplus > 0:
        free = [i for i in range(1, count) if holding[i] < largest] or [i for i in range(1, count) if holding[i] < most]
        mass, budget = sum([weights[i] for i in free]), surplus
        for i in free:
            more = min(most - holding[i], max(1, budget * weights[i] // mass), surplus)
            holding[i] = holding[i] + more
            surplus = surplus - more
    return np.array(holding)


def noise(rng, dims, deviation, limit, cuts=(), kind=jnp.bfloat16):
    drawn = deviation * jax.random.normal(rng, dims, jnp.float32)
    if cuts:
        drawn = drawn * level_of(rng, dims, cuts, -0.22, 0.18)
    return jnp.clip(drawn, -limit, limit).astype(kind)


def setup_inputs(seed: int = 0, part: int = 0) -> dict:
    keys = jax.random.split(jax.random.key(seed), 9)
    part_keys = jax.random.split(jax.random.fold_in(keys[8], part), 9)
    frames = noise(part_keys[0], (FRAMES, D), 1.0, 6.0, ((0, 16),))
    conv_kernel = noise(keys[1], (KSIZE, D), KSIZE ** -0.5, 1.0)
    norm_gain = jnp.clip(1.0 + 0.15 * jax.random.normal(keys[2], (D,), jnp.float32), 0.25, 1.75).astype(jnp.bfloat16)
    router = noise(keys[3], (D, EXPERTS), D ** -0.5, 0.1875)
    expert_in = noise(keys[4], (SLOTS, D, HALF), D ** -0.5, 0.1875, ((0, 16),))
    expert_out = noise(keys[5], (SLOTS, HALF, D), HIDDEN_SIZE ** -0.5, 0.125, ((0, 16),))
    expert_ids_keys = jax.random.split(jax.random.fold_in(part_keys[6], 1), FRAMES // TOK_DEV)
    expert_ids_turns = jax.random.permutation(jax.random.fold_in(part_keys[6], 3), FRAMES // TOK_DEV)
    expert_ids = jax.vmap(lambda own, number: shared_out(jax.random.fold_in(part_keys[6], 2), own, number, TOK_DEV, EXPERTS, 2, CAP, 2))(expert_ids_keys, expert_ids_turns).reshape((FRAMES, 2))
    out_grad = noise(part_keys[7], (FRAMES, D), 1.0, 6.0, ((0, 16),))
    return {"frames": frames, "conv_kernel": conv_kernel, "norm_gain": norm_gain, "router": router, "expert_in": expert_in, "expert_out": expert_out, "expert_ids": expert_ids, "out_grad": out_grad}


norm_eps = 1e-05

def swish_slope(values):
    logistic = jax.nn.sigmoid(values)
    return logistic * (1.0 + values * (1.0 - logistic))

def reference(frames, conv_kernel, norm_gain, router, expert_in, expert_out, expert_ids, out_grad):
    f32 = jnp.float32
    bf16 = jnp.bfloat16
    rim_size = (KSIZE - 1) // 2
    padded = jnp.pad(frames.astype(f32), ((rim_size, rim_size), (0, 0)))
    kernel_taps = conv_kernel.astype(f32)
    conv_out = jnp.zeros((FRAMES, D), f32)
    for offset in range(KSIZE):
        conv_out = conv_out + kernel_taps[offset] * padded[offset:offset + FRAMES]
    conv_gate = jax.nn.sigmoid(conv_out)
    mixed = frames.astype(f32) + conv_out * conv_gate
    inverse = lax.rsqrt(lax.optimization_barrier(jnp.mean(mixed * mixed, axis=-1, keepdims=True)) + norm_eps)
    normed = (mixed * inverse * norm_gain.astype(f32)).astype(bf16)
    logits = jnp.dot(normed, router, preferred_element_type=f32)
    onehot = (expert_ids[:, :, None] == jnp.arange(EXPERTS, dtype=jnp.int32)[None, None, :]).astype(f32)
    chosen = lax.optimization_barrier(jnp.sum(onehot * logits[:, None, :], axis=-1))
    gate_values = jax.nn.sigmoid(chosen)
    upstream = out_grad.astype(f32)
    grad_rows = (gate_values[:, :, None] * upstream[:, None, :]).astype(bf16).reshape(2 * FRAMES, D)
    flat_ids = expert_ids.reshape(-1)
    most_rows = N_SEQ * CAP
    normed_ext = jnp.concatenate([normed, jnp.zeros((1, D), bf16)], axis=0)
    grad_ext = jnp.concatenate([grad_rows, jnp.zeros((1, D), bf16)], axis=0)

    def one_expert(expert):
        picks = jnp.nonzero(flat_ids == expert, size=most_rows, fill_value=2 * FRAMES)[0].astype(jnp.int32)
        rows_in = normed_ext[picks // 2]
        rows_grad = grad_ext[picks]
        out_sum = jnp.zeros((most_rows, D), f32)
        back_sum = jnp.zeros((most_rows, D), f32)
        grads_in = []
        grads_out = []
        for half_index in range(2):
            slot = 2 * expert + half_index
            weight_in = expert_in[slot]
            weight_out = expert_out[slot]
            pre_act = jnp.dot(rows_in, weight_in, preferred_element_type=f32)
            active = jax.nn.silu(pre_act).astype(bf16)
            part_out = jnp.dot(active, weight_out, preferred_element_type=f32).astype(bf16)
            back_hidden = jnp.dot(rows_grad, weight_out.T, preferred_element_type=f32)
            pre_grad = (back_hidden * swish_slope(pre_act)).astype(bf16)
            grads_out.append(jnp.dot(active.T, rows_grad, preferred_element_type=f32).astype(bf16))
            grads_in.append(jnp.dot(rows_in.T, pre_grad, preferred_element_type=f32).astype(bf16))
            part_in = jnp.dot(pre_grad, weight_in.T, preferred_element_type=f32).astype(bf16)
            out_sum = out_sum + part_out.astype(f32)
            back_sum = back_sum + part_in.astype(f32)
        out_round = lax.optimization_barrier(out_sum.astype(bf16))
        back_round = lax.optimization_barrier(back_sum.astype(bf16))
        return (picks, out_round, back_round, jnp.stack(grads_in), jnp.stack(grads_out))
    picks, out_sum, back_sum, grads_in, grads_out = lax.map(one_expert, jnp.arange(EXPERTS, dtype=jnp.int32))
    flat_picks = picks.reshape(-1)
    expert_result = jnp.zeros((2 * FRAMES + 1, D), f32).at[flat_picks].add(out_sum.reshape(-1, D).astype(f32))
    expert_result = expert_result[:2 * FRAMES].reshape(FRAMES, 2, D)
    expert_back = jnp.zeros((2 * FRAMES + 1, D), f32).at[flat_picks].add(back_sum.reshape(-1, D).astype(f32))
    expert_back = lax.optimization_barrier(jnp.sum(expert_back[:2 * FRAMES].reshape(FRAMES, 2, D), axis=1))
    block_out = (mixed + lax.optimization_barrier(jnp.sum(gate_values[:, :, None] * expert_result, axis=1))).astype(bf16)
    grad_gate = lax.optimization_barrier(jnp.sum(upstream[:, None, :] * expert_result, axis=-1))
    grad_chosen = grad_gate * gate_values * (1.0 - gate_values)
    grad_logits = lax.optimization_barrier(jnp.sum(onehot * grad_chosen[:, :, None], axis=1)).astype(bf16)
    router_grad = jnp.dot(normed.T, grad_logits, preferred_element_type=f32)
    grad_normed = expert_back + jnp.dot(grad_logits, router.T, preferred_element_type=f32)
    gain_grad = lax.optimization_barrier(jnp.sum(grad_normed * mixed * inverse, axis=0))
    scaled = grad_normed * norm_gain.astype(f32)
    grad_mixed = upstream + inverse * scaled - mixed * inverse ** 3 * lax.optimization_barrier(jnp.mean(scaled * mixed, axis=-1, keepdims=True))
    grad_conv = (grad_mixed * swish_slope(conv_out)).astype(bf16)
    conv_padded = jnp.pad(grad_conv.astype(f32), ((rim_size, rim_size), (0, 0)))
    frames_grad = grad_mixed
    kernel_rows = []
    for offset in range(KSIZE):
        start = 2 * rim_size - offset
        frames_grad = frames_grad + kernel_taps[offset] * conv_padded[start:start + FRAMES]
        kernel_rows.append(lax.optimization_barrier(jnp.sum(grad_conv.astype(f32) * padded[offset:offset + FRAMES], axis=0)))
    kernel_grad = jnp.stack(kernel_rows)
    expert_in_grad = grads_in.reshape(SLOTS, D, HALF)
    expert_out_grad = grads_out.reshape(SLOTS, HALF, D)
    return (block_out, frames_grad.astype(bf16), kernel_grad, gain_grad, router_grad, expert_in_grad, expert_out_grad)
```

```python
import functools

import jax
import jax.numpy as jnp
from jax import lax
from jax.experimental import pallas as pl
from jax.experimental.pallas import tpu as pltpu
from jax.sharding import PartitionSpec as P

KSIZE = 31
RIM = 16
LANES = 128
NORM_EPS = 1e-05
F32 = jnp.float32
BF16 = jnp.bfloat16
LAST = (((1,), (1,)), ((), ()))
FIRST = (((0,), (0,)), ((), ()))
VMEM_LIMIT = 32 * 1024 * 1024


def dot(a, b):
    return jnp.dot(a, b, preferred_element_type=F32)


def dot_last(a, b):
    return lax.dot_general(a, b, LAST, preferred_element_type=F32)


def dot_first(a, b):
    return lax.dot_general(a, b, FIRST, preferred_element_type=F32)


def slope_of(values):
    logistic = jax.nn.sigmoid(values)
    return logistic * (1.0 + values * (1.0 - logistic))


def kernel_call(body, out_shape, scratch=(), flops=0, moved=0):
    return pl.pallas_call(
        body,
        out_shape=out_shape,
        scratch_shapes=list(scratch),
        compiler_params=pltpu.CompilerParams(vmem_limit_bytes=VMEM_LIMIT),
        cost_estimate=pl.CostEstimate(flops=flops, bytes_accessed=moved, transcendentals=0),
    )


def choices(ids, experts):
    lane = lax.broadcasted_iota(jnp.int32, (ids.shape[0], experts), 1)
    return (ids[:, 0:1] == lane).astype(F32), (ids[:, 1:2] == lane).astype(F32)


def placements(ids, experts, capacity):
    count = ids.shape[0]
    first, second = choices(ids, experts)
    named = (first + second).astype(BF16)
    row = lax.broadcasted_iota(jnp.int32, (count, count), 0)
    col = lax.broadcasted_iota(jnp.int32, (count, count), 1)
    before = dot((col < row).astype(BF16), named)
    start = lax.broadcasted_iota(jnp.int32, (count, experts), 1).astype(F32) * capacity
    place = before + start
    slot = lax.broadcasted_iota(jnp.int32, (count, experts * capacity), 1)
    picks = []
    for chosen in (first, second):
        at = jnp.sum(chosen * place, axis=1, keepdims=True).astype(jnp.int32)
        picks.append((slot == at).astype(BF16))
    return picks


def pack_kernel(experts, capacity, ids_ref, rows_ref, out_ref):
    first, second = placements(ids_ref[...], experts, capacity)
    out_ref[...] = dot_first(first + second, rows_ref[...]).astype(BF16)


def shifted(pad_ref, lanes, count):
    for rest in range(8):
        block = pad_ref[pl.ds(rest, count + 24), lanes]
        for turn in range(4):
            offset = 8 * turn + rest
            if 1 <= offset <= KSIZE:
                yield offset, block[8 * turn : 8 * turn + count]


def fill_padded(pad_ref, left_ref, mid_ref, right_ref):
    count = mid_ref.shape[0]
    pad_ref[0:RIM, :] = left_ref[...].astype(F32)
    pad_ref[RIM : RIM + count, :] = mid_ref[...].astype(F32)
    pad_ref[RIM + count : 2 * RIM + count, :] = right_ref[...].astype(F32)


def lane_loop(width, body):
    @pl.loop(0, width // LANES)
    def _(step):
        body(pl.ds(pl.multiple_of(step * LANES, LANES), LANES))


def front_kernel(
    experts, capacity, frames_ref, left_ref, right_ref, taps_ref, gain_ref, router_ref, ids_ref,
    conv_ref, mixed_ref, inverse_ref, normed_ref, gates_ref, payload_ref, pad_ref, taps32_ref, square_ref,
):
    count, width = frames_ref.shape
    fill_padded(pad_ref, left_ref, frames_ref, right_ref)
    taps32_ref[...] = taps_ref[...].astype(F32)
    square_ref[...] = jnp.zeros_like(square_ref)

    def conv(lanes):
        total = jnp.zeros((count, LANES), F32)
        for offset, rows in shifted(pad_ref, lanes, count):
            total = total + taps32_ref[offset - 1 : offset, lanes] * rows
        conv_ref[:, lanes] = total
        mixed = pad_ref[RIM : RIM + count, lanes] + total * jax.nn.sigmoid(total)
        mixed_ref[:, lanes] = mixed
        square_ref[...] += mixed * mixed

    lane_loop(width, conv)
    mean = jnp.sum(square_ref[...], axis=1, keepdims=True) / width
    inverse = lax.rsqrt(mean + NORM_EPS)
    inverse_ref[...] = inverse
    normed = (mixed_ref[...] * inverse * gain_ref[...].astype(F32)).astype(BF16)
    normed_ref[...] = normed
    gates_ref[...] = jax.nn.sigmoid(dot(normed, router_ref[...]))
    first, second = placements(ids_ref[...], experts, capacity)
    payload_ref[...] = dot_first(first + second, normed).astype(BF16)


def result_kernel(
    experts, capacity, rows_ref, ids_ref, mixed_ref, grad_ref, normed_ref, gates_ref,
    out_ref, logits_ref, router_ref,
):
    ids = ids_ref[...]
    gates = gates_ref[...]
    upstream = grad_ref[...].astype(F32)
    total = mixed_ref[...]
    added = jnp.zeros_like(total)
    grad_logits = jnp.zeros(gates.shape, F32)
    for pick, chosen in zip(placements(ids, experts, capacity), choices(ids, experts)):
        result = dot(pick, rows_ref[...])
        gate = jnp.sum(chosen * gates, axis=1, keepdims=True)
        added = added + gate * result
        grad_gate = jnp.sum(upstream * result, axis=1, keepdims=True)
        grad_logits = grad_logits + chosen * (grad_gate * gate * (1.0 - gate))
    out_ref[...] = (total + added).astype(BF16)
    grad_logits = grad_logits.astype(BF16)
    logits_ref[...] = grad_logits
    router_ref[...] = dot_first(grad_logits, normed_ref[...])


def back_kernel(
    experts, capacity, rows_ref, ids_ref, logits_ref, router_ref, mixed_ref, inverse_ref, conv_ref, grad_ref, gain_ref,
    mixed_grad_ref, conv_grad_ref, head_ref, tail_ref, gain_out_ref,
):
    count, width = mixed_ref.shape
    first, second = placements(ids_ref[...], experts, capacity)
    grad_normed = dot(first + second, rows_ref[...]) + dot_last(logits_ref[...], router_ref[...])
    mixed = mixed_ref[...]
    inverse = inverse_ref[...]
    gain_out_ref[...] = jnp.sum(grad_normed * mixed * inverse, axis=0, keepdims=True)
    scaled = grad_normed * gain_ref[...].astype(F32)
    mean = jnp.sum(scaled * mixed, axis=1, keepdims=True) / width
    mixed_grad = grad_ref[...].astype(F32) + inverse * scaled - mixed * (inverse * inverse * inverse * mean)
    mixed_grad_ref[...] = mixed_grad
    conv_grad = (mixed_grad * slope_of(conv_ref[...])).astype(BF16)
    conv_grad_ref[...] = conv_grad
    head_ref[...] = conv_grad[0:RIM]
    tail_ref[...] = conv_grad[count - RIM : count]


def taps_kernel(frames_ref, left_ref, right_ref, conv_grad_ref, gain_ref, router_ref, out_ref, pad_ref):
    count, width = frames_ref.shape
    fill_padded(pad_ref, left_ref, frames_ref, right_ref)

    def reduce(lanes):
        grad = conv_grad_ref[:, lanes].astype(F32)
        for offset, rows in shifted(pad_ref, lanes, count):
            out_ref[offset - 1 : offset, lanes] = jnp.sum(grad * rows, axis=0, keepdims=True)

    lane_loop(width, reduce)
    out_ref[KSIZE : KSIZE + 1, :] = gain_ref[...]
    out_ref[KSIZE + 1 :, :] = router_ref[...]


def frames_kernel(mixed_grad_ref, conv_grad_ref, left_ref, right_ref, taps_ref, out_ref, pad_ref, taps32_ref):
    count, width = mixed_grad_ref.shape
    fill_padded(pad_ref, left_ref, conv_grad_ref, right_ref)
    taps32_ref[...] = taps_ref[...].astype(F32)

    def conv(lanes):
        total = mixed_grad_ref[:, lanes]
        for offset, rows in shifted(pad_ref, lanes, count):
            total = total + taps32_ref[KSIZE - offset : KSIZE - offset + 1, lanes] * rows
        out_ref[:, lanes] = total.astype(BF16)

    lane_loop(width, conv)


def rims(head, tail, count):
    ends = count - 1
    left = lax.ppermute(tail, "seq", [(i, i + 1) for i in range(ends)])
    right = lax.ppermute(head, "seq", [(i + 1, i) for i in range(ends)])
    return left, right


def swap(values, count, bit):
    return lax.ppermute(values, "seq", [(i, i ^ bit) for i in range(count)])


def exchange(payload, count):
    groups = [[2 * chip + core for chip in range(count // 2)] for core in range(2)]
    return lax.all_to_all(payload, "seq", 0, 0, axis_index_groups=groups, tiled=True)


def per_device(frames, conv_kernel, norm_gain, router, expert_in, expert_out, expert_ids, out_grad):
    count, width = frames.shape
    devices = lax.axis_size("seq")
    experts = devices // 2
    capacity = 8 * count // devices
    slots = experts * capacity
    gain = norm_gain.reshape(1, width)
    taps = conv_kernel
    shape = jax.ShapeDtypeStruct
    pad = pltpu.VMEM((count + 2 * RIM, width), F32)
    taps32 = pltpu.VMEM((KSIZE, width), F32)

    grad_payload = kernel_call(
        functools.partial(pack_kernel, experts, capacity), shape((slots, width), BF16), moved=1 << 21
    )(expert_ids, out_grad)
    grads = exchange(grad_payload, devices)
    left, right = rims(frames[0:RIM], frames[count - RIM : count], devices)
    weight_in, weight_out = expert_in[0], expert_out[0]
    other_out = swap(weight_out, devices, 1)
    other_in = swap(weight_in, devices, 1)

    conv_out, mixed, inverse, normed, gates, payload = kernel_call(
        functools.partial(front_kernel, experts, capacity),
        (
            shape((count, width), F32),
            shape((count, width), F32),
            shape((count, 1), F32),
            shape((count, width), BF16),
            shape((count, experts), F32),
            shape((slots, width), BF16),
        ),
        (pad, taps32, pltpu.VMEM((count, LANES), F32)),
        moved=1 << 22,
    )(frames, left, right, taps, gain, router, expert_ids)
    rows = exchange(payload, devices)

    hidden = [dot_last(grads, weight) for weight in (weight_out, other_out)]
    mine = (jnp.arange(experts, dtype=jnp.int32) == lax.axis_index("seq") // 2).astype(F32)
    gate = jax.nn.sigmoid(jnp.sum(dot(rows, router) * mine[None, :], axis=1, keepdims=True))
    grad_rows = (gate * grads.astype(F32)).astype(BF16)
    pre_act = [dot(rows, weight) for weight in (weight_in, other_in)]
    active = [jax.nn.silu(values).astype(BF16) for values in pre_act]
    part_out = (dot(active[0], weight_out) + dot(active[1], other_out)).astype(BF16)
    results = exchange(part_out, devices)
    pre_grad = [(gate * h * slope_of(values)).astype(BF16) for h, values in zip(hidden, pre_act)]
    part_in = (dot_last(pre_grad[0], weight_in) + dot_last(pre_grad[1], other_in)).astype(BF16)
    backs = exchange(part_in, devices)
    far_rows, far_grads, far_active, far_pre = [
        swap(values, devices, 1) for values in (rows, grad_rows, active[1], pre_grad[1])
    ]
    expert_out_grad = (dot_first(active[0], grad_rows) + dot_first(far_active, far_grads)).astype(BF16)
    expert_in_grad = (dot_first(rows, pre_grad[0]) + dot_first(far_rows, far_pre)).astype(BF16)

    block_out, grad_logits, router_local = kernel_call(
        functools.partial(result_kernel, experts, capacity),
        (shape((count, width), BF16), shape((count, experts), BF16), shape((experts, width), F32)),
        moved=1 << 22,
    )(results, expert_ids, mixed, out_grad, normed, gates)
    mixed_grad, conv_grad, head, tail, gain_local = kernel_call(
        functools.partial(back_kernel, experts, capacity),
        (
            shape((count, width), F32),
            shape((count, width), BF16),
            shape((RIM, width), BF16),
            shape((RIM, width), BF16),
            shape((1, width), F32),
        ),
        moved=1 << 22,
    )(backs, expert_ids, grad_logits, router, mixed, inverse, conv_out, out_grad, gain)
    grad_left, grad_right = rims(head, tail, devices)
    local = kernel_call(
        taps_kernel, shape((KSIZE + 1 + experts, width), F32), (pad,), moved=1 << 20
    )(frames, left, right, conv_grad, gain_local, router_local)
    frames_grad = kernel_call(
        frames_kernel, shape((count, width), BF16), (pad, taps32), moved=1 << 20
    )(mixed_grad, conv_grad, grad_left, grad_right, taps)
    bit = 1
    while bit < devices:
        local = local + swap(local, devices, bit)
        bit *= 2
    return (
        block_out,
        frames_grad,
        local[0:KSIZE],
        local[KSIZE],
        local[KSIZE + 1 :].T,
        expert_in_grad[None],
        expert_out_grad[None],
    )


def solution(mesh):
    in_specs = (
        P(("groups", "seq"), None),
        P(),
        P(),
        P(),
        P("seq", None, None),
        P("seq", None, None),
        P(("groups", "seq"), None),
        P(("groups", "seq"), None),
    )
    out_specs = (
        P(("groups", "seq"), None),
        P(("groups", "seq"), None),
        P("groups", None),
        P("groups"),
        P("groups", None),
        P(("groups", "seq"), None, None),
        P(("groups", "seq"), None, None),
    )
    return jax.shard_map(
        per_device, mesh=mesh, in_specs=in_specs, out_specs=out_specs, check_vma=False
    )
```

```python
import functools

import jax
import jax.numpy as jnp
from jax import lax
from jax.experimental import pallas as pl
from jax.experimental.pallas import tpu as pltpu
from jax.sharding import PartitionSpec as P

KSIZE = 31
RIM = 16
LANES = 128
CHUNK = 256
NORM_EPS = 1e-05
F32 = jnp.float32
BF16 = jnp.bfloat16
LAST = (((1,), (1,)), ((), ()))
FIRST = (((0,), (0,)), ((), ()))
SMALL = 12 * 1024 * 1024
LARGE = 28 * 1024 * 1024


def dot(a, b):
    return jnp.dot(a, b, preferred_element_type=F32)


def dot_last(a, b):
    return lax.dot_general(a, b, LAST, preferred_element_type=F32)


def dot_first(a, b):
    return lax.dot_general(a, b, FIRST, preferred_element_type=F32)


def slope_of(values):
    logistic = jax.nn.sigmoid(values)
    return logistic * (1.0 + values * (1.0 - logistic))


class Staged:
    def __init__(self, source, held, semaphore):
        self.held, self.copy, self.waited = held, pltpu.make_async_copy(source, held, semaphore), False
        self.shape = held.shape
        self.copy.start()

    def wait(self):
        if not self.waited:
            self.copy.wait()
        self.waited = True

    def __getitem__(self, at):
        self.wait()
        return self.held[at]


def kernel_call(body, operands, outs, scratch=(), flops=0, moved=1 << 22, limit=SMALL, scalars=()):
    count, out_count = len(operands), len(outs)
    staged = [place for place in range(count) if place not in scalars]
    held = [pltpu.VMEM(operands[place].shape, operands[place].dtype) for place in staged]
    results = [pltpu.VMEM(out.shape, out.dtype) for out in outs]

    def kernel(*refs):
        ins, out_refs, rest = refs[0:count], refs[count : count + out_count], refs[count + out_count :]
        copies, made, rest = rest[0 : len(staged)], rest[len(staged) : len(staged) + out_count], rest[len(staged) + out_count :]
        in_semaphores, out_semaphores, rest = rest[0], rest[1], rest[2:]
        values = list(ins)
        for turn, place in enumerate(staged):
            values[place] = Staged(ins[place], copies[turn], in_semaphores.at[turn])
        writes = [
            pltpu.make_async_copy(buffer, out, out_semaphores.at[turn])
            for turn, (buffer, out) in enumerate(zip(made, out_refs))
        ]
        started = []

        def write(*turns):
            for turn in turns:
                writes[turn].start()
                started.append(turn)

        body(values, made, rest, write)
        for value in values:
            if isinstance(value, Staged):
                value.wait()
        write(*[turn for turn in range(out_count) if turn not in started])
        for copy in writes:
            copy.wait()

    return pl.pallas_call(
        kernel,
        out_shape=tuple(outs),
        in_specs=[pl.BlockSpec(memory_space=pltpu.SMEM if place in scalars else pl.ANY) for place in range(count)],
        out_specs=tuple(pl.BlockSpec(memory_space=pl.ANY) for _ in outs),
        scratch_shapes=held + results + [pltpu.SemaphoreType.DMA((len(staged),)), pltpu.SemaphoreType.DMA((out_count,))] + list(scratch),
        compiler_params=pltpu.CompilerParams(vmem_limit_bytes=limit),
        cost_estimate=pl.CostEstimate(flops=1, bytes_accessed=1, transcendentals=0),
    )(*operands)


def columns_of(ids):
    count = ids.shape[1]
    row = lax.broadcasted_iota(jnp.int32, (count, count), 0)
    col = lax.broadcasted_iota(jnp.int32, (count, count), 1)
    return dot_last((row == col).astype(BF16), ids.astype(F32).astype(BF16)).astype(jnp.int32)


def choices(ids, experts):
    lane = lax.broadcasted_iota(jnp.int32, (ids.shape[0], experts), 1)
    return (ids[:, 0:1] == lane).astype(F32), (ids[:, 1:2] == lane).astype(F32)


def placements(ids, chip, near, capacity):
    count = ids.shape[0]
    first, second = choices(ids ^ chip, near)
    named = (first + second).astype(BF16)
    row = lax.broadcasted_iota(jnp.int32, (count, count), 0)
    col = lax.broadcasted_iota(jnp.int32, (count, count), 1)
    before = dot((col < row).astype(BF16), named)
    start = lax.broadcasted_iota(jnp.int32, (count, near), 1).astype(F32) * capacity
    place = before + start + 1.0
    slot = lax.broadcasted_iota(jnp.int32, (count, near * capacity), 1)
    picks = []
    for chosen in (first, second):
        at = jnp.sum(chosen * place, axis=1, keepdims=True).astype(jnp.int32) - 1
        picks.append((slot == at).astype(BF16))
    return picks


def pack_kernel(near, capacity, ins, outs, scratch, write):
    chip, ids, far, rows, far_rows = ins
    count = rows.shape[0]
    blocks = ((ids[...], rows), (far_ids_of(far, count), far_rows))
    for block, (names, source) in enumerate(blocks):
        first, second = placements(columns_of(names), chip[0], near, capacity)
        packed = dot_first(first + second, source[0:count, :]).astype(BF16)
        for place, out in enumerate(outs):
            out[block * capacity : (block + 1) * capacity, :] = packed[place * capacity : (place + 1) * capacity]


def far_ids_of(far, count):
    return far[count : count + RIM, 0:count][0:2].astype(F32).astype(jnp.int32)


def block_rows(refs, block, capacity):
    return jnp.concatenate([ref[block * capacity : (block + 1) * capacity, :] for ref in refs], axis=0)


def shifted(pad_ref, lanes, count):
    for rest in range(8):
        block = pad_ref[pl.ds(rest, count + 24), lanes]
        for turn in range(4):
            offset = 8 * turn + rest
            if 1 <= offset <= KSIZE:
                yield offset, block[8 * turn : 8 * turn + count]


def fill_padded(pad_ref, left_ref, mid_ref, right_ref):
    count = mid_ref.shape[0]
    pad_ref[0:RIM, :] = left_ref[...].astype(F32)
    pad_ref[RIM : RIM + count, :] = mid_ref[...].astype(F32)
    pad_ref[RIM + count : 2 * RIM + count, :] = right_ref[...].astype(F32)


def lane_loop(width, body):
    @pl.loop(0, width // LANES)
    def _(step):
        body(pl.ds(pl.multiple_of(step * LANES, LANES), LANES))


def front_kernel(ins, outs, scratch, write):
    frames, left, right, taps, gain = ins
    conv_ref, normed_ref = outs
    pad_ref, taps32_ref, mixed_ref, square_ref = scratch
    count, width = frames.shape
    fill_padded(pad_ref, left, frames, right)
    taps32_ref[...] = taps[...].astype(F32)
    square_ref[...] = jnp.zeros_like(square_ref)

    def conv(lanes):
        total = jnp.zeros((count, LANES), F32)
        for offset, rows in shifted(pad_ref, lanes, count):
            total = total + taps32_ref[offset - 1 : offset, lanes] * rows
        conv_ref[:, lanes] = total
        mixed = pad_ref[RIM : RIM + count, lanes] + total * jax.nn.sigmoid(total)
        mixed_ref[:, lanes] = mixed
        square_ref[...] += mixed * mixed

    lane_loop(width, conv)
    write(0)
    mean = jnp.sum(square_ref[...], axis=1, keepdims=True) / width
    inverse = lax.rsqrt(mean + NORM_EPS)
    normed_ref[...] = (mixed_ref[...] * inverse * gain[...].astype(F32)).astype(BF16)


def result_kernel(near, capacity, ins, outs, scratch, write):
    chip, ids, upstream_near, normed_near, far, normed_far, router = ins[0:7]
    rows_refs = ins[7:]
    near_ref, far_ref, near_logits_ref, far_logits_ref, router_out_ref = outs
    count = upstream_near.shape[0]
    router_out = jnp.zeros(router_out_ref.shape, F32)
    blocks = ((ids[...], upstream_near, normed_near), (far_ids_of(far, count), far, normed_far))
    for block, (names, grad, normed) in reversed(list(enumerate(blocks))):
        names = columns_of(names)
        upstream = grad[0:count, :].astype(F32)
        normed = normed[...]
        gates = jax.nn.sigmoid(dot_last(normed, router[...]))
        rows = block_rows(rows_refs, block, capacity)
        added = jnp.zeros(upstream.shape, F32)
        grad_logits = jnp.zeros(gates.shape, F32)
        for pick, chosen in zip(placements(names, chip[0], near, capacity), choices(names, gates.shape[1])):
            result = dot(pick, rows)
            gate = jnp.sum(chosen * gates, axis=1, keepdims=True)
            added = added + gate * result
            grad_gate = jnp.sum(upstream * result, axis=1, keepdims=True)
            grad_logits = grad_logits + chosen * (grad_gate * gate * (1.0 - gate))
        grad_logits = grad_logits.astype(BF16)
        (near_ref, far_ref)[block][...] = added.astype((F32, BF16)[block])
        write(block)
        (near_logits_ref, far_logits_ref)[block][...] = grad_logits
        router_out = router_out + dot_first(grad_logits, normed)
    router_out_ref[...] = router_out


def back_kernel(near, capacity, ins, outs, scratch, write):
    chip, ids, logits_near, far, logits_far, router = ins[0:6]
    rows_refs = ins[6:]
    count = outs[0].shape[0]
    blocks = ((ids[...], logits_near), (far_ids_of(far, count), logits_far))
    for block, (names, logits) in reversed(list(enumerate(blocks))):
        first, second = placements(columns_of(names), chip[0], near, capacity)
        total = dot(first + second, block_rows(rows_refs, block, capacity))
        outs[block][...] = (total + dot(logits[...], router[...])).astype(outs[block].dtype)
        write(block)


def half_lanes(core, width):
    return pl.ds(pl.multiple_of(core * (width // 2), LANES), width // 2)


def final_kernel(ins, outs, scratch, write):
    core, frames, left, right, conv, grad, gain, near_sum, far_sum, router, near_back, far_back = ins
    out_ref, mixed_grad_ref, conv_grad_ref, head_ref, tail_ref, kept_ref, given_ref = outs
    pad_ref, local_ref = scratch
    count, width = frames.shape
    fill_padded(pad_ref, left, frames, right)
    conv_out = conv[...]
    logistic = jax.nn.sigmoid(conv_out)
    mixed = frames[...].astype(F32) + conv_out * logistic
    inverse = lax.rsqrt(jnp.sum(mixed * mixed, axis=1, keepdims=True) / width + NORM_EPS)
    out_ref[...] = (mixed + (near_sum[...] + far_sum[...].astype(F32))).astype(BF16)
    write(0)
    local_ref[KSIZE + 1 :, :] = router[...]
    grad_normed = near_back[...] + far_back[...].astype(F32)
    local_ref[KSIZE : KSIZE + 1, :] = jnp.sum(grad_normed * mixed * inverse, axis=0, keepdims=True)
    scaled = grad_normed * gain[...].astype(F32)
    mean = jnp.sum(scaled * mixed, axis=1, keepdims=True) / width
    mixed_grad = grad[...].astype(F32) + inverse * scaled - mixed * (inverse * inverse * inverse * mean)
    mixed_grad_ref[...] = mixed_grad
    conv_grad = (mixed_grad * (logistic * (1.0 + conv_out * (1.0 - logistic)))).astype(BF16)
    conv_grad_ref[...] = conv_grad
    head_ref[...] = conv_grad[0:RIM]
    tail_ref[...] = conv_grad[count - RIM : count]
    write(1, 2, 3, 4)

    def reduce(lanes):
        grad = conv_grad_ref[:, lanes].astype(F32)
        for offset, rows in shifted(pad_ref, lanes, count):
            local_ref[offset - 1 : offset, lanes] = jnp.sum(grad * rows, axis=0, keepdims=True)

    lane_loop(width, reduce)
    kept_ref[...] = local_ref[:, half_lanes(core[0], width)]
    given_ref[...] = local_ref[:, half_lanes(1 - core[0], width)]


def frames_kernel(ins, outs, scratch, write):
    mixed_grad, conv_grad, left, right, taps = ins
    (out_ref,), (pad_ref, taps32_ref) = outs, scratch
    count, width = mixed_grad.shape
    fill_padded(pad_ref, left, conv_grad, right)
    taps32_ref[...] = taps[...].astype(F32)
    mixed_grad.wait()

    def conv(lanes):
        total = mixed_grad[:, lanes]
        for offset, rows in shifted(pad_ref, lanes, count):
            total = total + taps32_ref[KSIZE - offset : KSIZE - offset + 1, lanes] * rows
        out_ref[:, lanes] = total.astype(BF16)

    lane_loop(width, conv)


def chunk_loop(width, body):
    @pl.loop(0, width // CHUNK)
    def _(step):
        body(pl.ds(pl.multiple_of(step * CHUNK, CHUNK), CHUNK))


def gather_rows(refs, rows_ref):
    each = refs[0].shape[0]
    for place, ref in enumerate(refs):
        rows_ref[place * each : (place + 1) * each, :] = ref[...]


def scatter_columns(refs, columns, values):
    each = refs[0].shape[0]
    for place, ref in enumerate(refs):
        ref[:, columns] = values[place * each : (place + 1) * each]


def forward_kernel(near, ins, outs, scratch, write):
    rows, (near_in, far_in, near_out, far_out) = ins[0:near], ins[near:]
    out_refs, (rows_ref, near_pre_ref, far_pre_ref, near_active_ref, far_active_ref) = outs[0:near], outs[near:]
    gather_rows(rows, rows_ref)
    write(near)
    for weight, pre, active in ((near_in, near_pre_ref, near_active_ref), (far_in, far_pre_ref, far_active_ref)):
        weight.wait()

        def inner(columns):
            values = dot(rows_ref[...], weight[:, columns])
            pre[:, columns] = values
            active[:, columns] = jax.nn.silu(values).astype(BF16)

        chunk_loop(weight.shape[1], inner)
    write(near + 1, near + 2, near + 3, near + 4)
    near_out.wait()
    far_out.wait()

    def outer(columns):
        total = dot(near_active_ref[...], near_out[:, columns])
        total = total + dot(far_active_ref[...], far_out[:, columns])
        scatter_columns(out_refs, columns, total.astype(BF16))

    chunk_loop(near_out.shape[1], outer)


def backward_kernel(near, ins, outs, scratch, write):
    grads, (rows, router, mine, near_out, far_out, near_pre, far_pre, near_in, far_in) = ins[0:near], ins[near:]
    out_refs, (near_grad_ref, far_grad_ref, grad_rows_ref) = outs[0:near], outs[near:]
    (grads_ref,) = scratch
    gather_rows(grads, grads_ref)
    logits = jnp.sum(dot_last(rows[...], router[...]) * mine[...], axis=1, keepdims=True)
    gate = jax.nn.sigmoid(logits)
    grad_rows_ref[...] = (gate * grads_ref[...].astype(F32)).astype(BF16)
    write(near + 2)
    for weight, pre, grad in ((near_out, near_pre, near_grad_ref), (far_out, far_pre, far_grad_ref)):
        weight.wait()
        pre.wait()

        def inner(columns):
            hidden = dot_last(grad_rows_ref[...], weight[columns, :])
            grad[:, columns] = (hidden * slope_of(pre[:, columns])).astype(BF16)

        chunk_loop(weight.shape[0], inner)
    write(near, near + 1)
    near_in.wait()
    far_in.wait()

    def outer(rows):
        total = dot_last(near_grad_ref[...], near_in[rows, :])
        total = total + dot_last(far_grad_ref[...], far_in[rows, :])
        scatter_columns(out_refs, rows, total.astype(BF16))

    chunk_loop(near_in.shape[0], outer)


def last_kernel(ins, outs, scratch, write):
    core, mine, other = ins
    taps_ref, gain_ref, router_ref = outs
    width = taps_ref.shape[1]
    for place, half in ((core[0], mine), (1 - core[0], other)):
        lanes = half_lanes(place, width)
        taps_ref[:, lanes] = half[0:KSIZE]
        gain_ref[:, lanes] = half[KSIZE : KSIZE + 1]
        router_ref[:, lanes] = half[KSIZE + 1 :]


def rims(head, tail, count):
    ends = count - 1
    left = lax.ppermute(tail, "seq", [(i, i + 1) for i in range(ends)])
    right = lax.ppermute(head, "seq", [(i + 1, i) for i in range(ends)])
    return left, right


def swap(values, count, bit):
    return lax.ppermute(values, "seq", [(i, i ^ bit) for i in range(count)])


def exchange(parts, devices):
    return [parts[0]] + [swap(part, devices, 2 * r) for r, part in enumerate(parts) if r]


def per_device(frames, conv_kernel, norm_gain, router, expert_in, expert_out, expert_ids, out_grad):
    count, width = frames.shape
    devices = lax.axis_size("seq")
    experts = devices // 2
    capacity = 8 * count // devices
    near = experts // 2
    slots = experts * capacity
    gain = norm_gain.reshape(1, width)
    taps = conv_kernel
    router = router.T
    ids = expert_ids.T
    shape = jax.ShapeDtypeStruct
    pad = pltpu.VMEM((count + 2 * RIM, width), F32)
    taps32 = pltpu.VMEM((KSIZE, width), F32)
    chip = lax.axis_index("seq") // 2
    chips = chip.reshape(1).astype(jnp.int32)
    mine = (jnp.arange(experts, dtype=jnp.int32) == chip).astype(F32).reshape(1, experts)
    cross = functools.partial(swap, count=devices, bit=devices // 2)

    named = jnp.pad(ids.astype(BF16), ((0, RIM - 2), (0, width - count)))
    far_grad = cross(jnp.concatenate([out_grad, named]))
    left, right = rims(frames[0:RIM], frames[count - RIM : count], devices)
    weight_in, weight_out = expert_in[0], expert_out[0]
    other_in = swap(weight_in, devices, 1)
    other_out = swap(weight_out, devices, 1)

    model32, model16 = shape((count, width), F32), shape((count, width), BF16)
    conv_out, normed = kernel_call(
        front_kernel,
        (frames, left, right, taps, gain),
        (model32, model16),
        (pad, taps32, pltpu.VMEM((count, width), F32), pltpu.VMEM((count, LANES), F32)),
    )
    far_normed = cross(normed)

    part = (shape((2 * capacity, width), BF16),) * near
    pack = functools.partial(pack_kernel, near, capacity)
    grads = exchange(
        kernel_call(pack, (chips, ids, far_grad, out_grad, far_grad), part, scalars=(0,)), devices
    )
    rows = exchange(
        kernel_call(pack, (chips, ids, far_grad, normed, far_normed), part, scalars=(0,)), devices
    )

    half = weight_in.shape[1]
    wide = shape((slots, half), F32)
    narrow = shape((slots, half), BF16)
    model = shape((slots, width), BF16)
    work = 8 * slots * width * half
    outs = kernel_call(
        functools.partial(forward_kernel, near),
        (*rows, weight_in, other_in, weight_out, other_out),
        part + (model, wide, wide, narrow, narrow),
        flops=work, moved=1 << 24, limit=LARGE,
    )
    parts_out, (all_rows, *pre_act), active = outs[0:near], outs[near : near + 3], outs[near + 3 :]
    results = exchange(parts_out, devices)
    outs = kernel_call(
        functools.partial(backward_kernel, near),
        (*grads, all_rows, router, mine, weight_out, other_out, *pre_act, weight_in, other_in),
        part + (narrow, narrow, model),
        (pltpu.VMEM((slots, width), BF16),),
        flops=work, moved=1 << 24, limit=LARGE,
    )
    results, all_rows, active, outs = lax.optimization_barrier((results, all_rows, active, outs))
    parts_in, pre_grad, grad_rows = outs[0:near], outs[near : near + 2], outs[near + 2]
    backs = exchange(parts_in, devices)
    far_rows, far_grads, far_active, far_pre = [
        swap(values, devices, 1) for values in (all_rows, grad_rows, active[1], pre_grad[1])
    ]
    expert_out_grad = (dot_first(active[0], grad_rows) + dot_first(far_active, far_grads)).astype(BF16)
    expert_in_grad = (dot_first(all_rows, pre_grad[0]) + dot_first(far_rows, far_pre)).astype(BF16)

    logits = shape((count, experts), BF16)
    near_sum, far_sum, near_logits, far_logits, router_local = kernel_call(
        functools.partial(result_kernel, near, capacity),
        (chips, ids, out_grad, normed, far_grad, far_normed, router, *results),
        (model32, model16, logits, logits, shape((experts, width), F32)),
        scalars=(0,),
    )
    far_sum = cross(far_sum)
    backs[1], far_sum = lax.optimization_barrier((backs[1], far_sum))
    near_back, far_back = kernel_call(
        functools.partial(back_kernel, near, capacity),
        (chips, ids, near_logits, far_grad, far_logits, router, *backs),
        (model32, model16),
        scalars=(0,),
    )
    far_back = cross(far_back)
    far_back, expert_in_grad, expert_out_grad = lax.optimization_barrier((far_back, expert_in_grad, expert_out_grad))

    rim = shape((RIM, width), BF16)
    lines = KSIZE + 1 + experts
    columns = shape((lines, width // 2), F32)
    core = (lax.axis_index("seq") % 2).reshape(1).astype(jnp.int32)
    block_out, mixed_grad, conv_grad, head, tail, kept, given = kernel_call(
        final_kernel,
        (core, frames, left, right, conv_out, out_grad, gain, near_sum, far_sum, router_local, near_back, far_back),
        (model16, model32, model16, rim, rim, columns, columns),
        (pad, pltpu.VMEM((lines, width), F32)),
        scalars=(0,),
    )
    grad_left, grad_right = rims(head, tail, devices)
    local = kept + swap(given, devices, 1)
    bit = 2
    while bit < devices:
        other = swap(local, devices, bit)
        if bit == 2:
            other, grad_left, grad_right = lax.optimization_barrier((other, grad_left, grad_right))
            (frames_grad,) = kernel_call(
                frames_kernel, (mixed_grad, conv_grad, grad_left, grad_right, taps), (model16,), (pad, taps32)
            )
        if bit == 4:
            other, frames_grad = lax.optimization_barrier((other, frames_grad))
        local = local + other
        bit *= 2
    kernel_grad, gain_grad, router_grad = kernel_call(
        last_kernel,
        (core, local, swap(local, devices, 1)),
        (shape((KSIZE, width), F32), shape((1, width), F32), shape((experts, width), F32)),
        scalars=(0,),
    )
    return (
        block_out,
        frames_grad,
        kernel_grad,
        gain_grad[0],
        router_grad.T,
        expert_in_grad[None],
        expert_out_grad[None],
    )


def solution(mesh):
    in_specs = (
        P(("groups", "seq"), None),
        P(),
        P(),
        P(),
        P("seq", None, None),
        P("seq", None, None),
        P(("groups", "seq"), None),
        P(("groups", "seq"), None),
    )
    out_specs = (
        P(("groups", "seq"), None),
        P(("groups", "seq"), None),
        P("groups", None),
        P("groups"),
        P("groups", None),
        P(("groups", "seq"), None, None),
        P(("groups", "seq"), None, None),
    )
    return jax.shard_map(
        per_device, mesh=mesh, in_specs=in_specs, out_specs=out_specs, check_vma=False
    )
```

```python
import functools

import jax
import jax.numpy as jnp
from jax import lax
from jax.experimental import pallas as pl
from jax.experimental.pallas import tpu as pltpu
from jax.sharding import PartitionSpec as P

KSIZE = 31
RIM = 16
LANES = 128
CHUNK = 256
NORM_EPS = 1e-05
F32 = jnp.float32
BF16 = jnp.bfloat16
LAST = (((1,), (1,)), ((), ()))
FIRST = (((0,), (0,)), ((), ()))
SMALL = 12 * 1024 * 1024
LARGE = 60 * 1024 * 1024
WEIGHT = 0.15 * 3.6e6


def dot(a, b):
    return jnp.dot(a, b, preferred_element_type=F32)


def dot_last(a, b):
    return lax.dot_general(a, b, LAST, preferred_element_type=F32)


def dot_first(a, b):
    return lax.dot_general(a, b, FIRST, preferred_element_type=F32)


def slope_of(values):
    logistic = jax.nn.sigmoid(values)
    return logistic * (1.0 + values * (1.0 - logistic))


class Staged:
    def __init__(self, source, held, semaphore):
        self.held, self.copy, self.waited = held, pltpu.make_async_copy(source, held, semaphore), False
        self.shape = held.shape
        self.copy.start()

    def wait(self):
        if not self.waited:
            self.copy.wait()
        self.waited = True

    def __getitem__(self, at):
        self.wait()
        return self.held[at]


def kernel_call(body, operands, outs, scratch=(), weight=0.0, limit=SMALL, scalars=()):
    count, out_count = len(operands), len(outs)
    staged = [place for place in range(count) if place not in scalars]
    held = [pltpu.VMEM(operands[place].shape, operands[place].dtype) for place in staged]
    results = [pltpu.VMEM(out.shape, out.dtype) for out in outs]

    def kernel(*refs):
        ins, out_refs, rest = refs[0:count], refs[count : count + out_count], refs[count + out_count :]
        copies, made, rest = rest[0 : len(staged)], rest[len(staged) : len(staged) + out_count], rest[len(staged) + out_count :]
        in_semaphores, out_semaphores, rest = rest[0], rest[1], rest[2:]
        values = list(ins)
        for turn, place in enumerate(staged):
            values[place] = Staged(ins[place], copies[turn], in_semaphores.at[turn])
        writes = [
            pltpu.make_async_copy(buffer, out, out_semaphores.at[turn])
            for turn, (buffer, out) in enumerate(zip(made, out_refs))
        ]
        started = []

        def write(*turns):
            for turn in turns:
                writes[turn].start()
                started.append(turn)

        body(values, made, rest, write)
        for value in values:
            if isinstance(value, Staged):
                value.wait()
        write(*[turn for turn in range(out_count) if turn not in started])
        for copy in writes:
            copy.wait()

    return pl.pallas_call(
        kernel,
        out_shape=tuple(outs),
        in_specs=[pl.BlockSpec(memory_space=pltpu.SMEM if place in scalars else pl.ANY) for place in range(count)],
        out_specs=tuple(pl.BlockSpec(memory_space=pl.ANY) for _ in outs),
        scratch_shapes=held + results + [pltpu.SemaphoreType.DMA((len(staged),)), pltpu.SemaphoreType.DMA((out_count,))] + list(scratch),
        compiler_params=pltpu.CompilerParams(vmem_limit_bytes=limit),
        cost_estimate=pl.CostEstimate(flops=1, bytes_accessed=int(WEIGHT * weight) + 1, transcendentals=0),
    )(*operands)


def columns_of(ids):
    count = ids.shape[1]
    row = lax.broadcasted_iota(jnp.int32, (count, count), 0)
    col = lax.broadcasted_iota(jnp.int32, (count, count), 1)
    return dot_last((row == col).astype(BF16), ids.astype(F32).astype(BF16)).astype(jnp.int32)


def choices(ids, experts):
    lane = lax.broadcasted_iota(jnp.int32, (ids.shape[0], experts), 1)
    return (ids[:, 0:1] == lane).astype(F32), (ids[:, 1:2] == lane).astype(F32)


def placements(ids, chip, near, capacity):
    count = ids.shape[0]
    first, second = choices(ids ^ chip, near)
    named = (first + second).astype(BF16)
    row = lax.broadcasted_iota(jnp.int32, (count, count), 0)
    col = lax.broadcasted_iota(jnp.int32, (count, count), 1)
    before = dot((col < row).astype(BF16), named)
    start = lax.broadcasted_iota(jnp.int32, (count, near), 1).astype(F32) * capacity
    place = before + start + 1.0
    slot = lax.broadcasted_iota(jnp.int32, (count, near * capacity), 1)
    picks = []
    for chosen in (first, second):
        at = jnp.sum(chosen * place, axis=1, keepdims=True).astype(jnp.int32) - 1
        picks.append((slot == at).astype(BF16))
    return picks


def pack_kernel(near, capacity, ins, outs, scratch, write):
    chip, normed, far_normed = ins[0:3]
    count = normed.shape[0] - RIM
    rows, far_rows = ins[3:5] if len(ins) > 3 else (normed, far_normed)
    blocks = ((ids_of(normed, count), rows), (ids_of(far_normed, count), far_rows))
    for block, (names, source) in enumerate(blocks):
        first, second = placements(columns_of(names), chip[0], near, capacity)
        packed = dot_first(first + second, source[0:count, :]).astype(BF16)
        for place, out in enumerate(outs):
            out[block * capacity : (block + 1) * capacity, :] = packed[place * capacity : (place + 1) * capacity]


def ids_of(normed, count):
    return normed[count : count + RIM, 0:count][0:2].astype(F32).astype(jnp.int32)


def block_rows(refs, block, capacity):
    return jnp.concatenate([ref[block * capacity : (block + 1) * capacity, :] for ref in refs], axis=0)


def shifted(pad_ref, lanes, count):
    for rest in range(8):
        block = pad_ref[pl.ds(rest, count + 24), lanes]
        for turn in range(4):
            offset = 8 * turn + rest
            if 1 <= offset <= KSIZE:
                yield offset, block[8 * turn : 8 * turn + count]


def fill_padded(pad_ref, left_ref, mid_ref, right_ref):
    count = mid_ref.shape[0]
    pad_ref[0:RIM, :] = left_ref[...].astype(F32)
    pad_ref[RIM : RIM + count, :] = mid_ref[...].astype(F32)
    pad_ref[RIM + count : 2 * RIM + count, :] = right_ref[...].astype(F32)


def lane_loop(width, body):
    @pl.loop(0, width // LANES)
    def _(step):
        body(pl.ds(pl.multiple_of(step * LANES, LANES), LANES))


def convolve_and_norm(frames, left, right, taps, gain, names, conv_ref, normed_ref, scratch):
    pad_ref, taps32_ref, mixed_ref, square_ref = scratch
    count, width = frames.shape
    fill_padded(pad_ref, left, frames, right)
    taps32_ref[...] = taps[...].astype(F32)
    square_ref[...] = jnp.zeros_like(square_ref)

    def conv(lanes):
        total = jnp.zeros((count, LANES), F32)
        for offset, rows in shifted(pad_ref, lanes, count):
            total = total + taps32_ref[offset - 1 : offset, lanes] * rows
        if conv_ref is not None:
            conv_ref[:, lanes] = total
        mixed = pad_ref[RIM : RIM + count, lanes] + total * jax.nn.sigmoid(total)
        mixed_ref[:, lanes] = mixed
        square_ref[...] += mixed * mixed

    lane_loop(width, conv)
    mean = jnp.sum(square_ref[...], axis=1, keepdims=True) / width
    inverse = lax.rsqrt(mean + NORM_EPS)
    normed_ref[0:count, :] = (mixed_ref[...] * inverse * gain[...].astype(F32)).astype(BF16)
    normed_ref[count : count + RIM, :] = names


def front_kernel(ins, outs, scratch, write):
    frames, left, right, taps, gain, names = ins
    convolve_and_norm(frames, left, right, taps, gain, names[...], outs[0], outs[1], scratch)


def far_front_kernel(near, capacity, ins, outs, scratch, write):
    chip, frames, rims_and_names, taps, gain, normed = ins
    far_normed, parts = outs[0], outs[1:]
    left, right = rims_and_names[0:RIM, :], rims_and_names[RIM : 2 * RIM, :]
    first, last = left.astype(F32)[0:1], right.astype(F32)[RIM - 1 : RIM]
    names = jnp.concatenate([first, last, jnp.zeros((RIM - 2, frames.shape[1]), F32)], axis=0).astype(BF16)
    convolve_and_norm(frames, left, right, taps, gain, names, None, far_normed, scratch)
    write(0)
    pack_kernel(near, capacity, (chip, normed, far_normed), parts, scratch, write)


def result_kernel(near, capacity, ins, outs, scratch, write):
    chip, upstream_near, normed_near, upstream_far, normed_far, router = ins[0:6]
    rows_refs = ins[6:]
    near_ref, far_ref, near_logits_ref, far_logits_ref, router_out_ref = outs
    count = upstream_near.shape[0]
    router_out = jnp.zeros(router_out_ref.shape, F32)
    blocks = ((upstream_near, normed_near), (upstream_far, normed_far))
    for block, (grad, normed) in reversed(list(enumerate(blocks))):
        names = columns_of(ids_of(normed, count))
        upstream = grad[...].astype(F32)
        normed = normed[0:count, :]
        gates = jax.nn.sigmoid(dot_last(normed, router[...]))
        rows = block_rows(rows_refs, block, capacity)
        added = jnp.zeros(upstream.shape, F32)
        grad_logits = jnp.zeros(gates.shape, F32)
        for pick, chosen in zip(placements(names, chip[0], near, capacity), choices(names, gates.shape[1])):
            result = dot(pick, rows)
            gate = jnp.sum(chosen * gates, axis=1, keepdims=True)
            added = added + gate * result
            grad_gate = jnp.sum(upstream * result, axis=1, keepdims=True)
            grad_logits = grad_logits + chosen * (grad_gate * gate * (1.0 - gate))
        grad_logits = grad_logits.astype(BF16)
        (near_ref, far_ref)[block][...] = added.astype((F32, BF16)[block])
        write(block)
        (near_logits_ref, far_logits_ref)[block][...] = grad_logits
        router_out = router_out + dot_first(grad_logits, normed)
    router_out_ref[...] = router_out


def back_kernel(near, capacity, ins, outs, scratch, write):
    chip, normed_near, logits_near, normed_far, logits_far, router = ins[0:6]
    rows_refs = ins[6:]
    count = outs[0].shape[0]
    blocks = ((normed_near, logits_near), (normed_far, logits_far))
    for block, (normed, logits) in reversed(list(enumerate(blocks))):
        first, second = placements(columns_of(ids_of(normed, count)), chip[0], near, capacity)
        total = dot(first + second, block_rows(rows_refs, block, capacity))
        outs[block][...] = (total + dot(logits[...], router[...])).astype(outs[block].dtype)
        write(block)


def half_lanes(core, width):
    return pl.ds(pl.multiple_of(core * (width // 2), LANES), width // 2)


def final_kernel(ins, outs, scratch, write):
    core, frames, left, right, conv, grad, gain, near_sum, far_sum, router, near_back, far_back = ins
    out_ref, mixed_grad_ref, conv_grad_ref, head_ref, tail_ref, kept_ref, given_ref = outs
    pad_ref, local_ref = scratch
    count, width = frames.shape
    fill_padded(pad_ref, left, frames, right)
    conv_out = conv[...]
    logistic = jax.nn.sigmoid(conv_out)
    mixed = frames[...].astype(F32) + conv_out * logistic
    inverse = lax.rsqrt(jnp.sum(mixed * mixed, axis=1, keepdims=True) / width + NORM_EPS)
    out_ref[...] = (mixed + (near_sum[...] + far_sum[...].astype(F32))).astype(BF16)
    write(0)
    local_ref[KSIZE + 1 :, :] = router[...]
    grad_normed = near_back[...] + far_back[...].astype(F32)
    local_ref[KSIZE : KSIZE + 1, :] = jnp.sum(grad_normed * mixed * inverse, axis=0, keepdims=True)
    scaled = grad_normed * gain[...].astype(F32)
    mean = jnp.sum(scaled * mixed, axis=1, keepdims=True) / width
    mixed_grad = grad[...].astype(F32) + inverse * scaled - mixed * (inverse * inverse * inverse * mean)
    mixed_grad_ref[...] = mixed_grad
    conv_grad = (mixed_grad * (logistic * (1.0 + conv_out * (1.0 - logistic)))).astype(BF16)
    conv_grad_ref[...] = conv_grad
    head_ref[...] = conv_grad[0:RIM]
    tail_ref[...] = conv_grad[count - RIM : count]
    write(1, 2, 3, 4)

    def reduce(lanes):
        grad = conv_grad_ref[:, lanes].astype(F32)
        for offset, rows in shifted(pad_ref, lanes, count):
            local_ref[offset - 1 : offset, lanes] = jnp.sum(grad * rows, axis=0, keepdims=True)

    lane_loop(width, reduce)
    kept_ref[...] = local_ref[:, half_lanes(core[0], width)]
    given_ref[...] = local_ref[:, half_lanes(1 - core[0], width)]


def frames_kernel(ins, outs, scratch, write):
    mixed_grad, conv_grad, left, right, taps = ins
    (out_ref,), (pad_ref, taps32_ref) = outs, scratch
    count, width = mixed_grad.shape
    fill_padded(pad_ref, left, conv_grad, right)
    taps32_ref[...] = taps[...].astype(F32)
    mixed_grad.wait()

    def conv(lanes):
        total = mixed_grad[:, lanes]
        for offset, rows in shifted(pad_ref, lanes, count):
            total = total + taps32_ref[KSIZE - offset : KSIZE - offset + 1, lanes] * rows
        out_ref[:, lanes] = total.astype(BF16)

    lane_loop(width, conv)


def chunk_loop(width, body):
    @pl.loop(0, width // CHUNK)
    def _(step):
        body(pl.ds(pl.multiple_of(step * CHUNK, CHUNK), CHUNK))


def gather_rows(refs, rows_ref):
    each = refs[0].shape[0]
    for place, ref in enumerate(refs):
        rows_ref[place * each : (place + 1) * each, :] = ref[...]


def scatter_columns(refs, columns, values):
    each = refs[0].shape[0]
    for place, ref in enumerate(refs):
        ref[:, columns] = values[place * each : (place + 1) * each]


def forward_kernel(near, ins, outs, scratch, write):
    rows, (near_in, far_in, near_out, far_out) = ins[0:near], ins[near:]
    out_refs, (rows_ref, near_pre_ref, far_pre_ref, near_active_ref, far_active_ref) = outs[0:near], outs[near:]
    gather_rows(rows, rows_ref)
    write(near)
    for weight, pre, active in ((near_in, near_pre_ref, near_active_ref), (far_in, far_pre_ref, far_active_ref)):
        weight.wait()

        def inner(columns):
            values = dot(rows_ref[...], weight[:, columns])
            pre[:, columns] = values
            active[:, columns] = jax.nn.silu(values).astype(BF16)

        chunk_loop(weight.shape[1], inner)
    write(near + 1, near + 2, near + 3, near + 4)
    near_out.wait()
    far_out.wait()

    def outer(columns):
        total = dot(near_active_ref[...], near_out[:, columns])
        total = total + dot(far_active_ref[...], far_out[:, columns])
        scatter_columns(out_refs, columns, total.astype(BF16))

    chunk_loop(near_out.shape[1], outer)


def backward_kernel(near, ins, outs, scratch, write):
    grads, (rows, router, mine, near_out, far_out, near_pre, far_pre, near_in, far_in) = ins[0:near], ins[near:]
    out_refs, (near_grad_ref, far_grad_ref, grad_rows_ref) = outs[0:near], outs[near:]
    (grads_ref,) = scratch
    gather_rows(grads, grads_ref)
    logits = jnp.sum(dot_last(rows[...], router[...]) * mine[...], axis=1, keepdims=True)
    gate = jax.nn.sigmoid(logits)
    grad_rows_ref[...] = (gate * grads_ref[...].astype(F32)).astype(BF16)
    write(near + 2)
    for weight, pre, grad in ((near_out, near_pre, near_grad_ref), (far_out, far_pre, far_grad_ref)):
        weight.wait()
        pre.wait()

        def inner(columns):
            hidden = dot_last(grad_rows_ref[...], weight[columns, :])
            grad[:, columns] = (hidden * slope_of(pre[:, columns])).astype(BF16)

        chunk_loop(weight.shape[0], inner)
    write(near, near + 1)
    near_in.wait()
    far_in.wait()

    def outer(rows):
        total = dot_last(near_grad_ref[...], near_in[rows, :])
        total = total + dot_last(far_grad_ref[...], far_in[rows, :])
        scatter_columns(out_refs, rows, total.astype(BF16))

    chunk_loop(near_in.shape[0], outer)


def last_kernel(ins, outs, scratch, write):
    core, mine, other = ins
    taps_ref, gain_ref, router_ref = outs
    width = taps_ref.shape[1]
    for place, half in ((core[0], mine), (1 - core[0], other)):
        lanes = half_lanes(place, width)
        taps_ref[:, lanes] = half[0:KSIZE]
        gain_ref[:, lanes] = half[KSIZE : KSIZE + 1]
        router_ref[:, lanes] = half[KSIZE + 1 :]


def rims(head, tail, count):
    ends = count - 1
    left = lax.ppermute(tail, "seq", [(i, i + 1) for i in range(ends)])
    right = lax.ppermute(head, "seq", [(i + 1, i) for i in range(ends)])
    return left, right


def swap(values, count, bit):
    return lax.ppermute(values, "seq", [(i, i ^ bit) for i in range(count)])


def exchange(parts, devices):
    return [parts[0]] + [swap(part, devices, 2 * r) for r, part in enumerate(parts) if r]


def per_device(frames, conv_kernel, norm_gain, router, expert_in, expert_out, expert_ids, out_grad):
    count, width = frames.shape
    devices = lax.axis_size("seq")
    experts = devices // 2
    capacity = 8 * count // devices
    near = experts // 2
    slots = experts * capacity
    gain = norm_gain.reshape(1, width)
    taps = conv_kernel
    router = router.T
    ids = expert_ids.T
    shape = jax.ShapeDtypeStruct
    pad = pltpu.VMEM((count + 2 * RIM, width), F32)
    taps32 = pltpu.VMEM((KSIZE, width), F32)
    chip = lax.axis_index("seq") // 2
    chips = chip.reshape(1).astype(jnp.int32)
    mine = (jnp.arange(experts, dtype=jnp.int32) == chip).astype(F32).reshape(1, experts)
    cross = functools.partial(swap, count=devices, bit=devices // 2)

    frames, head, tail = lax.optimization_barrier((frames, frames[0:RIM], frames[count - RIM : count]))
    left, right = rims(head, tail, devices)
    far_frames = cross(frames)
    names = jnp.pad(ids.astype(BF16), ((0, RIM - 2), (0, width - count)))
    weight_in, weight_out = expert_in[0], expert_out[0]
    other_in = swap(weight_in, devices, 1)
    other_out = swap(weight_out, devices, 1)
    left, right, other_in, other_out = lax.optimization_barrier((left, right, other_in, other_out))

    model32, model16 = shape((count, width), F32), shape((count, width), BF16)
    named16 = shape((count + RIM, width), BF16)
    front_scratch = (pad, taps32, pltpu.VMEM((count, width), F32), pltpu.VMEM((count, LANES), F32))
    conv_out, normed = kernel_call(
        front_kernel, (frames, left, right, taps, gain, names), (model32, named16), front_scratch, weight=3.3
    )
    far_rims = cross(jnp.concatenate([names[0:1], left[1:], right[: RIM - 1], names[1:2]]))
    far_rims, far_frames, out_grad = lax.optimization_barrier((far_rims, far_frames, out_grad))
    far_grad = cross(out_grad)
    part = (shape((2 * capacity, width), BF16),) * near
    far_normed, *parts = kernel_call(
        functools.partial(far_front_kernel, near, capacity),
        (chips, far_frames, far_rims, taps, gain, normed),
        (named16, *part),
        front_scratch,
        weight=0.0,
        scalars=(0,),
    )
    rows = exchange(parts, devices)
    parts = kernel_call(
        functools.partial(pack_kernel, near, capacity),
        (chips, normed, far_normed, out_grad, far_grad),
        part,
        weight=0.0,
        scalars=(0,),
    )
    rows[0:3], parts = lax.optimization_barrier((rows[0:3], parts))
    grads = exchange(parts, devices)

    half = weight_in.shape[1]
    wide = shape((slots, half), F32)
    narrow = shape((slots, half), BF16)
    model = shape((slots, width), BF16)
    outs = kernel_call(
        functools.partial(forward_kernel, near),
        (*rows, weight_in, other_in, weight_out, other_out),
        part + (model, wide, wide, narrow, narrow),
        weight=0.0, limit=LARGE,
    )
    parts_out, (all_rows, *pre_act), active = outs[0:near], outs[near : near + 3], outs[near + 3 :]
    results = exchange(parts_out, devices)
    outs = kernel_call(
        functools.partial(backward_kernel, near),
        (*grads, all_rows, router, mine, weight_out, other_out, *pre_act, weight_in, other_in),
        part + (narrow, narrow, model),
        (pltpu.VMEM((slots, width), BF16),),
        weight=0.0, limit=LARGE,
    )
    results, outs, all_rows, active = lax.optimization_barrier((results, outs, all_rows, active))
    parts_in, pre_grad, grad_rows = outs[0:near], outs[near : near + 2], outs[near + 2]
    backs = exchange(parts_in, devices)
    logits = shape((count, experts), BF16)
    near_sum, far_sum, near_logits, far_logits, router_local = kernel_call(
        functools.partial(result_kernel, near, capacity),
        (chips, out_grad, normed, far_grad, far_normed, router, *results),
        (model32, model16, logits, logits, shape((experts, width), F32)),
        weight=0.0,
        scalars=(0,),
    )
    far_sum = cross(far_sum)
    near_back, far_back = kernel_call(
        functools.partial(back_kernel, near, capacity),
        (chips, normed, near_logits, far_normed, far_logits, router, *backs),
        (model32, model16),
        weight=0.0,
        scalars=(0,),
    )
    far_back, far_sum, all_rows, active, grad_rows, pre_grad = lax.optimization_barrier(
        (far_back, far_sum, all_rows, active, grad_rows, pre_grad)
    )
    far_back = cross(far_back)
    far_rows, far_active, far_grads, far_pre = [
        swap(values, devices, 1) for values in (all_rows, active[1], grad_rows, pre_grad[1])
    ]
    expert_out_grad = (dot_first(active[0], grad_rows) + dot_first(far_active, far_grads)).astype(BF16)
    expert_in_grad = (dot_first(all_rows, pre_grad[0]) + dot_first(far_rows, far_pre)).astype(BF16)
    far_back, expert_in_grad, expert_out_grad = lax.optimization_barrier((far_back, expert_in_grad, expert_out_grad))

    rim = shape((RIM, width), BF16)
    lines = KSIZE + 1 + experts
    columns = shape((lines, width // 2), F32)
    core = (lax.axis_index("seq") % 2).reshape(1).astype(jnp.int32)
    block_out, mixed_grad, conv_grad, head, tail, kept, given = kernel_call(
        final_kernel,
        (core, frames, left, right, conv_out, out_grad, gain, near_sum, far_sum, router_local, near_back, far_back),
        (model16, model32, model16, rim, rim, columns, columns),
        (pad, pltpu.VMEM((lines, width), F32)),
        weight=0.0,
        scalars=(0,),
    )
    grad_left, grad_right = rims(head, tail, devices)
    local = kept + swap(given, devices, 1)
    bit = 2
    while bit < devices:
        other = swap(local, devices, bit)
        if bit == devices // 4:
            other, grad_left, grad_right = lax.optimization_barrier((other, grad_left, grad_right))
            (frames_grad,) = kernel_call(
                frames_kernel, (mixed_grad, conv_grad, grad_left, grad_right, taps), (model16,), (pad, taps32), weight=0.0
            )
        if 2 * bit == devices:
            other, frames_grad = lax.optimization_barrier((other, frames_grad))
        local = local + other
        bit *= 2
    kernel_grad, gain_grad, router_grad = kernel_call(
        last_kernel,
        (core, local, swap(local, devices, 1)),
        (shape((KSIZE, width), F32), shape((1, width), F32), shape((experts, width), F32)),
        weight=0.0,
        scalars=(0,),
    )
    return (
        block_out,
        frames_grad,
        kernel_grad,
        gain_grad[0],
        router_grad.T,
        expert_in_grad[None],
        expert_out_grad[None],
    )


def solution(mesh):
    in_specs = (
        P(("groups", "seq"), None),
        P(),
        P(),
        P(),
        P("seq", None, None),
        P("seq", None, None),
        P(("groups", "seq"), None),
        P(("groups", "seq"), None),
    )
    out_specs = (
        P(("groups", "seq"), None),
        P(("groups", "seq"), None),
        P("groups", None),
        P("groups"),
        P("groups", None),
        P(("groups", "seq"), None, None),
        P(("groups", "seq"), None, None),
    )
    return jax.shard_map(
        per_device, mesh=mesh, in_specs=in_specs, out_specs=out_specs, check_vma=False
    )
```

```python
import functools

import jax
import jax.numpy as jnp
from jax import lax
from jax.experimental import pallas as pl
from jax.experimental.pallas import tpu as pltpu
from jax.sharding import PartitionSpec as P

KSIZE = 31
RIM = 16
LANES = 128
CHUNK = 256
NORM_EPS = 1e-05
F32 = jnp.float32
BF16 = jnp.bfloat16
LAST = (((1,), (1,)), ((), ()))
FIRST = (((0,), (0,)), ((), ()))
SMALL = 12 * 1024 * 1024
LARGE = 60 * 1024 * 1024
WEIGHT = 0.15 * 3.6e6


def dot(a, b):
    return jnp.dot(a, b, preferred_element_type=F32)


def dot_last(a, b):
    return lax.dot_general(a, b, LAST, preferred_element_type=F32)


def dot_first(a, b):
    return lax.dot_general(a, b, FIRST, preferred_element_type=F32)


def slope_of(values):
    logistic = jax.nn.sigmoid(values)
    return logistic * (1.0 + values * (1.0 - logistic))


class Staged:
    def __init__(self, source, held, semaphore):
        self.held, self.copy = held, pltpu.make_async_copy(source, held, semaphore)
        self.shape, self.started, self.waited = held.shape, False, False

    def start(self):
        if not self.started:
            self.copy.start()
        self.started = True

    def wait(self):
        self.start()
        if not self.waited:
            self.copy.wait()
        self.waited = True

    def __getitem__(self, at):
        self.wait()
        return self.held[at]


def kernel_call(body, operands, outs, scratch=(), weight=0.0, limit=SMALL, scalars=(), first=None):
    count, out_count = len(operands), len(outs)
    staged = [place for place in range(count) if place not in scalars]
    held = [pltpu.VMEM(operands[place].shape, operands[place].dtype) for place in staged]
    results = [pltpu.VMEM(out.shape, out.dtype) for out in outs]

    def kernel(*refs):
        ins, out_refs, rest = refs[0:count], refs[count : count + out_count], refs[count + out_count :]
        copies, made, rest = rest[0 : len(staged)], rest[len(staged) : len(staged) + out_count], rest[len(staged) + out_count :]
        in_semaphores, out_semaphores, rest = rest[0], rest[1], rest[2:]
        values = list(ins)
        for turn, place in enumerate(staged):
            values[place] = Staged(ins[place], copies[turn], in_semaphores.at[turn])
            if first is None or place < first:
                values[place].start()
        writes = [
            pltpu.make_async_copy(buffer, out, out_semaphores.at[turn])
            for turn, (buffer, out) in enumerate(zip(made, out_refs))
        ]
        started = []

        def write(*turns):
            for turn in turns:
                writes[turn].start()
                started.append(turn)

        body(values, made, rest, write)
        for value in values:
            if isinstance(value, Staged):
                value.wait()
        write(*[turn for turn in range(out_count) if turn not in started])
        for copy in writes:
            copy.wait()

    return pl.pallas_call(
        kernel,
        out_shape=tuple(outs),
        in_specs=[pl.BlockSpec(memory_space=pltpu.SMEM if place in scalars else pl.ANY) for place in range(count)],
        out_specs=tuple(pl.BlockSpec(memory_space=pl.ANY) for _ in outs),
        scratch_shapes=held + results + [pltpu.SemaphoreType.DMA((len(staged),)), pltpu.SemaphoreType.DMA((out_count,))] + list(scratch),
        compiler_params=pltpu.CompilerParams(vmem_limit_bytes=limit),
        cost_estimate=pl.CostEstimate(flops=1, bytes_accessed=int(WEIGHT * weight) + 1, transcendentals=0),
    )(*operands)


def columns_of(ids):
    count = ids.shape[1]
    row = lax.broadcasted_iota(jnp.int32, (count, count), 0)
    col = lax.broadcasted_iota(jnp.int32, (count, count), 1)
    return dot_last((row == col).astype(BF16), ids.astype(F32).astype(BF16)).astype(jnp.int32)


def choices(ids, experts):
    lane = lax.broadcasted_iota(jnp.int32, (ids.shape[0], experts), 1)
    return (ids[:, 0:1] == lane).astype(F32), (ids[:, 1:2] == lane).astype(F32)


def placements(ids, chip, near, capacity):
    count = ids.shape[0]
    first, second = choices(ids ^ chip, near)
    named = (first + second).astype(BF16)
    row = lax.broadcasted_iota(jnp.int32, (count, count), 0)
    col = lax.broadcasted_iota(jnp.int32, (count, count), 1)
    before = dot((col < row).astype(BF16), named)
    start = lax.broadcasted_iota(jnp.int32, (count, near), 1).astype(F32) * capacity
    place = before + start + 1.0
    slot = lax.broadcasted_iota(jnp.int32, (count, near * capacity), 1)
    picks = []
    for chosen in (first, second):
        at = jnp.sum(chosen * place, axis=1, keepdims=True).astype(jnp.int32) - 1
        picks.append((slot == at).astype(BF16))
    return picks


def pack_kernel(near, capacity, ins, outs, scratch, write):
    chip, normed, far_normed = ins[0:3]
    count = normed.shape[0] - RIM
    rows, far_rows = ins[3:5] if len(ins) > 3 else (normed, far_normed)
    blocks = ((ids_of(normed, count), rows), (ids_of(far_normed, count), far_rows))
    for block, (names, source) in enumerate(blocks):
        first, second = placements(columns_of(names), chip[0], near, capacity)
        packed = dot_first(first + second, source[0:count, :]).astype(BF16)
        for place, out in enumerate(outs):
            out[block * capacity : (block + 1) * capacity, :] = packed[place * capacity : (place + 1) * capacity]


def ids_of(normed, count):
    return normed[count : count + RIM, 0:count][0:2].astype(F32).astype(jnp.int32)


def block_rows(refs, block, capacity):
    return jnp.concatenate([ref[block * capacity : (block + 1) * capacity, :] for ref in refs], axis=0)


def shifted(pad_ref, lanes, count):
    for rest in range(8):
        block = pad_ref[pl.ds(rest, count + 24), lanes]
        for turn in range(4):
            offset = 8 * turn + rest
            if 1 <= offset <= KSIZE:
                yield offset, block[8 * turn : 8 * turn + count]


def fill_padded(pad_ref, core, twin, mid, other):
    count = mid.shape[0]
    after = RIM + count
    pad_ref[pl.ds(pl.multiple_of((1 - core) * after, 8), RIM), :] = twin[...].astype(F32)
    pad_ref[RIM:after, :] = mid[...].astype(F32)
    pad_ref[pl.ds(pl.multiple_of(core * after, 8), RIM), :] = other[...].astype(F32)


def lane_loop(width, body):
    @pl.loop(0, width // LANES)
    def _(step):
        body(pl.ds(pl.multiple_of(step * LANES, LANES), LANES))


def convolve_and_norm(core, frames, twin, other, taps, gain, names, conv_ref, normed_ref, scratch):
    pad_ref, taps32_ref, mixed_ref, square_ref = scratch
    count, width = frames.shape
    fill_padded(pad_ref, core, twin, frames, other)
    taps32_ref[...] = taps[...].astype(F32)
    square_ref[...] = jnp.zeros_like(square_ref)

    def conv(lanes):
        total = jnp.zeros((count, LANES), F32)
        for offset, rows in shifted(pad_ref, lanes, count):
            total = total + taps32_ref[offset - 1 : offset, lanes] * rows
        if conv_ref is not None:
            conv_ref[:, lanes] = total
        mixed = pad_ref[RIM : RIM + count, lanes] + total * jax.nn.sigmoid(total)
        mixed_ref[:, lanes] = mixed
        square_ref[...] += mixed * mixed

    lane_loop(width, conv)
    mean = jnp.sum(square_ref[...], axis=1, keepdims=True) / width
    inverse = lax.rsqrt(mean + NORM_EPS)
    normed_ref[0:count, :] = (mixed_ref[...] * inverse * gain[...].astype(F32)).astype(BF16)
    normed_ref[count : count + RIM, :] = names


def front_kernel(ins, outs, scratch, write):
    core, frames, twin, other, taps, gain, names = ins
    convolve_and_norm(core[0], frames, twin, other, taps, gain, names[...], outs[0], outs[1], scratch)


def far_front_kernel(near, capacity, ins, outs, scratch, write):
    chip, core, frames, rims_and_names, taps, gain, normed = ins
    far_normed, parts = outs[0], outs[1:]
    twin, other = rims_and_names[0:RIM, :], rims_and_names[RIM : 2 * RIM, :]
    even = core[0] == 0
    first = jnp.where(even, twin.astype(F32)[RIM - 1 : RIM], twin.astype(F32)[0:1])
    last = jnp.where(even, other.astype(F32)[0:1], other.astype(F32)[RIM - 1 : RIM])
    names = jnp.concatenate([first, last, jnp.zeros((RIM - 2, frames.shape[1]), F32)], axis=0).astype(BF16)
    convolve_and_norm(core[0], frames, twin, other, taps, gain, names, None, far_normed, scratch)
    write(0)
    pack_kernel(near, capacity, (chip, normed, far_normed), parts, scratch, write)


def result_kernel(near, capacity, ins, outs, scratch, write):
    chip, upstream_near, normed_near, upstream_far, normed_far, router = ins[0:6]
    rows_refs = ins[6:]
    near_ref, far_ref, near_logits_ref, far_logits_ref, router_out_ref = outs
    count = upstream_near.shape[0]
    router_out = jnp.zeros(router_out_ref.shape, F32)
    blocks = ((upstream_near, normed_near), (upstream_far, normed_far))
    for block, (grad, normed) in reversed(list(enumerate(blocks))):
        names = columns_of(ids_of(normed, count))
        upstream = grad[...].astype(F32)
        normed = normed[0:count, :]
        gates = jax.nn.sigmoid(dot_last(normed, router[...]))
        rows = block_rows(rows_refs, block, capacity)
        added = jnp.zeros(upstream.shape, F32)
        grad_logits = jnp.zeros(gates.shape, F32)
        for pick, chosen in zip(placements(names, chip[0], near, capacity), choices(names, gates.shape[1])):
            result = dot(pick, rows)
            gate = jnp.sum(chosen * gates, axis=1, keepdims=True)
            added = added + gate * result
            grad_gate = jnp.sum(upstream * result, axis=1, keepdims=True)
            grad_logits = grad_logits + chosen * (grad_gate * gate * (1.0 - gate))
        grad_logits = grad_logits.astype(BF16)
        (near_ref, far_ref)[block][...] = added.astype((F32, BF16)[block])
        write(block)
        (near_logits_ref, far_logits_ref)[block][...] = grad_logits
        router_out = router_out + dot_first(grad_logits, normed)
    router_out_ref[...] = router_out


def back_kernel(near, capacity, ins, outs, scratch, write):
    chip, normed_near, logits_near, normed_far, logits_far, router = ins[0:6]
    rows_refs = ins[6:]
    count = outs[0].shape[0]
    blocks = ((normed_near, logits_near), (normed_far, logits_far))
    for block, (normed, logits) in reversed(list(enumerate(blocks))):
        first, second = placements(columns_of(ids_of(normed, count)), chip[0], near, capacity)
        total = dot(first + second, block_rows(rows_refs, block, capacity))
        outs[block][...] = (total + dot(logits[...], router[...])).astype(outs[block].dtype)
        write(block)


def half_lanes(core, width):
    return pl.ds(pl.multiple_of(core * (width // 2), LANES), width // 2)


def final_kernel(ins, outs, scratch, write):
    core, frames, twin, other, conv, grad, gain, near_sum, far_sum, router, near_back, far_back = ins
    out_ref, mixed_grad_ref, conv_grad_ref, twin_ref, other_ref, kept_ref, given_ref = outs
    pad_ref, local_ref = scratch
    count, width = frames.shape
    fill_padded(pad_ref, core[0], twin, frames, other)
    conv_out = conv[...]
    logistic = jax.nn.sigmoid(conv_out)
    mixed = frames[...].astype(F32) + conv_out * logistic
    inverse = lax.rsqrt(jnp.sum(mixed * mixed, axis=1, keepdims=True) / width + NORM_EPS)
    out_ref[...] = (mixed + (near_sum[...] + far_sum[...].astype(F32))).astype(BF16)
    write(0)
    local_ref[KSIZE + 1 :, :] = router[...]
    grad_normed = near_back[...] + far_back[...].astype(F32)
    local_ref[KSIZE : KSIZE + 1, :] = jnp.sum(grad_normed * mixed * inverse, axis=0, keepdims=True)
    scaled = grad_normed * gain[...].astype(F32)
    mean = jnp.sum(scaled * mixed, axis=1, keepdims=True) / width
    mixed_grad = grad[...].astype(F32) + inverse * scaled - mixed * (inverse * inverse * inverse * mean)
    mixed_grad_ref[...] = mixed_grad
    conv_grad = (mixed_grad * (logistic * (1.0 + conv_out * (1.0 - logistic)))).astype(BF16)
    conv_grad_ref[...] = conv_grad
    twin_ref[...] = jnp.where(core[0] == 0, conv_grad[count - RIM : count], conv_grad[0:RIM])
    other_ref[...] = jnp.where(core[0] == 0, conv_grad[0:RIM], conv_grad[count - RIM : count])
    write(1, 2, 3, 4)

    def reduce(lanes):
        grad = conv_grad_ref[:, lanes].astype(F32)
        for offset, rows in shifted(pad_ref, lanes, count):
            local_ref[offset - 1 : offset, lanes] = jnp.sum(grad * rows, axis=0, keepdims=True)

    lane_loop(width, reduce)
    kept_ref[...] = local_ref[:, half_lanes(core[0], width)]
    given_ref[...] = local_ref[:, half_lanes(1 - core[0], width)]


def frames_kernel(ins, outs, scratch, write):
    core, mixed_grad, conv_grad, twin, other, taps = ins
    (out_ref,), (pad_ref, taps32_ref) = outs, scratch
    count, width = mixed_grad.shape
    fill_padded(pad_ref, core[0], twin, conv_grad, other)
    taps32_ref[...] = taps[...].astype(F32)
    mixed_grad.wait()

    def conv(lanes):
        total = mixed_grad[:, lanes]
        for offset, rows in shifted(pad_ref, lanes, count):
            total = total + taps32_ref[KSIZE - offset : KSIZE - offset + 1, lanes] * rows
        out_ref[:, lanes] = total.astype(BF16)

    lane_loop(width, conv)


def chunks(width):
    return [slice(start, start + CHUNK) for start in range(0, width, CHUNK)]


def gather_rows(refs, rows_ref):
    each = refs[0].shape[0]
    for place, ref in enumerate(refs):
        rows_ref[place * each : (place + 1) * each, :] = ref[...]


def scatter_columns(refs, columns, values):
    each = refs[0].shape[0]
    for place, ref in enumerate(refs):
        ref[:, columns] = values[place * each : (place + 1) * each]


def forward_kernel(near, ins, outs, scratch, write):
    rows, (near_in, far_in, near_out, far_out) = ins[0:near], ins[near:]
    out_refs, (rows_ref, near_slope, far_slope, near_active, far_active) = outs[0:near], outs[near:]
    gather_rows(rows, rows_ref)
    near_in.wait()
    near_out.start()
    far_out.start()
    write(near)
    for weight, slope, active in ((near_in, near_slope, near_active), (far_in, far_slope, far_active)):
        weight.wait()
        for columns in chunks(weight.shape[1]):
            values = dot(rows_ref[...], weight[:, columns])
            logistic = jax.nn.sigmoid(values)
            active[:, columns] = (values * logistic).astype(BF16)
            slope[:, columns] = (logistic * (1.0 + values * (1.0 - logistic))).astype(BF16)
    write(near + 1, near + 2, near + 3, near + 4)
    near_out.wait()
    far_out.wait()
    for columns in chunks(near_out.shape[1]):
        total = dot(near_active[...], near_out[:, columns])
        total = total + dot(far_active[...], far_out[:, columns])
        scatter_columns(out_refs, columns, total.astype(BF16))


def backward_kernel(near, ins, outs, scratch, write):
    chip, grads, rest = ins[0], ins[1 : near + 1], ins[near + 1 :]
    rows, router, near_out, far_out, near_slope, far_slope, near_in, far_in, far_active = rest
    out_refs, (near_grad, sent) = outs[0:near], outs[near:]
    (grads_ref,) = scratch
    count = rows.shape[0]
    rows_part, active_part, grads_part, pre_part = (slice(turn * count, (turn + 1) * count) for turn in range(4))
    gather_rows(grads, grads_ref)
    logits = dot_last(rows[...], router[...])
    mine = lax.broadcasted_iota(jnp.int32, logits.shape, 1) == chip[0]
    gate = jax.nn.sigmoid(jnp.sum(jnp.where(mine, logits, 0.0), axis=1, keepdims=True))
    sent[grads_part, :] = (gate * grads_ref[...].astype(F32)).astype(BF16)
    for later in (far_out, near_slope, far_slope, near_in, far_in, far_active):
        later.start()
    for weight, slope, grad, part in ((near_out, near_slope, near_grad, slice(None)), (far_out, far_slope, sent, pre_part)):
        weight.wait()
        slope.wait()
        for columns in chunks(weight.shape[0]):
            hidden = dot_last(sent[grads_part, :], weight[columns, :])
            grad[part, columns] = (hidden * slope[:, columns].astype(F32)).astype(BF16)
    write(near)
    sent[rows_part, :] = rows[...]
    sent[active_part, :] = far_active[...]
    write(near + 1)
    near_in.wait()
    far_in.wait()
    for columns in chunks(near_in.shape[0]):
        total = dot_last(near_grad[...], near_in[columns, :])
        total = total + dot_last(sent[pre_part, :], far_in[columns, :])
        scatter_columns(out_refs, columns, total.astype(BF16))


def weights_kernel(ins, outs, scratch, write):
    near_active, near_grad, near_part, far_part = ins
    in_grad, out_grad = outs
    count, width = near_active.shape
    rows_part, active_part, grads_part, pre_part = (slice(turn * count, (turn + 1) * count) for turn in range(4))
    for ref in ins:
        ref.wait()
    for columns in chunks(width):
        total = dot_first(near_active[:, columns], near_part[grads_part, :])
        out_grad[columns, :] = (total + dot_first(far_part[active_part, columns], far_part[grads_part, :])).astype(BF16)
    write(1)
    for columns in chunks(width):
        total = dot_first(near_part[rows_part, columns], near_grad[...])
        in_grad[columns, :] = (total + dot_first(far_part[rows_part, columns], far_part[pre_part, :])).astype(BF16)


def last_kernel(ins, outs, scratch, write):
    core, mine, other = ins
    taps_ref, gain_ref, router_ref = outs
    width = taps_ref.shape[1]
    for place, half in ((core[0], mine), (1 - core[0], other)):
        lanes = half_lanes(place, width)
        taps_ref[:, lanes] = half[0:KSIZE]
        gain_ref[:, lanes] = half[KSIZE : KSIZE + 1]
        router_ref[:, lanes] = half[KSIZE + 1 :]


def pair_up(values, count):
    pairs = [(i, i + 1) for i in range(1, count - 1, 2)]
    return lax.ppermute(values, "seq", pairs + [(j, i) for i, j in pairs])


def swap(values, count, bit):
    return lax.ppermute(values, "seq", [(i, i ^ bit) for i in range(count)])


def exchange(parts, devices):
    return [parts[0]] + [swap(part, devices, 2 * r) for r, part in enumerate(parts) if r]


def per_device(frames, conv_kernel, norm_gain, router, expert_in, expert_out, expert_ids, out_grad):
    count, width = frames.shape
    devices = lax.axis_size("seq")
    experts = devices // 2
    capacity = 8 * count // devices
    near = experts // 2
    slots = experts * capacity
    gain = norm_gain.reshape(1, width)
    taps = conv_kernel
    router = router.T
    ids = expert_ids.T
    shape = jax.ShapeDtypeStruct
    pad = pltpu.VMEM((count + 2 * RIM, width), F32)
    taps32 = pltpu.VMEM((KSIZE, width), F32)
    chip = lax.axis_index("seq") // 2
    chips = chip.reshape(1).astype(jnp.int32)
    cross = functools.partial(swap, count=devices, bit=devices // 2)

    core = lax.axis_index("seq") % 2
    cores = core.reshape(1).astype(jnp.int32)
    ends = (frames[count - RIM : count], frames[0:RIM])
    frames, to_twin, to_other = lax.optimization_barrier(
        (frames, jnp.where(core == 0, *ends), jnp.where(core == 0, *ends[::-1]))
    )
    twin, other = swap(to_twin, devices, 1), pair_up(to_other, devices)
    far_frames = cross(frames)
    names = jnp.pad(ids.astype(BF16), ((0, RIM - 2), (0, width - count)))
    weight_in, weight_out = expert_in[0], expert_out[0]
    other_in = swap(weight_in, devices, 1)
    other_out = swap(weight_out, devices, 1)
    twin, other, other_in, other_out = lax.optimization_barrier((twin, other, other_in, other_out))

    model32, model16 = shape((count, width), F32), shape((count, width), BF16)
    named16 = shape((count + RIM, width), BF16)
    front_scratch = (pad, taps32, pltpu.VMEM((count, width), F32), pltpu.VMEM((count, LANES), F32))
    conv_out, normed = kernel_call(
        front_kernel,
        (cores, frames, twin, other, taps, gain, names),
        (model32, named16),
        front_scratch,
        weight=3.3,
        scalars=(0,),
    )
    even = jnp.concatenate([twin[: RIM - 1], names[0:1], names[1:2], other[1:]])
    odd = jnp.concatenate([names[0:1], twin[1:], other[: RIM - 1], names[1:2]])
    far_rims = cross(jnp.where(core == 0, even, odd))
    far_rims, far_frames, out_grad = lax.optimization_barrier((far_rims, far_frames, out_grad))
    far_grad = cross(out_grad)
    part = (shape((2 * capacity, width), BF16),) * near
    far_normed, *parts = kernel_call(
        functools.partial(far_front_kernel, near, capacity),
        (chips, cores, far_frames, far_rims, taps, gain, normed),
        (named16, *part),
        front_scratch,
        scalars=(0, 1),
    )
    rows = exchange(parts, devices)
    parts = kernel_call(
        functools.partial(pack_kernel, near, capacity),
        (chips, normed, far_normed, out_grad, far_grad),
        part,
        weight=0.0,
        scalars=(0,),
    )
    rows[0:3], parts = lax.optimization_barrier((rows[0:3], parts))
    grads = exchange(parts, devices)

    narrow = shape((slots, weight_in.shape[1]), BF16)
    outs = kernel_call(
        functools.partial(forward_kernel, near),
        (*rows, weight_in, other_in, weight_out, other_out),
        part + (shape((slots, width), BF16), narrow, narrow, narrow, narrow),
        limit=LARGE,
        first=near + 2,
    )
    parts_out, (all_rows, *slopes), (near_active, far_active) = outs[0:near], outs[near : near + 3], outs[near + 3 :]
    results = exchange(parts_out, devices)
    outs = kernel_call(
        functools.partial(backward_kernel, near),
        (chips, *grads, all_rows, router, weight_out, other_out, *slopes, weight_in, other_in, far_active),
        part + (narrow, shape((4 * slots, width), BF16)),
        (pltpu.VMEM((slots, width), BF16),),
        limit=LARGE,
        first=near + 4,
        scalars=(0,),
    )
    results, outs = lax.optimization_barrier((results, outs))
    parts_in, near_grad, sent = outs[0:near], outs[near], outs[near + 1]
    backs = exchange(parts_in, devices)

    logits = shape((count, experts), BF16)
    near_sum, far_sum, near_logits, far_logits, router_local = kernel_call(
        functools.partial(result_kernel, near, capacity),
        (chips, out_grad, normed, far_grad, far_normed, router, *results),
        (model32, model16, logits, logits, shape((experts, width), F32)),
        weight=0.0,
        scalars=(0,),
    )
    far_sum = cross(far_sum)
    near_back, far_back = kernel_call(
        functools.partial(back_kernel, near, capacity),
        (chips, normed, near_logits, far_normed, far_logits, router, *backs),
        (model32, model16),
        weight=0.0,
        scalars=(0,),
    )
    far_back, far_sum = lax.optimization_barrier((far_back, far_sum))
    far_back = cross(far_back)
    grad = shape(weight_in.shape, BF16)
    expert_in_grad, expert_out_grad = kernel_call(
        weights_kernel, (near_active, near_grad, sent, swap(sent, devices, 1)), (grad, grad), limit=LARGE
    )
    far_back, expert_in_grad, expert_out_grad = lax.optimization_barrier((far_back, expert_in_grad, expert_out_grad))

    rim = shape((RIM, width), BF16)
    lines = KSIZE + 1 + experts
    columns = shape((lines, width // 2), F32)
    block_out, mixed_grad, conv_grad, to_twin, to_other, kept, given = kernel_call(
        final_kernel,
        (cores, frames, twin, other, conv_out, out_grad, gain, near_sum, far_sum, router_local, near_back, far_back),
        (model16, model32, model16, rim, rim, columns, columns),
        (pad, pltpu.VMEM((lines, width), F32)),
        weight=0.0,
        scalars=(0,),
    )
    grad_twin, grad_other = swap(to_twin, devices, 1), pair_up(to_other, devices)
    local = kept + swap(given, devices, 1)
    bit = 2
    while bit < devices:
        last = 4 * bit > devices
        others = [swap(local, devices, step) for step in ((bit,) if last else (bit, 2 * bit, 3 * bit))]
        if bit == 2:
            others, grad_twin, grad_other = lax.optimization_barrier((others, grad_twin, grad_other))
            (frames_grad,) = kernel_call(
                frames_kernel,
                (cores, mixed_grad, conv_grad, grad_twin, grad_other, taps),
                (model16,),
                (pad, taps32),
                scalars=(0,),
            )
        bit *= 2 if last else 4
        if bit == devices:
            others, frames_grad = lax.optimization_barrier((others, frames_grad))
        local = local + others[0] if last else (local + others[0]) + (others[1] + others[2])
    kernel_grad, gain_grad, router_grad = kernel_call(
        last_kernel,
        (cores, local, swap(local, devices, 1)),
        (shape((KSIZE, width), F32), shape((1, width), F32), shape((experts, width), F32)),
        weight=0.0,
        scalars=(0,),
    )
    return (
        block_out,
        frames_grad,
        kernel_grad,
        gain_grad[0],
        router_grad.T,
        expert_in_grad[None],
        expert_out_grad[None],
    )


def solution(mesh):
    in_specs = (
        P(("groups", "seq"), None),
        P(),
        P(),
        P(),
        P("seq", None, None),
        P("seq", None, None),
        P(("groups", "seq"), None),
        P(("groups", "seq"), None),
    )
    out_specs = (
        P(("groups", "seq"), None),
        P(("groups", "seq"), None),
        P("groups", None),
        P("groups"),
        P("groups", None),
        P(("groups", "seq"), None, None),
        P(("groups", "seq"), None, None),
    )
    return jax.shard_map(
        per_device, mesh=mesh, in_specs=in_specs, out_specs=out_specs, check_vma=False
    )
```

```python
import functools

import jax
import jax.numpy as jnp
from jax import lax
from jax.experimental import pallas as pl
from jax.experimental.pallas import tpu as pltpu
from jax.sharding import PartitionSpec as P

KSIZE = 31
RIM = 16
LANES = 128
CHUNK = 256
NORM_EPS = 1e-05
F32 = jnp.float32
BF16 = jnp.bfloat16
LAST = (((1,), (1,)), ((), ()))
FIRST = (((0,), (0,)), ((), ()))
SMALL = 12 * 1024 * 1024
LARGE = 60 * 1024 * 1024
WEIGHTS = 24 * 1024 * 1024
FRONT = 3.3
WEIGHT = 0.15 * 3.6e6


def dot(a, b):
    return jnp.dot(a, b, preferred_element_type=F32)


def dot_last(a, b):
    return lax.dot_general(a, b, LAST, preferred_element_type=F32)


def dot_first(a, b):
    return lax.dot_general(a, b, FIRST, preferred_element_type=F32)


def slope_of(values):
    logistic = jax.nn.sigmoid(values)
    return logistic * (1.0 + values * (1.0 - logistic))


class Staged:
    def __init__(self, source, held, semaphore):
        self.held, self.copy = held, pltpu.make_async_copy(source, held, semaphore)
        self.shape, self.started, self.waited = held.shape, False, False

    def start(self):
        if not self.started:
            self.copy.start()
        self.started = True

    def wait(self):
        self.start()
        if not self.waited:
            self.copy.wait()
        self.waited = True

    def __getitem__(self, at):
        self.wait()
        return self.held[at]


class Rows:
    def __init__(self, array, start, size):
        self.array, self.start, self.shape, self.dtype = array, start, (size, array.shape[1]), array.dtype

    def of(self, ref):
        return ref.at[pl.ds(self.start, self.shape[0])]


def kernel_call(body, operands, outs, scratch=(), weight=0.0, limit=SMALL, scalars=(), first=None):
    count, out_count = len(operands), len(outs)
    staged = [place for place in range(count) if place not in scalars]
    held = [pltpu.VMEM(operands[place].shape, operands[place].dtype) for place in staged]
    results = [pltpu.VMEM(out.shape, out.dtype) for out in outs]

    def kernel(*refs):
        ins, out_refs, rest = refs[0:count], refs[count : count + out_count], refs[count + out_count :]
        copies, made, rest = rest[0 : len(staged)], rest[len(staged) : len(staged) + out_count], rest[len(staged) + out_count :]
        in_semaphores, out_semaphores, rest = rest[0], rest[1], rest[2:]
        values = list(ins)
        for turn, place in enumerate(staged):
            source = operands[place].of(ins[place]) if isinstance(operands[place], Rows) else ins[place]
            values[place] = Staged(source, copies[turn], in_semaphores.at[turn])
            if first is None or place < first:
                values[place].start()
        writes = [
            pltpu.make_async_copy(buffer, out, out_semaphores.at[turn])
            for turn, (buffer, out) in enumerate(zip(made, out_refs))
        ]
        started = []

        def write(*turns):
            for turn in turns:
                writes[turn].start()
                started.append(turn)

        body(values, made, rest, write)
        for value in values:
            if isinstance(value, Staged):
                value.wait()
        write(*[turn for turn in range(out_count) if turn not in started])
        for copy in writes:
            copy.wait()

    return pl.pallas_call(
        kernel,
        out_shape=tuple(outs),
        in_specs=[pl.BlockSpec(memory_space=pltpu.SMEM if place in scalars else pl.ANY) for place in range(count)],
        out_specs=tuple(pl.BlockSpec(memory_space=pl.ANY) for _ in outs),
        scratch_shapes=held + results + [pltpu.SemaphoreType.DMA((len(staged),)), pltpu.SemaphoreType.DMA((out_count,))] + list(scratch),
        compiler_params=pltpu.CompilerParams(vmem_limit_bytes=limit),
        cost_estimate=pl.CostEstimate(flops=1, bytes_accessed=int(WEIGHT * weight) + 1, transcendentals=0),
    )(*[each.array if isinstance(each, Rows) else each for each in operands])


def columns_of(ids):
    count = ids.shape[1]
    row = lax.broadcasted_iota(jnp.int32, (count, count), 0)
    col = lax.broadcasted_iota(jnp.int32, (count, count), 1)
    return dot_last((row == col).astype(BF16), ids.astype(F32).astype(BF16)).astype(jnp.int32)


def choices(ids, experts):
    lane = lax.broadcasted_iota(jnp.int32, (ids.shape[0], experts), 1)
    return (ids[:, 0:1] == lane).astype(F32), (ids[:, 1:2] == lane).astype(F32)


def placements(ids, chip, near, capacity):
    count = ids.shape[0]
    first, second = choices(ids ^ chip, near)
    named = (first + second).astype(BF16)
    row = lax.broadcasted_iota(jnp.int32, (count, count), 0)
    col = lax.broadcasted_iota(jnp.int32, (count, count), 1)
    before = dot((col < row).astype(BF16), named)
    start = lax.broadcasted_iota(jnp.int32, (count, near), 1).astype(F32) * capacity
    place = before + start + 1.0
    slot = lax.broadcasted_iota(jnp.int32, (count, near * capacity), 1)
    picks = []
    for chosen in (first, second):
        at = jnp.sum(chosen * place, axis=1, keepdims=True).astype(jnp.int32) - 1
        picks.append((slot == at).astype(BF16))
    return picks


def pack_kernel(near, capacity, ins, outs, scratch, write):
    chip, names, rows = ins
    count = rows.shape[0]
    first, second = placements(columns_of(ids_of(names[...], count)), chip[0], near, capacity)
    packed = dot_first(first + second, rows[...]).astype(BF16)
    for place, out in enumerate(outs):
        out[...] = packed[place * capacity : (place + 1) * capacity]


def pack_both_kernel(near, capacity, ins, outs, scratch, write):
    chip, names, rows, far_names, far_rows = ins
    for block, (these, source) in enumerate(((names, rows), (far_names, far_rows))):
        count = source.shape[0]
        first, second = placements(columns_of(ids_of(these[...], count)), chip[0], near, capacity)
        packed = dot_first(first + second, source[...]).astype(BF16)
        for place, out in enumerate(outs):
            out[block * capacity : (block + 1) * capacity, :] = packed[place * capacity : (place + 1) * capacity]


def ids_of(names, count):
    return names[:, 0:count][0:2].astype(F32).astype(jnp.int32)


def all_of(refs):
    return jnp.concatenate([ref[...] for ref in refs], axis=0)


def shifted(pad_ref, lanes, count):
    for rest in range(8):
        block = pad_ref[pl.ds(rest, count + 24), lanes]
        for turn in range(4):
            offset = 8 * turn + rest
            if 1 <= offset <= KSIZE:
                yield offset, block[8 * turn : 8 * turn + count]


def fill_padded(pad_ref, core, twin, mid, other):
    count = mid.shape[0]
    after = RIM + count
    pad_ref[pl.ds(pl.multiple_of((1 - core) * after, 8), RIM), :] = twin[...].astype(F32)
    pad_ref[RIM:after, :] = mid[...].astype(F32)
    pad_ref[pl.ds(pl.multiple_of(core * after, 8), RIM), :] = other[...].astype(F32)


def lane_loop(width, body):
    @pl.loop(0, width // LANES)
    def _(step):
        body(pl.ds(pl.multiple_of(step * LANES, LANES), LANES))


def convolve_and_norm(core, frames, twin, other, taps, gain, conv_ref, normed_ref, scratch):
    pad_ref, taps32_ref, mixed_ref, square_ref = scratch
    count, width = frames.shape
    fill_padded(pad_ref, core, twin, frames, other)
    taps32_ref[...] = taps[...].astype(F32)
    square_ref[...] = jnp.zeros_like(square_ref)

    def conv(lanes):
        total = jnp.zeros((count, LANES), F32)
        for offset, rows in shifted(pad_ref, lanes, count):
            total = total + taps32_ref[offset - 1 : offset, lanes] * rows
        if conv_ref is not None:
            conv_ref[:, lanes] = total
        mixed = pad_ref[RIM : RIM + count, lanes] + total * jax.nn.sigmoid(total)
        mixed_ref[:, lanes] = mixed
        square_ref[...] += mixed * mixed

    lane_loop(width, conv)
    mean = jnp.sum(square_ref[...], axis=1, keepdims=True) / width
    inverse = lax.rsqrt(mean + NORM_EPS)
    normed_ref[...] = (mixed_ref[...] * inverse * gain[...].astype(F32)).astype(BF16)


def front_kernel(near, capacity, ins, outs, scratch, write):
    chip, core, frames, twin, other, taps, gain, names = ins
    conv, normed, parts = outs[0], outs[1], outs[2:]
    convolve_and_norm(core[0], frames, twin, other, taps, gain, conv, normed, scratch)
    write(0, 1)
    pack_kernel(near, capacity, (chip, names, normed), parts, scratch, write)


def far_front_kernel(near, capacity, ins, outs, scratch, write):
    chip, core, frames, rims_and_names, taps, gain = ins
    names, normed, parts = outs[0], outs[1], outs[2:]
    twin, other = rims_and_names[0:RIM, :], rims_and_names[RIM : 2 * RIM, :]
    even = core[0] == 0
    first = jnp.where(even, twin.astype(F32)[RIM - 1 : RIM], twin.astype(F32)[0:1])
    last = jnp.where(even, other.astype(F32)[0:1], other.astype(F32)[RIM - 1 : RIM])
    names[...] = jnp.concatenate([first, last, jnp.zeros((RIM - 2, frames.shape[1]), F32)], axis=0).astype(BF16)
    convolve_and_norm(core[0], frames, twin, other, taps, gain, None, normed, scratch)
    write(0, 1)
    pack_kernel(near, capacity, (chip, names, normed), parts, scratch, write)


def result_kernel(near, capacity, ins, outs, scratch, write):
    chip, router, blocks, rows_refs = ins[0], ins[1], (ins[2:4], ins[4:6]), ins[6:]
    for block, (names, normed) in reversed(list(enumerate(blocks))):
        ids = columns_of(ids_of(names[...], normed.shape[0]))
        gates = jax.nn.sigmoid(dot_last(normed[...], router[...]))
        rows = jnp.concatenate([ref[block * capacity : (block + 1) * capacity, :] for ref in rows_refs], axis=0)
        added = jnp.zeros(outs[block].shape, F32)
        for pick, chosen in zip(placements(ids, chip[0], near, capacity), choices(ids, gates.shape[1])):
            added = added + jnp.sum(chosen * gates, axis=1, keepdims=True) * dot(pick, rows)
        outs[block][...] = added.astype(outs[block].dtype)
        write(block)


def block_kernel(ins, outs, scratch, write):
    near_sum, mixed, far_sum = ins
    outs[0][...] = (mixed[...] + (near_sum[...] + far_sum[...].astype(F32))).astype(BF16)


def back_kernel(near, capacity, ins, outs, scratch, write):
    chip, names, rows_refs = ins[0], ins[1], ins[2:]
    count = outs[0].shape[0]
    first, second = placements(columns_of(ids_of(names[...], count)), chip[0], near, capacity)
    outs[0][...] = dot(first + second, all_of(rows_refs)).astype(outs[0].dtype)


def half_lanes(core, width):
    return pl.ds(pl.multiple_of(core * (width // 2), LANES), width // 2)


def final_kernel(ins, outs, scratch, write):
    core, frames, twin, other, conv, grad, gain, router, near_back, far_back = ins
    mixed_ref, mixed_grad_ref, conv_grad_ref, twin_ref, other_ref, kept_ref, given_ref = outs
    pad_ref, local_ref = scratch
    count, width = frames.shape
    fill_padded(pad_ref, core[0], twin, frames, other)
    conv_out = conv[...]
    logistic = jax.nn.sigmoid(conv_out)
    mixed = frames[...].astype(F32) + conv_out * logistic
    inverse = lax.rsqrt(jnp.sum(mixed * mixed, axis=1, keepdims=True) / width + NORM_EPS)
    local_ref[KSIZE + 1 :, :] = router[...]
    mixed_ref[...] = mixed
    write(0)
    grad_normed = near_back[...] + far_back[...].astype(F32)
    local_ref[KSIZE : KSIZE + 1, :] = jnp.sum(grad_normed * mixed * inverse, axis=0, keepdims=True)
    scaled = grad_normed * gain[...].astype(F32)
    mean = jnp.sum(scaled * mixed, axis=1, keepdims=True) / width
    mixed_grad = grad[...].astype(F32) + inverse * scaled - mixed * (inverse * inverse * inverse * mean)
    mixed_grad_ref[...] = mixed_grad
    conv_grad = (mixed_grad * (logistic * (1.0 + conv_out * (1.0 - logistic)))).astype(BF16)
    conv_grad_ref[...] = conv_grad
    twin_ref[...] = jnp.where(core[0] == 0, conv_grad[count - RIM : count], conv_grad[0:RIM])
    other_ref[...] = jnp.where(core[0] == 0, conv_grad[0:RIM], conv_grad[count - RIM : count])
    write(1, 2, 3, 4)

    def reduce(lanes):
        grad = conv_grad_ref[:, lanes].astype(F32)
        for offset, rows in shifted(pad_ref, lanes, count):
            local_ref[offset - 1 : offset, lanes] = jnp.sum(grad * rows, axis=0, keepdims=True)

    lane_loop(width, reduce)
    kept_ref[...] = local_ref[:, half_lanes(core[0], width)]
    given_ref[...] = local_ref[:, half_lanes(1 - core[0], width)]


def frames_kernel(ins, outs, scratch, write):
    core, mixed_grad, conv_grad, twin, other, taps = ins
    (out_ref,), (pad_ref, taps32_ref) = outs, scratch
    count, width = mixed_grad.shape
    fill_padded(pad_ref, core[0], twin, conv_grad, other)
    taps32_ref[...] = taps[...].astype(F32)
    mixed_grad.wait()

    def conv(lanes):
        total = mixed_grad[:, lanes]
        for offset, rows in shifted(pad_ref, lanes, count):
            total = total + taps32_ref[KSIZE - offset : KSIZE - offset + 1, lanes] * rows
        out_ref[:, lanes] = total.astype(BF16)

    lane_loop(width, conv)


def chunks(width):
    return [slice(start, start + CHUNK) for start in range(0, width, CHUNK)]


def gather_rows(refs, rows_ref):
    each = refs[0].shape[0]
    for place, ref in enumerate(refs):
        rows_ref[place * each : (place + 1) * each, :] = ref[...]


def gather_pairs(refs, rows_ref):
    each = refs[0].shape[0] // 2
    for place, ref in enumerate(refs):
        for block, start in enumerate((place * each, (len(refs) + place) * each)):
            rows_ref[start : start + each, :] = ref[block * each : (block + 1) * each, :]


def scatter_columns(refs, columns, values):
    each = refs[0].shape[0]
    for place, ref in enumerate(refs):
        ref[:, columns] = values[place * each : (place + 1) * each]


def scatter_pairs(refs, columns, values):
    each = refs[0].shape[0] // 2
    for place, ref in enumerate(refs):
        for block, start in enumerate((place * each, (len(refs) + place) * each)):
            ref[block * each : (block + 1) * each, columns] = values[start : start + each]


def forward_kernel(near, ins, outs, scratch, write):
    rows, (near_in, far_in, near_out, far_out) = ins[0 : 2 * near], ins[2 * near :]
    out_refs, (rows_ref, near_slope, far_slope, near_active, far_active) = outs[0:near], outs[near:]
    gather_rows(rows, rows_ref)
    near_in.wait()
    near_out.start()
    far_out.start()
    write(near)
    for weight, slope, active in ((near_in, near_slope, near_active), (far_in, far_slope, far_active)):
        weight.wait()
        for columns in chunks(weight.shape[1]):
            values = dot(rows_ref[...], weight[:, columns])
            logistic = jax.nn.sigmoid(values)
            active[:, columns] = (values * logistic).astype(BF16)
            slope[:, columns] = (logistic * (1.0 + values * (1.0 - logistic))).astype(BF16)
    write(near + 1, near + 2, near + 3, near + 4)
    near_out.wait()
    far_out.wait()
    for columns in chunks(near_out.shape[1]):
        total = dot(near_active[...], near_out[:, columns])
        total = total + dot(far_active[...], far_out[:, columns])
        scatter_pairs(out_refs, columns, total.astype(BF16))


def backward_kernel(near, ins, outs, scratch, write):
    chip, grads, rest = ins[0], ins[1 : near + 1], ins[near + 1 :]
    rows, router, near_out, far_out, near_slope, far_slope, near_active, far_active, near_in, far_in = rest
    out_refs, (near_grad, sent, router_out) = outs[0 : 2 * near], outs[2 * near :]
    grads_ref, dots_ref = scratch
    count = rows.shape[0]
    rows_part, active_part, grads_part, pre_part = (slice(turn * count, (turn + 1) * count) for turn in range(4))
    gather_pairs(grads, grads_ref)
    logits = dot_last(rows[...], router[...])
    mine = lax.broadcasted_iota(jnp.int32, logits.shape, 1) == chip[0]
    gate = jax.nn.sigmoid(jnp.sum(jnp.where(mine, logits, 0.0), axis=1, keepdims=True))
    sent[grads_part, :] = (gate * grads_ref[...].astype(F32)).astype(BF16)
    for later in rest[3:]:
        later.start()
    dots_ref[...] = jnp.zeros_like(dots_ref)
    for weight, slope, active, grad, part in (
        (near_out, near_slope, near_active, near_grad, slice(None)),
        (far_out, far_slope, far_active, sent, pre_part),
    ):
        for ref in (weight, slope, active):
            ref.wait()
        for columns in chunks(weight.shape[0]):
            hidden = dot_last(sent[grads_part, :], weight[columns, :])
            dots_ref[...] += hidden * active[:, columns].astype(F32)
            grad[part, columns] = (hidden * slope[:, columns].astype(F32)).astype(BF16)
    write(2 * near)
    sent[rows_part, :] = rows[...]
    sent[active_part, :] = far_active[...]
    write(2 * near + 1)
    chosen = jnp.sum(dots_ref[...], axis=1, keepdims=True) * (1.0 - gate)
    grad_logits = jnp.where(mine, chosen, 0.0).astype(BF16)
    router_out[...] = dot_first(grad_logits, rows[...])
    near_in.wait()
    far_in.wait()
    for columns in chunks(near_in.shape[0]):
        total = dot_last(near_grad[...], near_in[columns, :])
        total = total + dot_last(sent[pre_part, :], far_in[columns, :])
        total = total + dot(grad_logits, router[:, columns])
        scatter_columns(out_refs, columns, total.astype(BF16))


def weights_kernel(ins, outs, scratch, write):
    near_active, near_grad, near_part, far_part = ins
    in_grad, out_grad = outs
    count, width = near_active.shape
    rows_part, active_part, grads_part, pre_part = (slice(turn * count, (turn + 1) * count) for turn in range(4))
    for ref in ins:
        ref.wait()
    for columns in chunks(width):
        total = dot_first(near_active[:, columns], near_part[grads_part, :])
        out_grad[columns, :] = (total + dot_first(far_part[active_part, columns], far_part[grads_part, :])).astype(BF16)
    write(1)
    for columns in chunks(width):
        total = dot_first(near_part[rows_part, columns], near_grad[...])
        in_grad[columns, :] = (total + dot_first(far_part[rows_part, columns], far_part[pre_part, :])).astype(BF16)


def last_kernel(ins, outs, scratch, write):
    core, mine, other = ins
    taps_ref, gain_ref, router_ref = outs
    width = taps_ref.shape[1]
    for place, half in ((core[0], mine), (1 - core[0], other)):
        lanes = half_lanes(place, width)
        taps_ref[:, lanes] = half[0:KSIZE]
        gain_ref[:, lanes] = half[KSIZE : KSIZE + 1]
        router_ref[:, lanes] = half[KSIZE + 1 :]


def pair_up(values, count):
    pairs = [(i, i + 1) for i in range(1, count - 1, 2)]
    return lax.ppermute(values, "seq", pairs + [(j, i) for i, j in pairs])


def swap(values, count, bit):
    return lax.ppermute(values, "seq", [(i, i ^ bit) for i in range(count)])


def exchange(parts, devices):
    return [parts[0]] + [swap(part, devices, 2 * r) for r, part in enumerate(parts) if r]


def per_device(frames, conv_kernel, norm_gain, router, expert_in, expert_out, expert_ids, out_grad):
    count, width = frames.shape
    devices = lax.axis_size("seq")
    experts = devices // 2
    capacity = 8 * count // devices
    near = experts // 2
    slots = experts * capacity
    gain = norm_gain.reshape(1, width)
    taps = conv_kernel
    router = router.T
    ids = expert_ids.T
    shape = jax.ShapeDtypeStruct
    pad = pltpu.VMEM((count + 2 * RIM, width), F32)
    taps32 = pltpu.VMEM((KSIZE, width), F32)
    chip = lax.axis_index("seq") // 2
    chips = chip.reshape(1).astype(jnp.int32)
    cross = functools.partial(swap, count=devices, bit=devices // 2)

    core = lax.axis_index("seq") % 2
    cores = core.reshape(1).astype(jnp.int32)
    ends = (frames[count - RIM : count], frames[0:RIM])
    frames, to_twin, to_other = lax.optimization_barrier(
        (frames, jnp.where(core == 0, *ends), jnp.where(core == 0, *ends[::-1]))
    )
    twin, other = swap(to_twin, devices, 1), pair_up(to_other, devices)
    far_frames = cross(frames)
    names = jnp.pad(ids.astype(BF16), ((0, RIM - 2), (0, width - count)))
    weight_in, weight_out = expert_in[0], expert_out[0]
    other_in = swap(weight_in, devices, 1)
    other_out = swap(weight_out, devices, 1)
    twin, other, other_in, other_out = lax.optimization_barrier((twin, other, other_in, other_out))

    model32, model16 = shape((count, width), F32), shape((count, width), BF16)
    part = (shape((capacity, width), BF16),) * near
    pair = (shape((2 * capacity, width), BF16),) * near
    even = jnp.concatenate([twin[: RIM - 1], names[0:1], names[1:2], other[1:]])
    odd = jnp.concatenate([names[0:1], twin[1:], other[: RIM - 1], names[1:2]])
    far_rims = cross(jnp.where(core == 0, even, odd))
    front_scratch = (pad, taps32, pltpu.VMEM((count, width), F32), pltpu.VMEM((count, LANES), F32))
    conv_out, normed, *parts = kernel_call(
        functools.partial(front_kernel, near, capacity),
        (chips, cores, frames, twin, other, taps, gain, names),
        (model32, model16, *part),
        front_scratch,
        weight=FRONT,
        scalars=(0, 1),
    )
    rows = exchange(parts, devices)
    far_rims, far_frames, out_grad = lax.optimization_barrier((far_rims, far_frames, out_grad))
    far_grad = cross(out_grad)
    far_names, far_normed, *parts = kernel_call(
        functools.partial(far_front_kernel, near, capacity),
        (chips, cores, far_frames, far_rims, taps, gain),
        (shape((RIM, width), BF16), model16, *part),
        front_scratch,
        limit=LARGE,
        scalars=(0, 1),
    )
    rows, parts = lax.optimization_barrier((rows, parts))
    far_rows = exchange(parts, devices)
    parts = kernel_call(
        functools.partial(pack_both_kernel, near, capacity),
        (chips, names, out_grad, far_names, far_grad),
        pair,
        scalars=(0,),
    )
    far_rows, parts = lax.optimization_barrier((far_rows, parts))
    rows, grads = rows + far_rows, exchange(parts, devices)

    narrow = shape((slots, weight_in.shape[1]), BF16)
    outs = kernel_call(
        functools.partial(forward_kernel, near),
        (*rows, weight_in, other_in, weight_out, other_out),
        pair + (shape((slots, width), BF16), narrow, narrow, narrow, narrow),
        limit=LARGE,
        first=2 * near + 2,
    )
    parts, all_rows, slopes, (near_active, far_active) = outs[0:near], outs[near], outs[near + 1 : near + 3], outs[near + 3 :]
    results = exchange(parts, devices)
    outs = kernel_call(
        functools.partial(backward_kernel, near),
        (chips, *grads, all_rows, router, weight_out, other_out, *slopes, near_active, far_active, weight_in, other_in),
        2 * part + (narrow, shape((4 * slots, width), BF16), shape((experts, width), F32)),
        (pltpu.VMEM((slots, width), BF16), pltpu.VMEM((slots, CHUNK), F32)),
        limit=LARGE,
        first=near + 4,
        scalars=(0,),
    )
    results, outs = lax.optimization_barrier((results, outs))
    own_in, far_in, (near_grad, sent, router_local) = outs[0:near], outs[near : 2 * near], outs[2 * near :]
    backs = exchange(far_in, devices)
    near_sum, far_sum = kernel_call(
        functools.partial(result_kernel, near, capacity),
        (chips, router, names, normed, far_names, far_normed, *results),
        (model32, model16),
        weight=2.4,
        scalars=(0,),
    )
    backs, near_sum, far_sum = lax.optimization_barrier((backs, near_sum, far_sum))
    (far_back,) = kernel_call(
        functools.partial(back_kernel, near, capacity), (chips, far_names, *backs), (model16,), scalars=(0,)
    )
    far_back, own_in, far_sum = lax.optimization_barrier((far_back, own_in, far_sum))
    far_back = cross(far_back)
    grad = shape(weight_in.shape, BF16)
    expert_in_grad, expert_out_grad = kernel_call(
        weights_kernel, (near_active, near_grad, sent, swap(sent, devices, 1)), (grad, grad), limit=WEIGHTS
    )
    backs, expert_in_grad, expert_out_grad = lax.optimization_barrier(
        (exchange(own_in, devices), expert_in_grad, expert_out_grad)
    )
    (near_back,) = kernel_call(
        functools.partial(back_kernel, near, capacity), (chips, names, *backs), (model32,), scalars=(0,)
    )
    far_back, expert_in_grad, expert_out_grad = lax.optimization_barrier((far_back, expert_in_grad, expert_out_grad))
    far_sum = cross(far_sum)

    rim = shape((RIM, width), BF16)
    lines = KSIZE + 1 + experts
    columns = shape((lines, width // 2), F32)
    mixed, mixed_grad, conv_grad, to_twin, to_other, kept, given = kernel_call(
        final_kernel,
        (cores, frames, twin, other, conv_out, out_grad, gain, router_local, near_back, far_back),
        (model32, model32, model16, rim, rim, columns, columns),
        (pad, pltpu.VMEM((lines, width), F32)),
        weight=0.0,
        scalars=(0,),
    )
    grad_twin, grad_other = swap(to_twin, devices, 1), pair_up(to_other, devices)
    local = kept + swap(given, devices, 1)
    bit = 2
    while bit < devices:
        last = 4 * bit > devices
        others = [swap(local, devices, step) for step in ((bit,) if last else (bit, 2 * bit, 3 * bit))]
        if bit == 2:
            others, grad_twin, grad_other, far_sum = lax.optimization_barrier((others, grad_twin, grad_other, far_sum))
            (block_out,) = kernel_call(block_kernel, (near_sum, mixed, far_sum), (model16,))
            (frames_grad,) = kernel_call(
                frames_kernel,
                (cores, mixed_grad, conv_grad, grad_twin, grad_other, taps),
                (model16,),
                (pad, taps32),
                scalars=(0,),
            )
        bit *= 2 if last else 4
        if bit == devices:
            others, frames_grad, block_out = lax.optimization_barrier((others, frames_grad, block_out))
        local = local + others[0] if last else (local + others[0]) + (others[1] + others[2])
    kernel_grad, gain_grad, router_grad = kernel_call(
        last_kernel,
        (cores, local, swap(local, devices, 1)),
        (shape((KSIZE, width), F32), shape((1, width), F32), shape((experts, width), F32)),
        weight=0.0,
        scalars=(0,),
    )
    return (
        block_out,
        frames_grad,
        kernel_grad,
        gain_grad[0],
        router_grad.T,
        expert_in_grad[None],
        expert_out_grad[None],
    )


def solution(mesh):
    in_specs = (
        P(("groups", "seq"), None),
        P(),
        P(),
        P(),
        P("seq", None, None),
        P("seq", None, None),
        P(("groups", "seq"), None),
        P(("groups", "seq"), None),
    )
    out_specs = (
        P(("groups", "seq"), None),
        P(("groups", "seq"), None),
        P("groups", None),
        P("groups"),
        P("groups", None),
        P(("groups", "seq"), None, None),
        P(("groups", "seq"), None, None),
    )
    return jax.shard_map(
        per_device, mesh=mesh, in_specs=in_specs, out_specs=out_specs, check_vma=False
    )
```

```python
import functools

import jax
import jax.numpy as jnp
from jax import lax
from jax.experimental import pallas as pl
from jax.experimental.pallas import tpu as pltpu
from jax.sharding import PartitionSpec as P

KSIZE = 31
RIM = 16
LANES = 128
CHUNK = 256
NORM_EPS = 1e-05
F32 = jnp.float32
BF16 = jnp.bfloat16
LAST = (((1,), (1,)), ((), ()))
FIRST = (((0,), (0,)), ((), ()))
SMALL = 12 * 1024 * 1024
LARGE = 60 * 1024 * 1024
WEIGHTS = 24 * 1024 * 1024
FRONT = 3.3
WEIGHT = 0.15 * 3.6e6


def dot(a, b):
    return jnp.dot(a, b, preferred_element_type=F32)


def dot_last(a, b):
    return lax.dot_general(a, b, LAST, preferred_element_type=F32)


def dot_first(a, b):
    return lax.dot_general(a, b, FIRST, preferred_element_type=F32)


def slope_of(values):
    logistic = jax.nn.sigmoid(values)
    return logistic * (1.0 + values * (1.0 - logistic))


class Staged:
    def __init__(self, source, held, semaphore):
        self.held, self.copy = held, pltpu.make_async_copy(source, held, semaphore)
        self.shape, self.started, self.waited = held.shape, False, False

    def start(self):
        if not self.started:
            self.copy.start()
        self.started = True

    def wait(self):
        self.start()
        if not self.waited:
            self.copy.wait()
        self.waited = True

    def __getitem__(self, at):
        self.wait()
        return self.held[at]


class Rows:
    def __init__(self, array, start, size):
        self.array, self.start, self.shape, self.dtype = array, start, (size, array.shape[1]), array.dtype

    def of(self, ref):
        return ref.at[pl.ds(self.start, self.shape[0])]


def kernel_call(body, operands, outs, scratch=(), weight=0.0, limit=SMALL, scalars=(), first=None):
    count, out_count = len(operands), len(outs)
    staged = [place for place in range(count) if place not in scalars]
    held = [pltpu.VMEM(operands[place].shape, operands[place].dtype) for place in staged]
    results = [pltpu.VMEM(out.shape, out.dtype) for out in outs]

    def kernel(*refs):
        ins, out_refs, rest = refs[0:count], refs[count : count + out_count], refs[count + out_count :]
        copies, made, rest = rest[0 : len(staged)], rest[len(staged) : len(staged) + out_count], rest[len(staged) + out_count :]
        in_semaphores, out_semaphores, rest = rest[0], rest[1], rest[2:]
        values = list(ins)
        for turn, place in enumerate(staged):
            source = operands[place].of(ins[place]) if isinstance(operands[place], Rows) else ins[place]
            values[place] = Staged(source, copies[turn], in_semaphores.at[turn])
            if first is None or place < first:
                values[place].start()
        writes = [
            pltpu.make_async_copy(buffer, out, out_semaphores.at[turn])
            for turn, (buffer, out) in enumerate(zip(made, out_refs))
        ]
        started = []

        def write(*turns):
            for turn in turns:
                writes[turn].start()
                started.append(turn)

        body(values, made, rest, write)
        for value in values:
            if isinstance(value, Staged):
                value.wait()
        write(*[turn for turn in range(out_count) if turn not in started])
        for copy in writes:
            copy.wait()

    return pl.pallas_call(
        kernel,
        out_shape=tuple(outs),
        in_specs=[pl.BlockSpec(memory_space=pltpu.SMEM if place in scalars else pl.ANY) for place in range(count)],
        out_specs=tuple(pl.BlockSpec(memory_space=pl.ANY) for _ in outs),
        scratch_shapes=held + results + [pltpu.SemaphoreType.DMA((len(staged),)), pltpu.SemaphoreType.DMA((out_count,))] + list(scratch),
        compiler_params=pltpu.CompilerParams(vmem_limit_bytes=limit),
        cost_estimate=pl.CostEstimate(flops=1, bytes_accessed=int(WEIGHT * weight) + 1, transcendentals=0),
    )(*[each.array if isinstance(each, Rows) else each for each in operands])


def columns_of(ids):
    count = ids.shape[1]
    row = lax.broadcasted_iota(jnp.int32, (count, count), 0)
    col = lax.broadcasted_iota(jnp.int32, (count, count), 1)
    return dot_last((row == col).astype(BF16), ids.astype(F32).astype(BF16)).astype(jnp.int32)


def choices(ids, experts):
    lane = lax.broadcasted_iota(jnp.int32, (ids.shape[0], experts), 1)
    return (ids[:, 0:1] == lane).astype(F32), (ids[:, 1:2] == lane).astype(F32)


def placements(ids, chip, near, capacity):
    count = ids.shape[0]
    first, second = choices(ids ^ chip, near)
    named = (first + second).astype(BF16)
    row = lax.broadcasted_iota(jnp.int32, (count, count), 0)
    col = lax.broadcasted_iota(jnp.int32, (count, count), 1)
    before = dot((col < row).astype(BF16), named)
    start = lax.broadcasted_iota(jnp.int32, (count, near), 1).astype(F32) * capacity
    place = before + start + 1.0
    slot = lax.broadcasted_iota(jnp.int32, (count, near * capacity), 1)
    picks = []
    for chosen in (first, second):
        at = jnp.sum(chosen * place, axis=1, keepdims=True).astype(jnp.int32) - 1
        picks.append((slot == at).astype(BF16))
    return picks


def pack_kernel(near, capacity, ins, outs, scratch, write):
    chip, names, rows = ins
    count = rows.shape[0]
    first, second = placements(columns_of(ids_of(names[...], count)), chip[0], near, capacity)
    packed = dot_first(first + second, rows[...]).astype(BF16)
    for place, out in enumerate(outs):
        out[...] = packed[place * capacity : (place + 1) * capacity]


def pack_both_kernel(near, capacity, ins, outs, scratch, write):
    chip, names, rows, far_names, far_rows = ins
    for block, (these, source) in enumerate(((names, rows), (far_names, far_rows))):
        count = source.shape[0]
        first, second = placements(columns_of(ids_of(these[...], count)), chip[0], near, capacity)
        packed = dot_first(first + second, source[...]).astype(BF16)
        for place, out in enumerate(outs):
            out[block * capacity : (block + 1) * capacity, :] = packed[place * capacity : (place + 1) * capacity]


def ids_of(names, count):
    return names[:, 0:count][0:2].astype(F32).astype(jnp.int32)


def all_of(refs):
    return jnp.concatenate([ref[...] for ref in refs], axis=0)


def shifted(pad_ref, lanes, count):
    for rest in range(8):
        block = pad_ref[pl.ds(rest, count + 24), lanes]
        for turn in range(4):
            offset = 8 * turn + rest
            if 1 <= offset <= KSIZE:
                yield offset, block[8 * turn : 8 * turn + count]


def fill_padded(pad_ref, core, twin, mid, other):
    count = mid.shape[0]
    after = RIM + count
    pad_ref[pl.ds(pl.multiple_of((1 - core) * after, 8), RIM), :] = twin[...].astype(F32)
    pad_ref[RIM:after, :] = mid[...].astype(F32)
    pad_ref[pl.ds(pl.multiple_of(core * after, 8), RIM), :] = other[...].astype(F32)


def lane_loop(width, body):
    @pl.loop(0, width // LANES)
    def _(step):
        body(pl.ds(pl.multiple_of(step * LANES, LANES), LANES))


def convolve_and_norm(core, frames, twin, other, taps, gain, conv_ref, normed_ref, scratch):
    pad_ref, taps32_ref, mixed_ref, square_ref = scratch
    count, width = frames.shape
    fill_padded(pad_ref, core, twin, frames, other)
    taps32_ref[...] = taps[...].astype(F32)
    square_ref[...] = jnp.zeros_like(square_ref)

    def conv(lanes):
        total = jnp.zeros((count, LANES), F32)
        for offset, rows in shifted(pad_ref, lanes, count):
            total = total + taps32_ref[offset - 1 : offset, lanes] * rows
        if conv_ref is not None:
            conv_ref[:, lanes] = total
        mixed = pad_ref[RIM : RIM + count, lanes] + total * jax.nn.sigmoid(total)
        mixed_ref[:, lanes] = mixed
        square_ref[...] += mixed * mixed

    lane_loop(width, conv)
    mean = jnp.sum(square_ref[...], axis=1, keepdims=True) / width
    inverse = lax.rsqrt(mean + NORM_EPS)
    normed_ref[...] = (mixed_ref[...] * inverse * gain[...].astype(F32)).astype(BF16)


def front_kernel(near, capacity, ins, outs, scratch, write):
    chip, core, frames, twin, other, taps, gain, names = ins
    conv, normed, parts = outs[0], outs[1], outs[2:]
    convolve_and_norm(core[0], frames, twin, other, taps, gain, conv, normed, scratch)
    write(0, 1)
    pack_kernel(near, capacity, (chip, names, normed), parts, scratch, write)


def far_front_kernel(near, capacity, ins, outs, scratch, write):
    chip, core, frames, rims_and_names, taps, gain = ins
    names, normed, parts = outs[0], outs[1], outs[2:]
    twin, other = rims_and_names[0:RIM, :], rims_and_names[RIM : 2 * RIM, :]
    even = core[0] == 0
    first = jnp.where(even, twin.astype(F32)[RIM - 1 : RIM], twin.astype(F32)[0:1])
    last = jnp.where(even, other.astype(F32)[0:1], other.astype(F32)[RIM - 1 : RIM])
    names[...] = jnp.concatenate([first, last, jnp.zeros((RIM - 2, frames.shape[1]), F32)], axis=0).astype(BF16)
    convolve_and_norm(core[0], frames, twin, other, taps, gain, None, normed, scratch)
    write(0, 1)
    pack_kernel(near, capacity, (chip, names, normed), parts, scratch, write)


def result_kernel(near, capacity, ins, outs, scratch, write):
    chip, router, blocks, rows_refs = ins[0], ins[1], (ins[2:4], ins[4:6]), ins[6:]
    for block, (names, normed) in reversed(list(enumerate(blocks))):
        ids = columns_of(ids_of(names[...], normed.shape[0]))
        gates = jax.nn.sigmoid(dot_last(normed[...], router[...]))
        rows = jnp.concatenate([ref[block * capacity : (block + 1) * capacity, :] for ref in rows_refs], axis=0)
        added = jnp.zeros(outs[block].shape, F32)
        for pick, chosen in zip(placements(ids, chip[0], near, capacity), choices(ids, gates.shape[1])):
            added = added + jnp.sum(chosen * gates, axis=1, keepdims=True) * dot(pick, rows)
        outs[block][...] = added.astype(outs[block].dtype)
        write(block)


def block_kernel(ins, outs, scratch, write):
    near_sum, mixed, far_sum = ins
    outs[0][...] = (mixed[...] + (near_sum[...] + far_sum[...].astype(F32))).astype(BF16)


def back_kernel(near, capacity, ins, outs, scratch, write):
    chip, names, rows_refs = ins[0], ins[1], ins[2:]
    count = outs[0].shape[0]
    first, second = placements(columns_of(ids_of(names[...], count)), chip[0], near, capacity)
    outs[0][...] = dot(first + second, all_of(rows_refs)).astype(outs[0].dtype)


def half_lanes(core, width):
    return pl.ds(pl.multiple_of(core * (width // 2), LANES), width // 2)


def final_kernel(ins, outs, scratch, write):
    core, frames, twin, other, conv, grad, gain, router, near_back, far_back = ins
    mixed_ref, mixed_grad_ref, conv_grad_ref, twin_ref, other_ref, kept_ref, given_ref = outs
    pad_ref, local_ref = scratch
    count, width = frames.shape
    fill_padded(pad_ref, core[0], twin, frames, other)
    conv_out = conv[...]
    logistic = jax.nn.sigmoid(conv_out)
    mixed = frames[...].astype(F32) + conv_out * logistic
    inverse = lax.rsqrt(jnp.sum(mixed * mixed, axis=1, keepdims=True) / width + NORM_EPS)
    local_ref[KSIZE + 1 :, :] = router[...]
    mixed_ref[...] = mixed
    write(0)
    grad_normed = near_back[...] + far_back[...].astype(F32)
    local_ref[KSIZE : KSIZE + 1, :] = jnp.sum(grad_normed * mixed * inverse, axis=0, keepdims=True)
    scaled = grad_normed * gain[...].astype(F32)
    mean = jnp.sum(scaled * mixed, axis=1, keepdims=True) / width
    mixed_grad = grad[...].astype(F32) + inverse * scaled - mixed * (inverse * inverse * inverse * mean)
    mixed_grad_ref[...] = mixed_grad
    conv_grad = (mixed_grad * (logistic * (1.0 + conv_out * (1.0 - logistic)))).astype(BF16)
    conv_grad_ref[...] = conv_grad
    twin_ref[...] = jnp.where(core[0] == 0, conv_grad[count - RIM : count], conv_grad[0:RIM])
    other_ref[...] = jnp.where(core[0] == 0, conv_grad[0:RIM], conv_grad[count - RIM : count])
    write(1, 2, 3, 4)

    def reduce(lanes):
        grad = conv_grad_ref[:, lanes].astype(F32)
        for offset, rows in shifted(pad_ref, lanes, count):
            local_ref[offset - 1 : offset, lanes] = jnp.sum(grad * rows, axis=0, keepdims=True)

    lane_loop(width, reduce)
    kept_ref[...] = local_ref[:, half_lanes(core[0], width)]
    given_ref[...] = local_ref[:, half_lanes(1 - core[0], width)]


def frames_kernel(ins, outs, scratch, write):
    core, mixed_grad, conv_grad, twin, other, taps = ins
    (out_ref,), (pad_ref, taps32_ref) = outs, scratch
    count, width = mixed_grad.shape
    fill_padded(pad_ref, core[0], twin, conv_grad, other)
    taps32_ref[...] = taps[...].astype(F32)
    mixed_grad.wait()

    def conv(lanes):
        total = mixed_grad[:, lanes]
        for offset, rows in shifted(pad_ref, lanes, count):
            total = total + taps32_ref[KSIZE - offset : KSIZE - offset + 1, lanes] * rows
        out_ref[:, lanes] = total.astype(BF16)

    lane_loop(width, conv)


def chunks(width):
    return [slice(start, start + CHUNK) for start in range(0, width, CHUNK)]


def gather_rows(refs, rows_ref):
    each = refs[0].shape[0]
    for place, ref in enumerate(refs):
        rows_ref[place * each : (place + 1) * each, :] = ref[...]


def gather_pairs(refs, rows_ref):
    each = refs[0].shape[0] // 2
    for place, ref in enumerate(refs):
        for block, start in enumerate((place * each, (len(refs) + place) * each)):
            rows_ref[start : start + each, :] = ref[block * each : (block + 1) * each, :]


def scatter_columns(refs, columns, values):
    each = refs[0].shape[0]
    for place, ref in enumerate(refs):
        ref[:, columns] = values[place * each : (place + 1) * each]


def scatter_pairs(refs, columns, values):
    each = refs[0].shape[0] // 2
    for place, ref in enumerate(refs):
        for block, start in enumerate((place * each, (len(refs) + place) * each)):
            ref[block * each : (block + 1) * each, columns] = values[start : start + each]


def forward_kernel(near, ins, outs, scratch, write):
    chip, rows, (router, near_in, far_in, near_out, far_out) = ins[0], ins[1 : 2 * near + 1], ins[2 * near + 1 :]
    out_refs, (sent, near_slope, far_slope, near_active, gate_ref) = outs[0:near], outs[near:]
    count = near_slope.shape[0]
    rows_part, active_part = slice(0, count), slice(count, 2 * count)
    gather_rows(rows, sent)
    logits = dot_last(sent[rows_part, :], router[...])
    mine = lax.broadcasted_iota(jnp.int32, logits.shape, 1) == chip[0]
    gate_ref[...] = jax.nn.sigmoid(jnp.sum(jnp.where(mine, logits, 0.0), axis=1, keepdims=True))
    near_in.wait()
    near_out.start()
    far_out.start()
    for weight, slope, active, part in (
        (near_in, near_slope, near_active, slice(None)),
        (far_in, far_slope, sent, active_part),
    ):
        weight.wait()
        for columns in chunks(weight.shape[1]):
            values = dot(sent[rows_part, :], weight[:, columns])
            logistic = jax.nn.sigmoid(values)
            active[part, columns] = (values * logistic).astype(BF16)
            slope[:, columns] = (logistic * (1.0 + values * (1.0 - logistic))).astype(BF16)
    write(near, near + 1, near + 2, near + 3, near + 4)
    near_out.wait()
    far_out.wait()
    for columns in chunks(near_out.shape[1]):
        total = dot(near_active[...], near_out[:, columns])
        total = total + dot(sent[active_part, :], far_out[:, columns])
        scatter_pairs(out_refs, columns, total.astype(BF16))


def backward_kernel(near, ins, outs, scratch, write):
    chip, grads, rest = ins[0], ins[1 : near + 1], ins[near + 1 :]
    gate_ref, near_out, near_slope, near_active, far_out, far_slope, far_active, near_in, far_in, router, rows = rest
    out_refs, (near_grad, sent, router_out) = outs[0 : 2 * near], outs[2 * near :]
    grads_ref, dots_ref = scratch
    count = rows.shape[0]
    grads_part, pre_part = slice(0, count), slice(count, 2 * count)
    gather_pairs(grads, grads_ref)
    gate = gate_ref[...]
    sent[grads_part, :] = (gate * grads_ref[...].astype(F32)).astype(BF16)
    near_out.wait()
    for later in rest[2:]:
        later.start()
    dots_ref[...] = jnp.zeros_like(dots_ref)
    for weight, slope, active, grad, part in (
        (near_out, near_slope, near_active, near_grad, slice(None)),
        (far_out, far_slope, far_active, sent, pre_part),
    ):
        for ref in (weight, slope, active):
            ref.wait()
        for columns in chunks(weight.shape[0]):
            hidden = dot_last(sent[grads_part, :], weight[columns, :])
            product = hidden * active[:, columns].astype(F32)
            dots_ref[...] += sum(product[:, at : at + LANES] for at in range(0, CHUNK, LANES))
            grad[part, columns] = (hidden * slope[:, columns].astype(F32)).astype(BF16)
    write(2 * near, 2 * near + 1)
    chosen = (jnp.sum(dots_ref[...], axis=1, keepdims=True) * (1.0 - gate)).astype(BF16)
    experts = router.shape[0]
    mine = lax.broadcasted_iota(jnp.int32, (count, experts), 1) == chip[0]
    router_out[...] = dot_first(jnp.where(mine, chosen.astype(F32), 0.0).astype(BF16), rows[...])
    own = lax.broadcasted_iota(jnp.int32, router.shape, 0) == chip[0]
    router_row = jnp.sum(jnp.where(own, router[...].astype(F32), 0.0), axis=0, keepdims=True)
    chosen = chosen.astype(F32)
    near_in.wait()
    far_in.wait()
    for columns in chunks(near_in.shape[0]):
        total = dot_last(near_grad[...], near_in[columns, :])
        total = total + dot_last(sent[pre_part, :], far_in[columns, :])
        total = total + chosen * router_row[:, columns]
        scatter_columns(out_refs, columns, total.astype(BF16))


def weights_kernel(ins, outs, scratch, write):
    near_active, near_grads, far_active, far_grads, near_rows, near_grad, far_rows, far_grad = ins
    in_grad, out_grad = outs
    for turn, (a, b, c, d) in ((1, ins[0:4]), (0, ins[4:8])):
        for ref in (a, b, c, d):
            ref.wait()
        for ref in ins[4:8]:
            ref.start()
        for columns in chunks(a.shape[1]):
            total = dot_first(a[:, columns], b[...]) + dot_first(c[:, columns], d[...])
            outs[turn][columns, :] = total.astype(BF16)
        write(turn)


def last_kernel(ins, outs, scratch, write):
    core, mine, other = ins
    taps_ref, gain_ref, router_ref = outs
    width = taps_ref.shape[1]
    for place, half in ((core[0], mine), (1 - core[0], other)):
        lanes = half_lanes(place, width)
        taps_ref[:, lanes] = half[0:KSIZE]
        gain_ref[:, lanes] = half[KSIZE : KSIZE + 1]
        router_ref[:, lanes] = half[KSIZE + 1 :]


def pair_up(values, count):
    pairs = [(i, i + 1) for i in range(1, count - 1, 2)]
    return lax.ppermute(values, "seq", pairs + [(j, i) for i, j in pairs])


def swap(values, count, bit):
    return lax.ppermute(values, "seq", [(i, i ^ bit) for i in range(count)])


def exchange(parts, devices):
    return [parts[0]] + [swap(part, devices, 2 * r) for r, part in enumerate(parts) if r]


def per_device(frames, conv_kernel, norm_gain, router, expert_in, expert_out, expert_ids, out_grad):
    count, width = frames.shape
    devices = lax.axis_size("seq")
    experts = devices // 2
    capacity = 8 * count // devices
    near = experts // 2
    slots = experts * capacity
    gain = norm_gain.reshape(1, width)
    taps = conv_kernel
    router = router.T
    ids = expert_ids.T
    shape = jax.ShapeDtypeStruct
    pad = pltpu.VMEM((count + 2 * RIM, width), F32)
    taps32 = pltpu.VMEM((KSIZE, width), F32)
    chip = lax.axis_index("seq") // 2
    chips = chip.reshape(1).astype(jnp.int32)
    cross = functools.partial(swap, count=devices, bit=devices // 2)

    core = lax.axis_index("seq") % 2
    cores = core.reshape(1).astype(jnp.int32)
    ends = (frames[count - RIM : count], frames[0:RIM])
    frames, to_twin, to_other = lax.optimization_barrier(
        (frames, jnp.where(core == 0, *ends), jnp.where(core == 0, *ends[::-1]))
    )
    twin, other = swap(to_twin, devices, 1), pair_up(to_other, devices)
    far_frames = cross(frames)
    names = jnp.pad(ids.astype(BF16), ((0, RIM - 2), (0, width - count)))
    weight_in, weight_out = expert_in[0], expert_out[0]
    other_in = swap(weight_in, devices, 1)
    other_out = swap(weight_out, devices, 1)
    twin, other, other_in, other_out = lax.optimization_barrier((twin, other, other_in, other_out))

    model32, model16 = shape((count, width), F32), shape((count, width), BF16)
    part = (shape((capacity, width), BF16),) * near
    pair = (shape((2 * capacity, width), BF16),) * near
    even = jnp.concatenate([twin[: RIM - 1], names[0:1], names[1:2], other[1:]])
    odd = jnp.concatenate([names[0:1], twin[1:], other[: RIM - 1], names[1:2]])
    far_rims = cross(jnp.where(core == 0, even, odd))
    front_scratch = (pad, taps32, pltpu.VMEM((count, width), F32), pltpu.VMEM((count, LANES), F32))
    conv_out, normed, *parts = kernel_call(
        functools.partial(front_kernel, near, capacity),
        (chips, cores, frames, twin, other, taps, gain, names),
        (model32, model16, *part),
        front_scratch,
        weight=FRONT,
        limit=LARGE,
        scalars=(0, 1),
    )
    rows = exchange(parts, devices)
    far_rims, far_frames, out_grad = lax.optimization_barrier((far_rims, far_frames, out_grad))
    far_grad = cross(out_grad)
    far_names, far_normed, *parts = kernel_call(
        functools.partial(far_front_kernel, near, capacity),
        (chips, cores, far_frames, far_rims, taps, gain),
        (shape((RIM, width), BF16), model16, *part),
        front_scratch,
        limit=LARGE,
        scalars=(0, 1),
    )
    rows, parts = lax.optimization_barrier((rows, parts))
    far_rows = exchange(parts, devices)
    parts = kernel_call(
        functools.partial(pack_both_kernel, near, capacity),
        (chips, names, out_grad, far_names, far_grad),
        pair,
        limit=LARGE,
        scalars=(0,),
    )
    far_rows, parts = lax.optimization_barrier((far_rows, parts))
    rows, grads = rows + far_rows, exchange(parts, devices)

    narrow = shape((slots, weight_in.shape[1]), BF16)
    *parts, sent, near_slope, far_slope, near_active, gate = kernel_call(
        functools.partial(forward_kernel, near),
        (chips, *rows, router, weight_in, other_in, weight_out, other_out),
        pair + (shape((2 * slots, width), BF16), narrow, narrow, narrow, shape((slots, 1), F32)),
        limit=LARGE,
        first=2 * near + 4,
        scalars=(0,),
    )
    results = exchange(parts, devices)
    all_rows, far_active = Rows(sent, 0, slots), Rows(sent, slots, slots)
    outs = kernel_call(
        functools.partial(backward_kernel, near),
        (chips, *grads, gate, weight_out, near_slope, near_active, other_out, far_slope, far_active)
        + (weight_in, other_in, router, all_rows),
        2 * part + (narrow, shape((2 * slots, width), BF16), shape((experts, width), F32)),
        (pltpu.VMEM((slots, width), BF16), pltpu.VMEM((slots, LANES), F32)),
        limit=LARGE,
        first=near + 3,
        scalars=(0,),
    )
    results, outs, sent = lax.optimization_barrier((results, outs, sent))
    own_in, far_in, (near_grad, sent_grads, router_local) = outs[0:near], outs[near : 2 * near], outs[2 * near :]
    backs = exchange(far_in, devices)
    near_sum, far_sum = kernel_call(
        functools.partial(result_kernel, near, capacity),
        (chips, router, names, normed, far_names, far_normed, *results),
        (model32, model16),
        weight=2.4,
        scalars=(0,),
    )
    come, come_grads = swap(sent, devices, 1), swap(sent_grads, devices, 1)
    backs[1], own_in, come, come_grads = lax.optimization_barrier((backs[1], own_in, come, come_grads))
    own_backs = exchange(own_in, devices)
    backs, near_sum, far_sum = lax.optimization_barrier((backs, near_sum, far_sum))
    (far_back,) = kernel_call(
        functools.partial(back_kernel, near, capacity), (chips, far_names, *backs), (model16,), scalars=(0,)
    )
    far_back, far_sum = lax.optimization_barrier((far_back, far_sum))
    far_back = cross(far_back)
    grad = shape(weight_in.shape, BF16)
    first, second = (functools.partial(Rows, start=start, size=slots) for start in (0, slots))
    expert_in_grad, expert_out_grad = kernel_call(
        weights_kernel,
        (near_active, first(sent_grads), second(come), first(come_grads))
        + (first(sent), near_grad, first(come), second(come_grads)),
        (grad, grad),
        limit=WEIGHTS,
        first=4,
    )
    backs, expert_in_grad, expert_out_grad = lax.optimization_barrier(
        (own_backs, expert_in_grad, expert_out_grad)
    )
    (near_back,) = kernel_call(
        functools.partial(back_kernel, near, capacity), (chips, names, *backs), (model32,), scalars=(0,)
    )
    far_back, expert_in_grad, expert_out_grad = lax.optimization_barrier((far_back, expert_in_grad, expert_out_grad))
    far_sum = cross(far_sum)

    rim = shape((RIM, width), BF16)
    lines = KSIZE + 1 + experts
    columns = shape((lines, width // 2), F32)
    mixed, mixed_grad, conv_grad, to_twin, to_other, kept, given = kernel_call(
        final_kernel,
        (cores, frames, twin, other, conv_out, out_grad, gain, router_local, near_back, far_back),
        (model32, model32, model16, rim, rim, columns, columns),
        (pad, pltpu.VMEM((lines, width), F32)),
        weight=0.0,
        scalars=(0,),
    )
    grad_twin, grad_other = swap(to_twin, devices, 1), pair_up(to_other, devices)
    local = kept + swap(given, devices, 1)
    bit = 2
    while bit < devices:
        last = 4 * bit > devices
        others = [swap(local, devices, step) for step in ((bit,) if last else (bit, 2 * bit, 3 * bit))]
        if bit == 2:
            others, grad_twin, grad_other, far_sum = lax.optimization_barrier((others, grad_twin, grad_other, far_sum))
            (block_out,) = kernel_call(block_kernel, (near_sum, mixed, far_sum), (model16,))
            (frames_grad,) = kernel_call(
                frames_kernel,
                (cores, mixed_grad, conv_grad, grad_twin, grad_other, taps),
                (model16,),
                (pad, taps32),
                scalars=(0,),
            )
        bit *= 2 if last else 4
        if bit == devices:
            others, frames_grad = lax.optimization_barrier((others, frames_grad))
        local = local + others[0] if last else (local + others[0]) + (others[1] + others[2])
    kernel_grad, gain_grad, router_grad = kernel_call(
        last_kernel,
        (cores, local, swap(local, devices, 1)),
        (shape((KSIZE, width), F32), shape((1, width), F32), shape((experts, width), F32)),
        weight=0.0,
        scalars=(0,),
    )
    return (
        block_out,
        frames_grad,
        kernel_grad,
        gain_grad[0],
        router_grad.T,
        expert_in_grad[None],
        expert_out_grad[None],
    )


def solution(mesh):
    in_specs = (
        P(("groups", "seq"), None),
        P(),
        P(),
        P(),
        P("seq", None, None),
        P("seq", None, None),
        P(("groups", "seq"), None),
        P(("groups", "seq"), None),
    )
    out_specs = (
        P(("groups", "seq"), None),
        P(("groups", "seq"), None),
        P("groups", None),
        P("groups"),
        P("groups", None),
        P(("groups", "seq"), None, None),
        P(("groups", "seq"), None, None),
    )
    return jax.shard_map(
        per_device, mesh=mesh, in_specs=in_specs, out_specs=out_specs, check_vma=False
    )
```

```python
import functools

import jax
import jax.numpy as jnp
from jax import lax
from jax.experimental import pallas as pl
from jax.experimental.pallas import tpu as pltpu
from jax.sharding import PartitionSpec as P

KSIZE = 31
RIM = 16
LANES = 128
CHUNK = 256
NORM_EPS = 1e-05
F32 = jnp.float32
BF16 = jnp.bfloat16
LAST = (((1,), (1,)), ((), ()))
FIRST = (((0,), (0,)), ((), ()))
SMALL = 12 * 1024 * 1024
LARGE = 60 * 1024 * 1024
WEIGHTS = 24 * 1024 * 1024
FRONT = 3.3
WEIGHT = 0.15 * 3.6e6


def dot(a, b):
    return jnp.dot(a, b, preferred_element_type=F32)


def dot_last(a, b):
    return lax.dot_general(a, b, LAST, preferred_element_type=F32)


def dot_first(a, b):
    return lax.dot_general(a, b, FIRST, preferred_element_type=F32)


def slope_of(values):
    logistic = jax.nn.sigmoid(values)
    return logistic * (1.0 + values * (1.0 - logistic))


class Staged:
    def __init__(self, source, held, semaphore):
        self.held, self.copy = held, pltpu.make_async_copy(source, held, semaphore)
        self.shape, self.started, self.waited = held.shape, False, False

    def start(self):
        if not self.started:
            self.copy.start()
        self.started = True

    def wait(self):
        self.start()
        if not self.waited:
            self.copy.wait()
        self.waited = True

    def __getitem__(self, at):
        self.wait()
        return self.held[at]


class Rows:
    def __init__(self, array, start, size):
        self.array, self.start, self.shape, self.dtype = array, start, (size, array.shape[1]), array.dtype

    def of(self, ref):
        return ref.at[pl.ds(self.start, self.shape[0])]


def kernel_call(body, operands, outs, scratch=(), weight=0.0, limit=SMALL, scalars=(), first=None):
    count, out_count = len(operands), len(outs)
    staged = [place for place in range(count) if place not in scalars]
    held = [pltpu.VMEM(operands[place].shape, operands[place].dtype) for place in staged]
    results = [pltpu.VMEM(out.shape, out.dtype) for out in outs]

    def kernel(*refs):
        ins, out_refs, rest = refs[0:count], refs[count : count + out_count], refs[count + out_count :]
        copies, made, rest = rest[0 : len(staged)], rest[len(staged) : len(staged) + out_count], rest[len(staged) + out_count :]
        in_semaphores, out_semaphores, rest = rest[0], rest[1], rest[2:]
        values = list(ins)
        for turn, place in enumerate(staged):
            source = operands[place].of(ins[place]) if isinstance(operands[place], Rows) else ins[place]
            values[place] = Staged(source, copies[turn], in_semaphores.at[turn])
            if first is None or place < first:
                values[place].start()
        writes = [
            pltpu.make_async_copy(buffer, out, out_semaphores.at[turn])
            for turn, (buffer, out) in enumerate(zip(made, out_refs))
        ]
        started = []

        def write(*turns):
            for turn in turns:
                writes[turn].start()
                started.append(turn)

        body(values, made, rest, write)
        for value in values:
            if isinstance(value, Staged):
                value.wait()
        write(*[turn for turn in range(out_count) if turn not in started])
        for copy in writes:
            copy.wait()

    return pl.pallas_call(
        kernel,
        out_shape=tuple(outs),
        in_specs=[pl.BlockSpec(memory_space=pltpu.SMEM if place in scalars else pl.ANY) for place in range(count)],
        out_specs=tuple(pl.BlockSpec(memory_space=pl.ANY) for _ in outs),
        scratch_shapes=held + results + [pltpu.SemaphoreType.DMA((len(staged),)), pltpu.SemaphoreType.DMA((out_count,))] + list(scratch),
        compiler_params=pltpu.CompilerParams(vmem_limit_bytes=limit),
        cost_estimate=pl.CostEstimate(flops=1, bytes_accessed=int(WEIGHT * weight) + 1, transcendentals=0),
    )(*[each.array if isinstance(each, Rows) else each for each in operands])


def columns_of(ids):
    count = ids.shape[1]
    row = lax.broadcasted_iota(jnp.int32, (count, count), 0)
    col = lax.broadcasted_iota(jnp.int32, (count, count), 1)
    return dot_last((row == col).astype(BF16), ids.astype(F32).astype(BF16)).astype(jnp.int32)


def choices(ids, experts):
    lane = lax.broadcasted_iota(jnp.int32, (ids.shape[0], experts), 1)
    return (ids[:, 0:1] == lane).astype(F32), (ids[:, 1:2] == lane).astype(F32)


def placements(ids, chip, near, capacity):
    count = ids.shape[0]
    first, second = choices(ids ^ chip, near)
    named = (first + second).astype(BF16)
    row = lax.broadcasted_iota(jnp.int32, (count, count), 0)
    col = lax.broadcasted_iota(jnp.int32, (count, count), 1)
    before = dot((col < row).astype(BF16), named)
    start = lax.broadcasted_iota(jnp.int32, (count, near), 1).astype(F32) * capacity
    place = before + start + 1.0
    slot = lax.broadcasted_iota(jnp.int32, (count, near * capacity), 1)
    picks = []
    for chosen in (first, second):
        at = jnp.sum(chosen * place, axis=1, keepdims=True).astype(jnp.int32) - 1
        picks.append((slot == at).astype(BF16))
    return picks


def picks_of(names, count, chip, near, capacity):
    first, second = placements(columns_of(ids_of(names, count)), chip[0], near, capacity)
    return first + second


def pack_rows(picks, rows, outs):
    capacity = outs[0].shape[0]
    packed = dot_first(picks, rows).astype(BF16)
    for place, out in enumerate(outs):
        out[...] = packed[place * capacity : (place + 1) * capacity]


def pack_both_kernel(near, capacity, ins, outs, scratch, write):
    chip, names, rows, far_names, far_rows = ins
    count = rows.shape[0]
    picks = [picks_of(these[...], count, chip, near, capacity) for these in (names, far_names)]
    for block, source in enumerate((rows, far_rows)):
        packed = dot_first(picks[block], source[...]).astype(BF16)
        for place, out in enumerate(outs):
            out[block * capacity : (block + 1) * capacity, :] = packed[place * capacity : (place + 1) * capacity]


def ids_of(names, count):
    return names[:, 0:count][0:2].astype(F32).astype(jnp.int32)


def all_of(refs):
    return jnp.concatenate([ref[...] for ref in refs], axis=0)


def shifted(pad_ref, lanes, count):
    for rest in range(8):
        block = pad_ref[pl.ds(rest, count + 24), lanes]
        for turn in range(4):
            offset = 8 * turn + rest
            if 1 <= offset <= KSIZE:
                yield offset, block[8 * turn : 8 * turn + count]


def fill_padded(pad_ref, core, twin, mid, other):
    count = mid.shape[0]
    after = RIM + count
    pad_ref[pl.ds(pl.multiple_of((1 - core) * after, 8), RIM), :] = twin[...].astype(F32)
    pad_ref[RIM:after, :] = mid[...].astype(F32)
    pad_ref[pl.ds(pl.multiple_of(core * after, 8), RIM), :] = other[...].astype(F32)


def lane_loop(width, body):
    @pl.loop(0, width // LANES)
    def _(step):
        body(pl.ds(pl.multiple_of(step * LANES, LANES), LANES))


def convolve_and_norm(core, frames, twin, other, taps, gain, conv_ref, normed_ref, scratch):
    pad_ref, taps32_ref, mixed_ref, square_ref = scratch
    count, width = frames.shape
    fill_padded(pad_ref, core, twin, frames, other)
    taps32_ref[...] = taps[...].astype(F32)
    square_ref[...] = jnp.zeros_like(square_ref)

    def conv(lanes):
        total = jnp.zeros((count, LANES), F32)
        for offset, rows in shifted(pad_ref, lanes, count):
            total = total + taps32_ref[offset - 1 : offset, lanes] * rows
        if conv_ref is not None:
            conv_ref[:, lanes] = total
        mixed = pad_ref[RIM : RIM + count, lanes] + total * jax.nn.sigmoid(total)
        mixed_ref[:, lanes] = mixed
        square_ref[...] += mixed * mixed

    lane_loop(width, conv)
    mean = jnp.sum(square_ref[...], axis=1, keepdims=True) / width
    inverse = lax.rsqrt(mean + NORM_EPS)
    normed_ref[...] = (mixed_ref[...] * inverse * gain[...].astype(F32)).astype(BF16)


def front_kernel(near, capacity, ins, outs, scratch, write):
    chip, core, frames, twin, other, taps, gain, names = ins
    conv, normed, parts = outs[0], outs[1], outs[2:]
    picks_ref, scratch = scratch[0], scratch[1:]
    picks_ref[...] = picks_of(names[...], frames.shape[0], chip, near, capacity)
    convolve_and_norm(core[0], frames, twin, other, taps, gain, conv, normed, scratch)
    write(0, 1)
    pack_rows(picks_ref[...], normed[...], parts)


def far_front_kernel(near, capacity, ins, outs, scratch, write):
    chip, core, frames, rims_and_names, taps, gain = ins
    names, normed, parts = outs[0], outs[1], outs[2:]
    twin, other = rims_and_names[0:RIM, :], rims_and_names[RIM : 2 * RIM, :]
    even = core[0] == 0
    first = jnp.where(even, twin.astype(F32)[RIM - 1 : RIM], twin.astype(F32)[0:1])
    last = jnp.where(even, other.astype(F32)[0:1], other.astype(F32)[RIM - 1 : RIM])
    names[...] = jnp.concatenate([first, last, jnp.zeros((RIM - 2, frames.shape[1]), F32)], axis=0).astype(BF16)
    picks_ref, scratch = scratch[0], scratch[1:]
    picks_ref[...] = picks_of(names[...], frames.shape[0], chip, near, capacity)
    convolve_and_norm(core[0], frames, twin, other, taps, gain, None, normed, scratch)
    write(0, 1)
    pack_rows(picks_ref[...], normed[...], parts)


def result_kernel(near, capacity, ins, outs, scratch, write):
    chip, router, blocks, rows_refs = ins[0], ins[1], (ins[2:4], ins[4:6]), ins[6:]
    for block, (names, normed) in reversed(list(enumerate(blocks))):
        ids = columns_of(ids_of(names[...], normed.shape[0]))
        gates = jax.nn.sigmoid(dot_last(normed[...], router[...]))
        rows = jnp.concatenate([ref[block * capacity : (block + 1) * capacity, :] for ref in rows_refs], axis=0)
        added = jnp.zeros(outs[block].shape, F32)
        for pick, chosen in zip(placements(ids, chip[0], near, capacity), choices(ids, gates.shape[1])):
            added = added + jnp.sum(chosen * gates, axis=1, keepdims=True) * dot(pick, rows)
        outs[block][...] = added.astype(outs[block].dtype)
        write(block)


def block_kernel(ins, outs, scratch, write):
    near_sum, mixed, far_sum = ins
    outs[0][...] = (mixed[...] + (near_sum[...] + far_sum[...].astype(F32))).astype(BF16)


def back_kernel(near, capacity, ins, outs, scratch, write):
    chip, names, rows_refs = ins[0], ins[1], ins[2:]
    count = outs[0].shape[0]
    first, second = placements(columns_of(ids_of(names[...], count)), chip[0], near, capacity)
    outs[0][...] = dot(first + second, all_of(rows_refs)).astype(outs[0].dtype)


def half_lanes(core, width):
    return pl.ds(pl.multiple_of(core * (width // 2), LANES), width // 2)


def final_kernel(ins, outs, scratch, write):
    core, frames, twin, other, conv, grad, gain, router, near_back, far_back = ins
    mixed_ref, mixed_grad_ref, conv_grad_ref, twin_ref, other_ref, kept_ref, given_ref = outs
    pad_ref, local_ref = scratch
    count, width = frames.shape
    fill_padded(pad_ref, core[0], twin, frames, other)
    conv_out = conv[...]
    logistic = jax.nn.sigmoid(conv_out)
    mixed = frames[...].astype(F32) + conv_out * logistic
    inverse = lax.rsqrt(jnp.sum(mixed * mixed, axis=1, keepdims=True) / width + NORM_EPS)
    local_ref[KSIZE + 1 :, :] = router[...]
    mixed_ref[...] = mixed
    write(0)
    grad_normed = near_back[...] + far_back[...].astype(F32)
    local_ref[KSIZE : KSIZE + 1, :] = jnp.sum(grad_normed * mixed * inverse, axis=0, keepdims=True)
    scaled = grad_normed * gain[...].astype(F32)
    mean = jnp.sum(scaled * mixed, axis=1, keepdims=True) / width
    mixed_grad = grad[...].astype(F32) + inverse * scaled - mixed * (inverse * inverse * inverse * mean)
    mixed_grad_ref[...] = mixed_grad
    conv_grad = (mixed_grad * (logistic * (1.0 + conv_out * (1.0 - logistic)))).astype(BF16)
    conv_grad_ref[...] = conv_grad
    twin_ref[...] = jnp.where(core[0] == 0, conv_grad[count - RIM : count], conv_grad[0:RIM])
    other_ref[...] = jnp.where(core[0] == 0, conv_grad[0:RIM], conv_grad[count - RIM : count])
    write(1, 2, 3, 4)

    def reduce(lanes):
        grad = conv_grad_ref[:, lanes].astype(F32)
        for offset, rows in shifted(pad_ref, lanes, count):
            local_ref[offset - 1 : offset, lanes] = jnp.sum(grad * rows, axis=0, keepdims=True)

    lane_loop(width, reduce)
    kept_ref[...] = local_ref[:, half_lanes(core[0], width)]
    given_ref[...] = local_ref[:, half_lanes(1 - core[0], width)]


def frames_kernel(ins, outs, scratch, write):
    core, mixed_grad, conv_grad, twin, other, taps = ins
    (out_ref,), (pad_ref, taps32_ref) = outs, scratch
    count, width = mixed_grad.shape
    fill_padded(pad_ref, core[0], twin, conv_grad, other)
    taps32_ref[...] = taps[...].astype(F32)
    mixed_grad.wait()

    def conv(lanes):
        total = mixed_grad[:, lanes]
        for offset, rows in shifted(pad_ref, lanes, count):
            total = total + taps32_ref[KSIZE - offset : KSIZE - offset + 1, lanes] * rows
        out_ref[:, lanes] = total.astype(BF16)

    lane_loop(width, conv)


def chunks(width):
    return [slice(start, start + CHUNK) for start in range(0, width, CHUNK)]


def gather_rows(refs, rows_ref):
    each = refs[0].shape[0]
    for place, ref in enumerate(refs):
        rows_ref[place * each : (place + 1) * each, :] = ref[...]


def gather_pairs(refs, rows_ref):
    each = refs[0].shape[0] // 2
    for place, ref in enumerate(refs):
        for block, start in enumerate((place * each, (len(refs) + place) * each)):
            rows_ref[start : start + each, :] = ref[block * each : (block + 1) * each, :]


def scatter_columns(refs, columns, values):
    each = refs[0].shape[0]
    for place, ref in enumerate(refs):
        ref[:, columns] = values[place * each : (place + 1) * each]


def scatter_pairs(refs, columns, values):
    each = refs[0].shape[0] // 2
    for place, ref in enumerate(refs):
        for block, start in enumerate((place * each, (len(refs) + place) * each)):
            ref[block * each : (block + 1) * each, columns] = values[start : start + each]


def forward_kernel(near, ins, outs, scratch, write):
    chip, rows, (router, near_in, far_in, near_out, far_out) = ins[0], ins[1 : 2 * near + 1], ins[2 * near + 1 :]
    out_refs, (sent, near_slope, far_slope, near_active, gate_ref) = outs[0:near], outs[near:]
    count = near_slope.shape[0]
    rows_part, active_part = slice(0, count), slice(count, 2 * count)
    gather_rows(rows, sent)
    logits = dot_last(sent[rows_part, :], router[...])
    mine = lax.broadcasted_iota(jnp.int32, logits.shape, 1) == chip[0]
    gate_ref[...] = jax.nn.sigmoid(jnp.sum(jnp.where(mine, logits, 0.0), axis=1, keepdims=True))
    near_in.wait()
    near_out.start()
    far_out.start()
    for weight, slope, active, part in (
        (near_in, near_slope, near_active, slice(None)),
        (far_in, far_slope, sent, active_part),
    ):
        weight.wait()
        for columns in chunks(weight.shape[1]):
            values = dot(sent[rows_part, :], weight[:, columns])
            logistic = jax.nn.sigmoid(values)
            active[part, columns] = (values * logistic).astype(BF16)
            slope[:, columns] = (logistic * (1.0 + values * (1.0 - logistic))).astype(BF16)
    write(near, near + 1, near + 2, near + 3, near + 4)
    near_out.wait()
    far_out.wait()
    for columns in chunks(near_out.shape[1]):
        total = dot(near_active[...], near_out[:, columns])
        total = total + dot(sent[active_part, :], far_out[:, columns])
        scatter_pairs(out_refs, columns, total.astype(BF16))


def backward_kernel(near, ins, outs, scratch, write):
    chip, grads, rest = ins[0], ins[1 : near + 1], ins[near + 1 :]
    gate_ref, near_out, near_slope, near_active, far_out, far_slope, far_active, near_in, far_in, router, rows = rest
    out_refs, (near_grad, sent, router_out) = outs[0 : 2 * near], outs[2 * near :]
    grads_ref, dots_ref = scratch
    count = rows.shape[0]
    grads_part, pre_part = slice(0, count), slice(count, 2 * count)
    gather_pairs(grads, grads_ref)
    gate = gate_ref[...]
    sent[grads_part, :] = (gate * grads_ref[...].astype(F32)).astype(BF16)
    near_out.wait()
    for later in rest[2:]:
        later.start()
    dots_ref[...] = jnp.zeros_like(dots_ref)
    for weight, slope, active, grad, part in (
        (near_out, near_slope, near_active, near_grad, slice(None)),
        (far_out, far_slope, far_active, sent, pre_part),
    ):
        for ref in (weight, slope, active):
            ref.wait()
        for columns in chunks(weight.shape[0]):
            hidden = dot_last(sent[grads_part, :], weight[columns, :])
            product = hidden * active[:, columns].astype(F32)
            dots_ref[...] += sum(product[:, at : at + LANES] for at in range(0, CHUNK, LANES))
            grad[part, columns] = (hidden * slope[:, columns].astype(F32)).astype(BF16)
    write(2 * near, 2 * near + 1)
    chosen = (jnp.sum(dots_ref[...], axis=1, keepdims=True) * (1.0 - gate)).astype(BF16)
    experts = router.shape[0]
    mine = lax.broadcasted_iota(jnp.int32, (count, experts), 1) == chip[0]
    router_out[...] = dot_first(jnp.where(mine, chosen.astype(F32), 0.0).astype(BF16), rows[...])
    own = lax.broadcasted_iota(jnp.int32, router.shape, 0) == chip[0]
    router_row = jnp.sum(jnp.where(own, router[...].astype(F32), 0.0), axis=0, keepdims=True)
    chosen = chosen.astype(F32)
    near_in.wait()
    far_in.wait()
    for columns in chunks(near_in.shape[0]):
        total = dot_last(near_grad[...], near_in[columns, :])
        total = total + dot_last(sent[pre_part, :], far_in[columns, :])
        total = total + chosen * router_row[:, columns]
        scatter_columns(out_refs, columns, total.astype(BF16))


def weights_kernel(ins, outs, scratch, write):
    near_active, near_grads, far_active, far_grads, near_rows, near_grad, far_rows, far_grad = ins
    in_grad, out_grad = outs
    for turn, (a, b, c, d) in ((1, ins[0:4]), (0, ins[4:8])):
        for ref in (a, b, c, d):
            ref.wait()
        for ref in ins[4:8]:
            ref.start()
        for columns in chunks(a.shape[1]):
            total = dot_first(a[:, columns], b[...]) + dot_first(c[:, columns], d[...])
            outs[turn][columns, :] = total.astype(BF16)
        write(turn)


def last_kernel(ins, outs, scratch, write):
    core, mine, other = ins
    taps_ref, gain_ref, router_ref = outs
    width = taps_ref.shape[1]
    for place, half in ((core[0], mine), (1 - core[0], other)):
        lanes = half_lanes(place, width)
        taps_ref[:, lanes] = half[0:KSIZE]
        gain_ref[:, lanes] = half[KSIZE : KSIZE + 1]
        router_ref[:, lanes] = half[KSIZE + 1 :]


def pair_up(values, count):
    pairs = [(i, i + 1) for i in range(1, count - 1, 2)]
    return lax.ppermute(values, "seq", pairs + [(j, i) for i, j in pairs])


def swap(values, count, bit):
    return lax.ppermute(values, "seq", [(i, i ^ bit) for i in range(count)])


def exchange(parts, devices):
    return [parts[0]] + [swap(part, devices, 2 * r) for r, part in enumerate(parts) if r]


def per_device(frames, conv_kernel, norm_gain, router, expert_in, expert_out, expert_ids, out_grad):
    count, width = frames.shape
    devices = lax.axis_size("seq")
    experts = devices // 2
    capacity = 8 * count // devices
    near = experts // 2
    slots = experts * capacity
    gain = norm_gain.reshape(1, width)
    taps = conv_kernel
    router = router.T
    ids = expert_ids.T
    shape = jax.ShapeDtypeStruct
    pad = pltpu.VMEM((count + 2 * RIM, width), F32)
    taps32 = pltpu.VMEM((KSIZE, width), F32)
    chip = lax.axis_index("seq") // 2
    chips = chip.reshape(1).astype(jnp.int32)
    cross = functools.partial(swap, count=devices, bit=devices // 2)

    core = lax.axis_index("seq") % 2
    cores = core.reshape(1).astype(jnp.int32)
    ends = (frames[count - RIM : count], frames[0:RIM])
    frames, to_twin, to_other = lax.optimization_barrier(
        (frames, jnp.where(core == 0, *ends), jnp.where(core == 0, *ends[::-1]))
    )
    twin, other = swap(to_twin, devices, 1), pair_up(to_other, devices)
    far_frames = cross(frames)
    names = jnp.pad(ids.astype(BF16), ((0, RIM - 2), (0, width - count)))
    weight_in, weight_out = expert_in[0], expert_out[0]
    other_in = swap(weight_in, devices, 1)
    other_out = swap(weight_out, devices, 1)
    twin, other, other_in, other_out = lax.optimization_barrier((twin, other, other_in, other_out))

    model32, model16 = shape((count, width), F32), shape((count, width), BF16)
    part = (shape((capacity, width), BF16),) * near
    pair = (shape((2 * capacity, width), BF16),) * near
    even = jnp.concatenate([twin[: RIM - 1], names[0:1], names[1:2], other[1:]])
    odd = jnp.concatenate([names[0:1], twin[1:], other[: RIM - 1], names[1:2]])
    far_rims = cross(jnp.where(core == 0, even, odd))
    front_scratch = (pltpu.VMEM((count, near * capacity), BF16), pad, taps32)
    front_scratch += (pltpu.VMEM((count, width), F32), pltpu.VMEM((count, LANES), F32))
    conv_out, normed, *parts = kernel_call(
        functools.partial(front_kernel, near, capacity),
        (chips, cores, frames, twin, other, taps, gain, names),
        (model32, model16, *part),
        front_scratch,
        weight=FRONT,
        limit=LARGE,
        scalars=(0, 1),
    )
    rows = exchange(parts, devices)
    far_rims, far_frames, out_grad = lax.optimization_barrier((far_rims, far_frames, out_grad))
    far_grad = cross(out_grad)
    far_names, far_normed, *parts = kernel_call(
        functools.partial(far_front_kernel, near, capacity),
        (chips, cores, far_frames, far_rims, taps, gain),
        (shape((RIM, width), BF16), model16, *part),
        front_scratch,
        limit=LARGE,
        scalars=(0, 1),
    )
    rows, parts = lax.optimization_barrier((rows, parts))
    far_rows = exchange(parts, devices)
    parts = kernel_call(
        functools.partial(pack_both_kernel, near, capacity),
        (chips, names, out_grad, far_names, far_grad),
        pair,
        limit=LARGE,
        scalars=(0,),
    )
    far_rows, parts = lax.optimization_barrier((far_rows, parts))
    rows, grads = rows + far_rows, exchange(parts, devices)

    narrow = shape((slots, weight_in.shape[1]), BF16)
    *parts, sent, near_slope, far_slope, near_active, gate = kernel_call(
        functools.partial(forward_kernel, near),
        (chips, *rows, router, weight_in, other_in, weight_out, other_out),
        pair + (shape((2 * slots, width), BF16), narrow, narrow, narrow, shape((slots, 1), F32)),
        limit=LARGE,
        scalars=(0,),
    )
    results = exchange(parts, devices)
    all_rows, far_active = Rows(sent, 0, slots), Rows(sent, slots, slots)
    outs = kernel_call(
        functools.partial(backward_kernel, near),
        (chips, *grads, gate, weight_out, near_slope, near_active, other_out, far_slope, far_active)
        + (weight_in, other_in, router, all_rows),
        2 * part + (narrow, shape((2 * slots, width), BF16), shape((experts, width), F32)),
        (pltpu.VMEM((slots, width), BF16), pltpu.VMEM((slots, LANES), F32)),
        limit=LARGE,
        scalars=(0,),
    )
    results, outs, sent = lax.optimization_barrier((results, outs, sent))
    own_in, far_in, (near_grad, sent_grads, router_local) = outs[0:near], outs[near : 2 * near], outs[2 * near :]
    backs = exchange(far_in, devices)
    near_sum, far_sum = kernel_call(
        functools.partial(result_kernel, near, capacity),
        (chips, router, names, normed, far_names, far_normed, *results),
        (model32, model16),
        weight=2.4,
        scalars=(0,),
    )
    come, come_grads = swap(sent, devices, 1), swap(sent_grads, devices, 1)
    backs[1], own_in, come, come_grads = lax.optimization_barrier((backs[1], own_in, come, come_grads))
    own_backs = exchange(own_in, devices)
    backs, near_sum, far_sum = lax.optimization_barrier((backs, near_sum, far_sum))
    (far_back,) = kernel_call(
        functools.partial(back_kernel, near, capacity), (chips, far_names, *backs), (model16,), scalars=(0,)
    )
    far_back, far_sum = lax.optimization_barrier((far_back, far_sum))
    far_back = cross(far_back)
    grad = shape(weight_in.shape, BF16)
    first, second = (functools.partial(Rows, start=start, size=slots) for start in (0, slots))
    expert_in_grad, expert_out_grad = kernel_call(
        weights_kernel,
        (near_active, first(sent_grads), second(come), first(come_grads))
        + (first(sent), near_grad, first(come), second(come_grads)),
        (grad, grad),
        limit=WEIGHTS,
    )
    backs, expert_in_grad, expert_out_grad = lax.optimization_barrier(
        (own_backs, expert_in_grad, expert_out_grad)
    )
    (near_back,) = kernel_call(
        functools.partial(back_kernel, near, capacity), (chips, names, *backs), (model32,), scalars=(0,)
    )
    far_back, expert_in_grad, expert_out_grad = lax.optimization_barrier((far_back, expert_in_grad, expert_out_grad))
    far_sum = cross(far_sum)

    rim = shape((RIM, width), BF16)
    lines = KSIZE + 1 + experts
    columns = shape((lines, width // 2), F32)
    mixed, mixed_grad, conv_grad, to_twin, to_other, kept, given = kernel_call(
        final_kernel,
        (cores, frames, twin, other, conv_out, out_grad, gain, router_local, near_back, far_back),
        (model32, model32, model16, rim, rim, columns, columns),
        (pad, pltpu.VMEM((lines, width), F32)),
        weight=0.0,
        scalars=(0,),
    )
    grad_twin, grad_other = swap(to_twin, devices, 1), pair_up(to_other, devices)
    local = kept + swap(given, devices, 1)
    bit = 2
    while bit < devices:
        last = 4 * bit > devices
        others = [swap(local, devices, step) for step in ((bit,) if last else (bit, 2 * bit, 3 * bit))]
        if bit == 2:
            others, grad_twin, grad_other, far_sum = lax.optimization_barrier((others, grad_twin, grad_other, far_sum))
            (block_out,) = kernel_call(block_kernel, (near_sum, mixed, far_sum), (model16,))
            (frames_grad,) = kernel_call(
                frames_kernel,
                (cores, mixed_grad, conv_grad, grad_twin, grad_other, taps),
                (model16,),
                (pad, taps32),
                scalars=(0,),
            )
        bit *= 2 if last else 4
        if bit == devices:
            others, frames_grad = lax.optimization_barrier((others, frames_grad))
        local = local + others[0] if last else (local + others[0]) + (others[1] + others[2])
    kernel_grad, gain_grad, router_grad = kernel_call(
        last_kernel,
        (cores, local, swap(local, devices, 1)),
        (shape((KSIZE, width), F32), shape((1, width), F32), shape((experts, width), F32)),
        weight=0.0,
        scalars=(0,),
    )
    return (
        block_out,
        frames_grad,
        kernel_grad,
        gain_grad[0],
        router_grad.T,
        expert_in_grad[None],
        expert_out_grad[None],
    )


def solution(mesh):
    in_specs = (
        P(("groups", "seq"), None),
        P(),
        P(),
        P(),
        P("seq", None, None),
        P("seq", None, None),
        P(("groups", "seq"), None),
        P(("groups", "seq"), None),
    )
    out_specs = (
        P(("groups", "seq"), None),
        P(("groups", "seq"), None),
        P("groups", None),
        P("groups"),
        P("groups", None),
        P(("groups", "seq"), None, None),
        P(("groups", "seq"), None, None),
    )
    return jax.shard_map(
        per_device, mesh=mesh, in_specs=in_specs, out_specs=out_specs, check_vma=False
    )
```

```python
import functools

import jax
import jax.numpy as jnp
from jax import lax
from jax.experimental import pallas as pl
from jax.experimental.pallas import tpu as pltpu
from jax.sharding import PartitionSpec as P

KSIZE = 31
RIM = 16
LANES = 128
CHUNK = 256
NORM_EPS = 1e-05
F32 = jnp.float32
BF16 = jnp.bfloat16
LAST = (((1,), (1,)), ((), ()))
FIRST = (((0,), (0,)), ((), ()))
SMALL = 12 * 1024 * 1024
LARGE = 60 * 1024 * 1024
WEIGHTS = 24 * 1024 * 1024
FRONT = 3.3
WEIGHT = 0.15 * 3.6e6


def dot(a, b):
    return jnp.dot(a, b, preferred_element_type=F32)


def dot_last(a, b):
    return lax.dot_general(a, b, LAST, preferred_element_type=F32)


def dot_first(a, b):
    return lax.dot_general(a, b, FIRST, preferred_element_type=F32)


def slope_of(values):
    logistic = jax.nn.sigmoid(values)
    return logistic * (1.0 + values * (1.0 - logistic))


class Staged:
    def __init__(self, source, held, semaphore):
        self.held, self.copy = held, pltpu.make_async_copy(source, held, semaphore)
        self.shape, self.started, self.waited = held.shape, False, False

    def start(self):
        if not self.started:
            self.copy.start()
        self.started = True

    def wait(self):
        self.start()
        if not self.waited:
            self.copy.wait()
        self.waited = True

    def __getitem__(self, at):
        self.wait()
        return self.held[at]


class Rows:
    def __init__(self, array, start, size):
        self.array, self.start, self.shape, self.dtype = array, start, (size, array.shape[1]), array.dtype

    def of(self, ref):
        return ref.at[pl.ds(self.start, self.shape[0])]


def kernel_call(body, operands, outs, scratch=(), weight=0.0, limit=SMALL, scalars=(), first=None):
    count, out_count = len(operands), len(outs)
    staged = [place for place in range(count) if place not in scalars]
    held = [pltpu.VMEM(operands[place].shape, operands[place].dtype) for place in staged]
    results = [pltpu.VMEM(out.shape, out.dtype) for out in outs]

    def kernel(*refs):
        ins, out_refs, rest = refs[0:count], refs[count : count + out_count], refs[count + out_count :]
        copies, made, rest = rest[0 : len(staged)], rest[len(staged) : len(staged) + out_count], rest[len(staged) + out_count :]
        in_semaphores, out_semaphores, rest = rest[0], rest[1], rest[2:]
        values = list(ins)
        for turn, place in enumerate(staged):
            source = operands[place].of(ins[place]) if isinstance(operands[place], Rows) else ins[place]
            values[place] = Staged(source, copies[turn], in_semaphores.at[turn])
            if first is None or place < first:
                values[place].start()
        writes = [
            pltpu.make_async_copy(buffer, out, out_semaphores.at[turn])
            for turn, (buffer, out) in enumerate(zip(made, out_refs))
        ]
        started = []

        def write(*turns):
            for turn in turns:
                writes[turn].start()
                started.append(turn)

        body(values, made, rest, write)
        for value in values:
            if isinstance(value, Staged):
                value.wait()
        write(*[turn for turn in range(out_count) if turn not in started])
        for copy in writes:
            copy.wait()

    return pl.pallas_call(
        kernel,
        out_shape=tuple(outs),
        in_specs=[pl.BlockSpec(memory_space=pltpu.SMEM if place in scalars else pl.ANY) for place in range(count)],
        out_specs=tuple(pl.BlockSpec(memory_space=pl.ANY) for _ in outs),
        scratch_shapes=held + results + [pltpu.SemaphoreType.DMA((len(staged),)), pltpu.SemaphoreType.DMA((out_count,))] + list(scratch),
        compiler_params=pltpu.CompilerParams(vmem_limit_bytes=limit),
        cost_estimate=pl.CostEstimate(flops=1, bytes_accessed=int(WEIGHT * weight) + 1, transcendentals=0),
    )(*[each.array if isinstance(each, Rows) else each for each in operands])


def columns_of(ids):
    count = ids.shape[1]
    row = lax.broadcasted_iota(jnp.int32, (count, count), 0)
    col = lax.broadcasted_iota(jnp.int32, (count, count), 1)
    return dot_last((row == col).astype(BF16), ids.astype(F32).astype(BF16)).astype(jnp.int32)


def choices(ids, experts):
    lane = lax.broadcasted_iota(jnp.int32, (ids.shape[0], experts), 1)
    return (ids[:, 0:1] == lane).astype(F32), (ids[:, 1:2] == lane).astype(F32)


def placements(ids, chip, near, capacity):
    count = ids.shape[0]
    first, second = choices(ids ^ chip, near)
    named = (first + second).astype(BF16)
    row = lax.broadcasted_iota(jnp.int32, (count, count), 0)
    col = lax.broadcasted_iota(jnp.int32, (count, count), 1)
    before = dot((col < row).astype(BF16), named)
    start = lax.broadcasted_iota(jnp.int32, (count, near), 1).astype(F32) * capacity
    place = before + start + 1.0
    slot = lax.broadcasted_iota(jnp.int32, (count, near * capacity), 1)
    picks = []
    for chosen in (first, second):
        at = jnp.sum(chosen * place, axis=1, keepdims=True).astype(jnp.int32) - 1
        picks.append((slot == at).astype(BF16))
    return picks


def picks_of(names, count, chip, near, capacity):
    first, second = placements(columns_of(ids_of(names, count)), chip[0], near, capacity)
    return first + second


def pack_rows(picks, rows, outs):
    capacity = outs[0].shape[0]
    packed = dot_first(picks, rows).astype(BF16)
    for place, out in enumerate(outs):
        out[...] = packed[place * capacity : (place + 1) * capacity]


def pack_both_kernel(near, capacity, ins, outs, scratch, write):
    chip, names, rows, far_names, far_rows = ins
    count = rows.shape[0]
    picks = [picks_of(these[...], count, chip, near, capacity) for these in (names, far_names)]
    for block, source in enumerate((rows, far_rows)):
        packed = dot_first(picks[block], source[...]).astype(BF16)
        for place, out in enumerate(outs):
            out[block * capacity : (block + 1) * capacity, :] = packed[place * capacity : (place + 1) * capacity]


def ids_of(names, count):
    return names[:, 0:count][0:2].astype(F32).astype(jnp.int32)


def all_of(refs):
    return jnp.concatenate([ref[...] for ref in refs], axis=0)


def shifted(pad_ref, lanes, count):
    for rest in range(8):
        block = pad_ref[pl.ds(rest, count + 24), lanes]
        for turn in range(4):
            offset = 8 * turn + rest
            if 1 <= offset <= KSIZE:
                yield offset, block[8 * turn : 8 * turn + count]


def fill_padded(pad_ref, core, twin, mid, other):
    count = mid.shape[0]
    after = RIM + count
    pad_ref[pl.ds(pl.multiple_of((1 - core) * after, 8), RIM), :] = twin[...].astype(F32)
    pad_ref[RIM:after, :] = mid[...].astype(F32)
    pad_ref[pl.ds(pl.multiple_of(core * after, 8), RIM), :] = other[...].astype(F32)


def lane_loop(width, body):
    @pl.loop(0, width // LANES)
    def _(step):
        body(pl.ds(pl.multiple_of(step * LANES, LANES), LANES))


def convolve_and_norm(core, frames, twin, other, taps, gain, conv_ref, normed_ref, scratch):
    pad_ref, taps32_ref, mixed_ref, square_ref = scratch
    count, width = frames.shape
    fill_padded(pad_ref, core, twin, frames, other)
    taps32_ref[...] = taps[...].astype(F32)
    square_ref[...] = jnp.zeros_like(square_ref)

    def conv(lanes):
        total = jnp.zeros((count, LANES), F32)
        for offset, rows in shifted(pad_ref, lanes, count):
            total = total + taps32_ref[offset - 1 : offset, lanes] * rows
        if conv_ref is not None:
            conv_ref[:, lanes] = total
        mixed = pad_ref[RIM : RIM + count, lanes] + total * jax.nn.sigmoid(total)
        mixed_ref[:, lanes] = mixed
        square_ref[...] += mixed * mixed

    lane_loop(width, conv)
    mean = jnp.sum(square_ref[...], axis=1, keepdims=True) / width
    inverse = lax.rsqrt(mean + NORM_EPS)
    normed_ref[...] = (mixed_ref[...] * inverse * gain[...].astype(F32)[0:1]).astype(BF16)


def front_kernel(near, capacity, ins, outs, scratch, write):
    chip, core, frames, twin, other, taps, gain, names = ins
    conv, normed, parts = outs[0], outs[1], outs[2:]
    picks_ref, scratch = scratch[0], scratch[1:]
    picks_ref[...] = picks_of(names[...], frames.shape[0], chip, near, capacity)
    convolve_and_norm(core[0], frames, twin, other, taps, gain, conv, normed, scratch)
    write(0, 1)
    pack_rows(picks_ref[...], normed[...], parts)


def far_front_kernel(near, capacity, ins, outs, scratch, write):
    chip, core, frames, rims_and_names, taps, gain = ins
    names, normed, parts = outs[0], outs[1], outs[2:]
    twin, other = rims_and_names[0:RIM, :], rims_and_names[RIM : 2 * RIM, :]
    even = core[0] == 0
    first = jnp.where(even, twin.astype(F32)[RIM - 1 : RIM], twin.astype(F32)[0:1])
    last = jnp.where(even, other.astype(F32)[0:1], other.astype(F32)[RIM - 1 : RIM])
    names[...] = jnp.concatenate([first, last, jnp.zeros((RIM - 2, frames.shape[1]), F32)], axis=0).astype(BF16)
    picks_ref, scratch = scratch[0], scratch[1:]
    picks_ref[...] = picks_of(names[...], frames.shape[0], chip, near, capacity)
    convolve_and_norm(core[0], frames, twin, other, taps, gain, None, normed, scratch)
    write(0, 1)
    pack_rows(picks_ref[...], normed[...], parts)


def result_kernel(near, capacity, ins, outs, scratch, write):
    chip, router, blocks, rows_refs = ins[0], ins[1], (ins[2:4], ins[4:6]), ins[6:]
    for block, (names, normed) in reversed(list(enumerate(blocks))):
        ids = columns_of(ids_of(names[...], normed.shape[0]))
        gates = jax.nn.sigmoid(dot_last(normed[...], router[...]))
        rows = jnp.concatenate([ref[block * capacity : (block + 1) * capacity, :] for ref in rows_refs], axis=0)
        added = jnp.zeros(outs[block].shape, F32)
        for pick, chosen in zip(placements(ids, chip[0], near, capacity), choices(ids, gates.shape[1])):
            added = added + jnp.sum(chosen * gates, axis=1, keepdims=True) * dot(pick, rows)
        outs[block][...] = added.astype(outs[block].dtype)
        write(block)


def block_kernel(ins, outs, scratch, write):
    near_sum, mixed, far_sum = ins
    outs[0][...] = (mixed[...] + (near_sum[...] + far_sum[...].astype(F32))).astype(BF16)


def back_kernel(near, capacity, ins, outs, scratch, write):
    chip, names, rows_refs = ins[0], ins[1], ins[2:]
    count = outs[0].shape[0]
    first, second = placements(columns_of(ids_of(names[...], count)), chip[0], near, capacity)
    outs[0][...] = dot(first + second, all_of(rows_refs)).astype(outs[0].dtype)


def half_lanes(core, width):
    return pl.ds(pl.multiple_of(core * (width // 2), LANES), width // 2)


def final_kernel(ins, outs, scratch, write):
    core, frames, twin, other, conv, grad, gain, router, near_back, far_back = ins
    mixed_ref, mixed_grad_ref, conv_grad_ref, twin_ref, other_ref, kept_ref, given_ref = outs
    pad_ref, local_ref = scratch
    count, width = frames.shape
    fill_padded(pad_ref, core[0], twin, frames, other)
    conv_out = conv[...]
    logistic = jax.nn.sigmoid(conv_out)
    mixed = frames[...].astype(F32) + conv_out * logistic
    inverse = lax.rsqrt(jnp.sum(mixed * mixed, axis=1, keepdims=True) / width + NORM_EPS)
    local_ref[KSIZE + 1 :, :] = router[...]
    mixed_ref[...] = mixed
    write(0)
    grad_normed = near_back[...] + far_back[...].astype(F32)
    local_ref[KSIZE : KSIZE + 1, :] = jnp.sum(grad_normed * mixed * inverse, axis=0, keepdims=True)
    scaled = grad_normed * gain[...].astype(F32)[0:1]
    mean = jnp.sum(scaled * mixed, axis=1, keepdims=True) / width
    mixed_grad = grad[...].astype(F32) + inverse * scaled - mixed * (inverse * inverse * inverse * mean)
    mixed_grad_ref[...] = mixed_grad
    conv_grad = (mixed_grad * (logistic * (1.0 + conv_out * (1.0 - logistic)))).astype(BF16)
    conv_grad_ref[...] = conv_grad
    twin_ref[...] = jnp.where(core[0] == 0, conv_grad[count - RIM : count], conv_grad[0:RIM])
    other_ref[...] = jnp.where(core[0] == 0, conv_grad[0:RIM], conv_grad[count - RIM : count])
    write(1, 2, 3, 4)

    def reduce(lanes):
        grad = conv_grad_ref[:, lanes].astype(F32)
        for offset, rows in shifted(pad_ref, lanes, count):
            local_ref[offset - 1 : offset, lanes] = jnp.sum(grad * rows, axis=0, keepdims=True)

    lane_loop(width, reduce)
    kept_ref[...] = local_ref[:, half_lanes(core[0], width)]
    given_ref[...] = local_ref[:, half_lanes(1 - core[0], width)]


def frames_kernel(ins, outs, scratch, write):
    core, mixed_grad, conv_grad, twin, other, taps = ins
    (out_ref,), (pad_ref, taps32_ref) = outs, scratch
    count, width = mixed_grad.shape
    fill_padded(pad_ref, core[0], twin, conv_grad, other)
    taps32_ref[...] = taps[...].astype(F32)
    mixed_grad.wait()

    def conv(lanes):
        total = mixed_grad[:, lanes]
        for offset, rows in shifted(pad_ref, lanes, count):
            total = total + taps32_ref[KSIZE - offset : KSIZE - offset + 1, lanes] * rows
        out_ref[:, lanes] = total.astype(BF16)

    lane_loop(width, conv)


def chunks(width):
    return [slice(start, start + CHUNK) for start in range(0, width, CHUNK)]


def gather_rows(refs, rows_ref):
    each = refs[0].shape[0]
    for place, ref in enumerate(refs):
        rows_ref[place * each : (place + 1) * each, :] = ref[...]


def gather_pairs(refs, rows_ref):
    each = refs[0].shape[0] // 2
    for place, ref in enumerate(refs):
        for block, start in enumerate((place * each, (len(refs) + place) * each)):
            rows_ref[start : start + each, :] = ref[block * each : (block + 1) * each, :]


def scatter_columns(refs, columns, values):
    each = refs[0].shape[0]
    for place, ref in enumerate(refs):
        ref[:, columns] = values[place * each : (place + 1) * each]


def scatter_pairs(refs, columns, values):
    each = refs[0].shape[0] // 2
    for place, ref in enumerate(refs):
        for block, start in enumerate((place * each, (len(refs) + place) * each)):
            ref[block * each : (block + 1) * each, columns] = values[start : start + each]


def forward_kernel(near, ins, outs, scratch, write):
    chip, rows, (router, near_in, far_in, near_out, far_out) = ins[0], ins[1 : 2 * near + 1], ins[2 * near + 1 :]
    out_refs, (sent, near_slope, far_slope, near_active, gate_ref) = outs[0:near], outs[near:]
    count = near_slope.shape[0]
    rows_part, active_part = slice(0, count), slice(count, 2 * count)
    gather_rows(rows, sent)
    logits = dot_last(sent[rows_part, :], router[...])
    mine = lax.broadcasted_iota(jnp.int32, logits.shape, 1) == chip[0]
    gate = jax.nn.sigmoid(jnp.sum(jnp.where(mine, logits, 0.0), axis=1, keepdims=True))
    gate_ref[...] = jnp.broadcast_to(gate, gate_ref.shape)
    near_in.wait()
    near_out.start()
    far_out.start()
    for weight, slope, active, part in (
        (near_in, near_slope, near_active, slice(None)),
        (far_in, far_slope, sent, active_part),
    ):
        weight.wait()
        for columns in chunks(weight.shape[1]):
            values = dot(sent[rows_part, :], weight[:, columns])
            logistic = jax.nn.sigmoid(values)
            active[part, columns] = (values * logistic).astype(BF16)
            slope[:, columns] = (logistic * (1.0 + values * (1.0 - logistic))).astype(BF16)
    write(near, near + 1, near + 2, near + 3, near + 4)
    near_out.wait()
    far_out.wait()
    for columns in chunks(near_out.shape[1]):
        total = dot(near_active[...], near_out[:, columns])
        total = total + dot(sent[active_part, :], far_out[:, columns])
        scatter_pairs(out_refs, columns, total.astype(BF16))


def backward_kernel(near, ins, outs, scratch, write):
    chip, grads, rest = ins[0], ins[1 : near + 1], ins[near + 1 :]
    gate_ref, near_out, near_slope, near_active, far_out, far_slope, far_active, near_in, far_in, router, rows = rest
    out_refs, (near_grad, sent, router_out) = outs[0 : 2 * near], outs[2 * near :]
    grads_ref, dots_ref = scratch
    count = rows.shape[0]
    grads_part, pre_part = slice(0, count), slice(count, 2 * count)
    gather_pairs(grads, grads_ref)
    gate = gate_ref[...][:, 0:1]
    sent[grads_part, :] = (gate * grads_ref[...].astype(F32)).astype(BF16)
    near_out.wait()
    for later in rest[2:]:
        later.start()
    dots_ref[...] = jnp.zeros_like(dots_ref)
    for weight, slope, active, grad, part in (
        (near_out, near_slope, near_active, near_grad, slice(None)),
        (far_out, far_slope, far_active, sent, pre_part),
    ):
        for ref in (weight, slope, active):
            ref.wait()
        for columns in chunks(weight.shape[0]):
            hidden = dot_last(sent[grads_part, :], weight[columns, :])
            product = hidden * active[:, columns].astype(F32)
            dots_ref[...] += sum(product[:, at : at + LANES] for at in range(0, CHUNK, LANES))
            grad[part, columns] = (hidden * slope[:, columns].astype(F32)).astype(BF16)
    write(2 * near, 2 * near + 1)
    chosen = (jnp.sum(dots_ref[...], axis=1, keepdims=True) * (1.0 - gate)).astype(BF16)
    experts = router_out.shape[0]
    mine = lax.broadcasted_iota(jnp.int32, (count, experts), 1) == chip[0]
    router_out[...] = dot_first(jnp.where(mine, chosen.astype(F32), 0.0).astype(BF16), rows[...])
    own = lax.broadcasted_iota(jnp.int32, router.shape, 0) == chip[0]
    router_row = jnp.sum(jnp.where(own, router[...].astype(F32), 0.0), axis=0, keepdims=True)
    chosen = chosen.astype(F32)
    near_in.wait()
    far_in.wait()
    for columns in chunks(near_in.shape[0]):
        total = dot_last(near_grad[...], near_in[columns, :])
        total = total + dot_last(sent[pre_part, :], far_in[columns, :])
        total = total + chosen * router_row[:, columns]
        scatter_columns(out_refs, columns, total.astype(BF16))


def weights_kernel(ins, outs, scratch, write):
    near_active, near_grads, far_active, far_grads, near_rows, near_grad, far_rows, far_grad = ins
    in_grad, out_grad = outs
    for turn, (a, b, c, d) in ((1, ins[0:4]), (0, ins[4:8])):
        for ref in (a, b, c, d):
            ref.wait()
        for ref in ins[4:8]:
            ref.start()
        for columns in chunks(a.shape[1]):
            total = dot_first(a[:, columns], b[...]) + dot_first(c[:, columns], d[...])
            outs[turn][columns, :] = total.astype(BF16)
        write(turn)


def last_kernel(ins, outs, scratch, write):
    core, mine, other = ins
    taps_ref, gain_ref, router_ref = outs
    width = taps_ref.shape[1]
    for place, half in ((core[0], mine), (1 - core[0], other)):
        lanes = half_lanes(place, width)
        taps_ref[:, lanes] = half[0:KSIZE]
        gain_ref[:, lanes] = half[KSIZE : KSIZE + 1]
        router_ref[:, lanes] = half[KSIZE + 1 :]


def pair_up(values, count):
    pairs = [(i, i + 1) for i in range(1, count - 1, 2)]
    return lax.ppermute(values, "seq", pairs + [(j, i) for i, j in pairs])


def swap(values, count, bit):
    return lax.ppermute(values, "seq", [(i, i ^ bit) for i in range(count)])


def exchange(parts, devices):
    return [parts[0]] + [swap(part, devices, 2 * r) for r, part in enumerate(parts) if r]


def per_device(frames, conv_kernel, norm_gain, router, expert_in, expert_out, expert_ids, out_grad):
    count, width = frames.shape
    devices = lax.axis_size("seq")
    experts = devices // 2
    capacity = 8 * count // devices
    near = experts // 2
    slots = experts * capacity
    gain_at, router_at, router_rows = 2 * RIM, 3 * RIM, -(-experts // RIM) * RIM
    params = jnp.concatenate(
        [
            jnp.pad(conv_kernel, ((0, gain_at - KSIZE), (0, 0))),
            jnp.pad(norm_gain.reshape(1, width), ((0, RIM - 1), (0, 0))),
            jnp.pad(router.T, ((0, router_rows - experts), (0, 0))),
        ]
    )
    taps, gain = Rows(params, 0, gain_at), Rows(params, gain_at, RIM)
    router = Rows(params, router_at, router_rows)
    ids = expert_ids.T
    shape = jax.ShapeDtypeStruct
    pad = pltpu.VMEM((count + 2 * RIM, width), F32)
    taps32 = pltpu.VMEM((KSIZE + 1, width), F32)
    chip = lax.axis_index("seq") // 2
    chips = chip.reshape(1).astype(jnp.int32)
    cross = functools.partial(swap, count=devices, bit=devices // 2)

    core = lax.axis_index("seq") % 2
    cores = core.reshape(1).astype(jnp.int32)
    ends = (frames[count - RIM : count], frames[0:RIM])
    frames, to_twin, to_other = lax.optimization_barrier(
        (frames, jnp.where(core == 0, *ends), jnp.where(core == 0, *ends[::-1]))
    )
    twin, other = swap(to_twin, devices, 1), pair_up(to_other, devices)
    far_frames = cross(frames)
    names = jnp.pad(ids.astype(BF16), ((0, RIM - 2), (0, width - count)))
    weight_in, weight_out = expert_in[0], expert_out[0]
    other_in = swap(weight_in, devices, 1)
    other_out = swap(weight_out, devices, 1)
    twin, other, other_in, other_out = lax.optimization_barrier((twin, other, other_in, other_out))

    model32, model16 = shape((count, width), F32), shape((count, width), BF16)
    part = (shape((capacity, width), BF16),) * near
    pair = (shape((2 * capacity, width), BF16),) * near
    even = jnp.concatenate([twin[: RIM - 1], names[0:1], names[1:2], other[1:]])
    odd = jnp.concatenate([names[0:1], twin[1:], other[: RIM - 1], names[1:2]])
    far_rims = cross(jnp.where(core == 0, even, odd))
    front_scratch = (pltpu.VMEM((count, near * capacity), BF16), pad, taps32)
    front_scratch += (pltpu.VMEM((count, width), F32), pltpu.VMEM((count, LANES), F32))
    conv_out, normed, *parts = kernel_call(
        functools.partial(front_kernel, near, capacity),
        (chips, cores, frames, twin, other, taps, gain, names),
        (model32, model16, *part),
        front_scratch,
        weight=FRONT,
        limit=LARGE,
        scalars=(0, 1),
    )
    rows = exchange(parts, devices)
    far_rims, far_frames, out_grad = lax.optimization_barrier((far_rims, far_frames, out_grad))
    far_grad = cross(out_grad)
    far_names, far_normed, *parts = kernel_call(
        functools.partial(far_front_kernel, near, capacity),
        (chips, cores, far_frames, far_rims, taps, gain),
        (shape((RIM, width), BF16), model16, *part),
        front_scratch,
        limit=LARGE,
        scalars=(0, 1),
    )
    rows, parts = lax.optimization_barrier((rows, parts))
    far_rows = exchange(parts, devices)
    parts = kernel_call(
        functools.partial(pack_both_kernel, near, capacity),
        (chips, names, out_grad, far_names, far_grad),
        pair,
        limit=LARGE,
        scalars=(0,),
    )
    far_rows, parts = lax.optimization_barrier((far_rows, parts))
    rows, grads = rows + far_rows, exchange(parts, devices)

    narrow = shape((slots, weight_in.shape[1]), BF16)
    *parts, sent, near_slope, far_slope, near_active, gate = kernel_call(
        functools.partial(forward_kernel, near),
        (chips, *rows, router, weight_in, other_in, weight_out, other_out),
        pair + (shape((2 * slots, width), BF16), narrow, narrow, narrow, shape((slots, LANES), F32)),
        limit=LARGE,
        scalars=(0,),
    )
    results = exchange(parts, devices)
    all_rows, far_active = Rows(sent, 0, slots), Rows(sent, slots, slots)
    outs = kernel_call(
        functools.partial(backward_kernel, near),
        (chips, *grads, gate, weight_out, near_slope, near_active, other_out, far_slope, far_active)
        + (weight_in, other_in, router, all_rows),
        2 * part + (narrow, shape((2 * slots, width), BF16), shape((experts, width), F32)),
        (pltpu.VMEM((slots, width), BF16), pltpu.VMEM((slots, LANES), F32)),
        limit=LARGE,
        scalars=(0,),
    )
    results, outs, sent = lax.optimization_barrier((results, outs, sent))
    own_in, far_in, (near_grad, sent_grads, router_local) = outs[0:near], outs[near : 2 * near], outs[2 * near :]
    backs = exchange(far_in, devices)
    near_sum, far_sum = kernel_call(
        functools.partial(result_kernel, near, capacity),
        (chips, router, names, normed, far_names, far_normed, *results),
        (model32, model16),
        weight=2.4,
        scalars=(0,),
    )
    come, come_grads = swap(sent, devices, 1), swap(sent_grads, devices, 1)
    backs[1], own_in, come, come_grads = lax.optimization_barrier((backs[1], own_in, come, come_grads))
    own_backs = exchange(own_in, devices)
    backs, near_sum, far_sum = lax.optimization_barrier((backs, near_sum, far_sum))
    (far_back,) = kernel_call(
        functools.partial(back_kernel, near, capacity), (chips, far_names, *backs), (model16,), scalars=(0,)
    )
    far_back, far_sum = lax.optimization_barrier((far_back, far_sum))
    far_back = cross(far_back)
    grad = shape(weight_in.shape, BF16)
    first, second = (functools.partial(Rows, start=start, size=slots) for start in (0, slots))
    expert_in_grad, expert_out_grad = kernel_call(
        weights_kernel,
        (near_active, first(sent_grads), second(come), first(come_grads))
        + (first(sent), near_grad, first(come), second(come_grads)),
        (grad, grad),
        limit=WEIGHTS,
    )
    backs, expert_in_grad, expert_out_grad = lax.optimization_barrier(
        (own_backs, expert_in_grad, expert_out_grad)
    )
    (near_back,) = kernel_call(
        functools.partial(back_kernel, near, capacity), (chips, names, *backs), (model32,), scalars=(0,)
    )
    far_back, expert_in_grad, expert_out_grad = lax.optimization_barrier((far_back, expert_in_grad, expert_out_grad))
    far_sum = cross(far_sum)

    rim = shape((RIM, width), BF16)
    lines = KSIZE + 1 + experts
    columns = shape((lines, width // 2), F32)
    mixed, mixed_grad, conv_grad, to_twin, to_other, kept, given = kernel_call(
        final_kernel,
        (cores, frames, twin, other, conv_out, out_grad, gain, router_local, near_back, far_back),
        (model32, model32, model16, rim, rim, columns, columns),
        (pad, pltpu.VMEM((lines, width), F32)),
        weight=0.0,
        scalars=(0,),
    )
    grad_twin, grad_other = swap(to_twin, devices, 1), pair_up(to_other, devices)
    local = kept + swap(given, devices, 1)
    bit = 2
    while bit < devices:
        last = 4 * bit > devices
        others = [swap(local, devices, step) for step in ((bit,) if last else (bit, 2 * bit, 3 * bit))]
        if bit == 2:
            others, grad_twin, grad_other, far_sum = lax.optimization_barrier((others, grad_twin, grad_other, far_sum))
            (block_out,) = kernel_call(block_kernel, (near_sum, mixed, far_sum), (model16,))
            (frames_grad,) = kernel_call(
                frames_kernel,
                (cores, mixed_grad, conv_grad, grad_twin, grad_other, taps),
                (model16,),
                (pad, taps32),
                scalars=(0,),
            )
        bit *= 2 if last else 4
        if bit == devices:
            others, frames_grad = lax.optimization_barrier((others, frames_grad))
        local = local + others[0] if last else (local + others[0]) + (others[1] + others[2])
    kernel_grad, gain_grad, router_grad = kernel_call(
        last_kernel,
        (cores, local, swap(local, devices, 1)),
        (shape((KSIZE, width), F32), shape((1, width), F32), shape((experts, width), F32)),
        weight=0.0,
        scalars=(0,),
    )
    return (
        block_out,
        frames_grad,
        kernel_grad,
        gain_grad[0],
        router_grad.T,
        expert_in_grad[None],
        expert_out_grad[None],
    )


def solution(mesh):
    in_specs = (
        P(("groups", "seq"), None),
        P(),
        P(),
        P(),
        P("seq", None, None),
        P("seq", None, None),
        P(("groups", "seq"), None),
        P(("groups", "seq"), None),
    )
    out_specs = (
        P(("groups", "seq"), None),
        P(("groups", "seq"), None),
        P("groups", None),
        P("groups"),
        P("groups", None),
        P(("groups", "seq"), None, None),
        P(("groups", "seq"), None, None),
    )
    return jax.shard_map(
        per_device, mesh=mesh, in_specs=in_specs, out_specs=out_specs, check_vma=False
    )
```

```python
import functools

import jax
import jax.numpy as jnp
from jax import lax
from jax.experimental import pallas as pl
from jax.experimental.pallas import tpu as pltpu
from jax.sharding import PartitionSpec as P

KSIZE = 31
RIM = 16
LANES = 128
CHUNK = 256
NORM_EPS = 1e-05
F32 = jnp.float32
BF16 = jnp.bfloat16
LAST = (((1,), (1,)), ((), ()))
FIRST = (((0,), (0,)), ((), ()))
SMALL = 12 * 1024 * 1024
LARGE = 60 * 1024 * 1024
WEIGHTS = 24 * 1024 * 1024
FRONT = 3.3
WEIGHT = 0.15 * 3.6e6


def dot(a, b):
    return jnp.dot(a, b, preferred_element_type=F32)


def dot_last(a, b):
    return lax.dot_general(a, b, LAST, preferred_element_type=F32)


def dot_first(a, b):
    return lax.dot_general(a, b, FIRST, preferred_element_type=F32)


def slope_of(values):
    logistic = jax.nn.sigmoid(values)
    return logistic * (1.0 + values * (1.0 - logistic))


class Staged:
    def __init__(self, source, held, semaphore):
        self.held, self.copy = held, pltpu.make_async_copy(source, held, semaphore)
        self.shape, self.started, self.waited = held.shape, False, False

    def start(self):
        if not self.started:
            self.copy.start()
        self.started = True

    def wait(self):
        self.start()
        if not self.waited:
            self.copy.wait()
        self.waited = True

    def __getitem__(self, at):
        self.wait()
        return self.held[at]


class Rows:
    def __init__(self, array, start, size):
        self.array, self.start, self.shape, self.dtype = array, start, (size, array.shape[1]), array.dtype

    def of(self, ref):
        return ref.at[pl.ds(self.start, self.shape[0])]


def kernel_call(body, operands, outs, scratch=(), weight=0.0, limit=SMALL, scalars=(), first=None):
    count, out_count = len(operands), len(outs)
    staged = [place for place in range(count) if place not in scalars]
    held = [pltpu.VMEM(operands[place].shape, operands[place].dtype) for place in staged]
    results = [pltpu.VMEM(out.shape, out.dtype) for out in outs]

    def kernel(*refs):
        ins, out_refs, rest = refs[0:count], refs[count : count + out_count], refs[count + out_count :]
        copies, made, rest = rest[0 : len(staged)], rest[len(staged) : len(staged) + out_count], rest[len(staged) + out_count :]
        in_semaphores, out_semaphores, rest = rest[0], rest[1], rest[2:]
        values = list(ins)
        for turn, place in enumerate(staged):
            source = operands[place].of(ins[place]) if isinstance(operands[place], Rows) else ins[place]
            values[place] = Staged(source, copies[turn], in_semaphores.at[turn])
            if first is None or place < first:
                values[place].start()
        writes = [
            pltpu.make_async_copy(buffer, out, out_semaphores.at[turn])
            for turn, (buffer, out) in enumerate(zip(made, out_refs))
        ]
        started = []

        def write(*turns):
            for turn in turns:
                writes[turn].start()
                started.append(turn)

        body(values, made, rest, write)
        for value in values:
            if isinstance(value, Staged):
                value.wait()
        write(*[turn for turn in range(out_count) if turn not in started])
        for copy in writes:
            copy.wait()

    return pl.pallas_call(
        kernel,
        out_shape=tuple(outs),
        in_specs=[pl.BlockSpec(memory_space=pltpu.SMEM if place in scalars else pl.ANY) for place in range(count)],
        out_specs=tuple(pl.BlockSpec(memory_space=pl.ANY) for _ in outs),
        scratch_shapes=held + results + [pltpu.SemaphoreType.DMA((len(staged),)), pltpu.SemaphoreType.DMA((out_count,))] + list(scratch),
        compiler_params=pltpu.CompilerParams(vmem_limit_bytes=limit),
        cost_estimate=pl.CostEstimate(flops=1, bytes_accessed=int(WEIGHT * weight) + 1, transcendentals=0),
    )(*[each.array if isinstance(each, Rows) else each for each in operands])


def columns_of(ids):
    count = ids.shape[1]
    row = lax.broadcasted_iota(jnp.int32, (count, count), 0)
    col = lax.broadcasted_iota(jnp.int32, (count, count), 1)
    return dot_last((row == col).astype(BF16), ids.astype(F32).astype(BF16)).astype(jnp.int32)


def choices(ids, experts):
    lane = lax.broadcasted_iota(jnp.int32, (ids.shape[0], experts), 1)
    return (ids[:, 0:1] == lane).astype(F32), (ids[:, 1:2] == lane).astype(F32)


def placements(ids, chip, near, capacity):
    count = ids.shape[0]
    first, second = choices(ids ^ chip, near)
    named = (first + second).astype(BF16)
    row = lax.broadcasted_iota(jnp.int32, (count, count), 0)
    col = lax.broadcasted_iota(jnp.int32, (count, count), 1)
    before = dot((col < row).astype(BF16), named)
    start = lax.broadcasted_iota(jnp.int32, (count, near), 1).astype(F32) * capacity
    place = before + start + 1.0
    slot = lax.broadcasted_iota(jnp.int32, (count, near * capacity), 1)
    picks = []
    for chosen in (first, second):
        at = jnp.sum(chosen * place, axis=1, keepdims=True).astype(jnp.int32) - 1
        picks.append((slot == at).astype(BF16))
    return picks


def picks_of(names, count, chip, near, capacity):
    first, second = placements(columns_of(ids_of(names, count)), chip[0], near, capacity)
    return first + second


def pack_rows(picks, rows, outs):
    capacity = outs[0].shape[0]
    packed = dot_first(picks, rows).astype(BF16)
    for place, out in enumerate(outs):
        out[...] = packed[place * capacity : (place + 1) * capacity]


def pack_both_kernel(near, capacity, ins, outs, scratch, write):
    chip, names, rows, far_names, far_rows = ins
    count = rows.shape[0]
    picks = [picks_of(these[...], count, chip, near, capacity) for these in (names, far_names)]
    for block, source in enumerate((rows, far_rows)):
        packed = dot_first(picks[block], source[...]).astype(BF16)
        for place, out in enumerate(outs):
            out[block * capacity : (block + 1) * capacity, :] = packed[place * capacity : (place + 1) * capacity]


def ids_of(names, count):
    return names[:, 0:count][0:2].astype(F32).astype(jnp.int32)


def all_of(refs):
    return jnp.concatenate([ref[...] for ref in refs], axis=0)


def shifted(pad_ref, lanes, count):
    for rest in range(8):
        block = pad_ref[pl.ds(rest, count + 24), lanes]
        for turn in range(4):
            offset = 8 * turn + rest
            if 1 <= offset <= KSIZE:
                yield offset, block[8 * turn : 8 * turn + count]


def fill_padded(pad_ref, core, twin, mid, other):
    count = mid.shape[0]
    after = RIM + count
    pad_ref[pl.ds(pl.multiple_of((1 - core) * after, 8), RIM), :] = twin[...].astype(F32)
    pad_ref[RIM:after, :] = mid[...].astype(F32)
    pad_ref[pl.ds(pl.multiple_of(core * after, 8), RIM), :] = other[...].astype(F32)


def lane_loop(width, body):
    @pl.loop(0, width // LANES)
    def _(step):
        body(pl.ds(pl.multiple_of(step * LANES, LANES), LANES))


def convolve_and_norm(core, frames, twin, other, taps, gain, conv_ref, normed_ref, scratch):
    pad_ref, taps32_ref, mixed_ref, square_ref = scratch
    count, width = frames.shape
    fill_padded(pad_ref, core, twin, frames, other)
    taps32_ref[...] = taps[...].astype(F32)
    square_ref[...] = jnp.zeros_like(square_ref)

    def conv(lanes):
        total = jnp.zeros((count, LANES), F32)
        for offset, rows in shifted(pad_ref, lanes, count):
            total = total + taps32_ref[offset - 1 : offset, lanes] * rows
        if conv_ref is not None:
            conv_ref[:, lanes] = total
        mixed = pad_ref[RIM : RIM + count, lanes] + total * jax.nn.sigmoid(total)
        mixed_ref[:, lanes] = mixed
        square_ref[...] += mixed * mixed

    lane_loop(width, conv)
    mean = jnp.sum(square_ref[...], axis=1, keepdims=True) / width
    inverse = lax.rsqrt(mean + NORM_EPS)
    normed_ref[...] = (mixed_ref[...] * inverse * gain[...].astype(F32)[0:1]).astype(BF16)


def front_kernel(near, capacity, ins, outs, scratch, write):
    chip, core, frames, twin, other, taps, gain, names = ins
    conv, normed, parts = outs[0], outs[1], outs[2:]
    picks_ref, scratch = scratch[0], scratch[1:]
    picks_ref[...] = picks_of(names[...], frames.shape[0], chip, near, capacity)
    convolve_and_norm(core[0], frames, twin, other, taps, gain, conv, normed, scratch)
    write(0, 1)
    pack_rows(picks_ref[...], normed[...], parts)


def far_front_kernel(near, capacity, ins, outs, scratch, write):
    chip, core, frames, rims_and_names, taps, gain = ins
    names, normed, parts = outs[0], outs[1], outs[2:]
    twin, other = rims_and_names[0:RIM, :], rims_and_names[RIM : 2 * RIM, :]
    even = core[0] == 0
    first = jnp.where(even, twin.astype(F32)[RIM - 1 : RIM], twin.astype(F32)[0:1])
    last = jnp.where(even, other.astype(F32)[0:1], other.astype(F32)[RIM - 1 : RIM])
    names[...] = jnp.concatenate([first, last, jnp.zeros((RIM - 2, frames.shape[1]), F32)], axis=0).astype(BF16)
    picks_ref, scratch = scratch[0], scratch[1:]
    picks_ref[...] = picks_of(names[...], frames.shape[0], chip, near, capacity)
    convolve_and_norm(core[0], frames, twin, other, taps, gain, None, normed, scratch)
    write(0, 1)
    pack_rows(picks_ref[...], normed[...], parts)


def result_kernel(near, capacity, ins, outs, scratch, write):
    chip, router, blocks, rows_refs = ins[0], ins[1], (ins[2:4], ins[4:6]), ins[6:]
    for block, (names, normed) in reversed(list(enumerate(blocks))):
        ids = columns_of(ids_of(names[...], normed.shape[0]))
        gates = jax.nn.sigmoid(dot_last(normed[...], router[...]))
        rows = jnp.concatenate([ref[block * capacity : (block + 1) * capacity, :] for ref in rows_refs], axis=0)
        added = jnp.zeros(outs[block].shape, F32)
        for pick, chosen in zip(placements(ids, chip[0], near, capacity), choices(ids, gates.shape[1])):
            added = added + jnp.sum(chosen * gates, axis=1, keepdims=True) * dot(pick, rows)
        outs[block][...] = added.astype(outs[block].dtype)
        write(block)


def block_kernel(ins, outs, scratch, write):
    near_sum, mixed, far_sum = ins
    outs[0][...] = (mixed[...] + (near_sum[...] + far_sum[...].astype(F32))).astype(BF16)


def back_kernel(near, capacity, ins, outs, scratch, write):
    chip, names, rows_refs = ins[0], ins[1], ins[2:]
    count = outs[0].shape[0]
    first, second = placements(columns_of(ids_of(names[...], count)), chip[0], near, capacity)
    outs[0][...] = dot(first + second, all_of(rows_refs)).astype(outs[0].dtype)


def half_lanes(core, width):
    return pl.ds(pl.multiple_of(core * (width // 2), LANES), width // 2)


def final_kernel(ins, outs, scratch, write):
    core, frames, twin, other, conv, grad, gain, router, near_back, far_back = ins
    mixed_ref, mixed_grad_ref, conv_grad_ref, twin_ref, other_ref, kept_ref, given_ref = outs
    pad_ref, local_ref = scratch
    count, width = frames.shape
    fill_padded(pad_ref, core[0], twin, frames, other)
    conv_out = conv[...]
    logistic = jax.nn.sigmoid(conv_out)
    mixed = frames[...].astype(F32) + conv_out * logistic
    inverse = lax.rsqrt(jnp.sum(mixed * mixed, axis=1, keepdims=True) / width + NORM_EPS)
    local_ref[KSIZE + 1 :, :] = router[...]
    mixed_ref[...] = mixed
    write(0)
    grad_normed = near_back[...] + far_back[...].astype(F32)
    local_ref[KSIZE : KSIZE + 1, :] = jnp.sum(grad_normed * mixed * inverse, axis=0, keepdims=True)
    scaled = grad_normed * gain[...].astype(F32)[0:1]
    mean = jnp.sum(scaled * mixed, axis=1, keepdims=True) / width
    mixed_grad = grad[...].astype(F32) + inverse * scaled - mixed * (inverse * inverse * inverse * mean)
    mixed_grad_ref[...] = mixed_grad
    conv_grad = (mixed_grad * (logistic * (1.0 + conv_out * (1.0 - logistic)))).astype(BF16)
    conv_grad_ref[...] = conv_grad
    twin_ref[...] = jnp.where(core[0] == 0, conv_grad[count - RIM : count], conv_grad[0:RIM])
    other_ref[...] = jnp.where(core[0] == 0, conv_grad[0:RIM], conv_grad[count - RIM : count])
    write(1, 2, 3, 4)

    def reduce(lanes):
        grad = conv_grad_ref[:, lanes].astype(F32)
        for offset, rows in shifted(pad_ref, lanes, count):
            local_ref[offset - 1 : offset, lanes] = jnp.sum(grad * rows, axis=0, keepdims=True)

    lane_loop(width, reduce)
    kept_ref[...] = local_ref[:, half_lanes(core[0], width)]
    given_ref[...] = local_ref[:, half_lanes(1 - core[0], width)]


def frames_kernel(ins, outs, scratch, write):
    core, mixed_grad, conv_grad, twin, other, taps = ins
    (out_ref,), (pad_ref, taps32_ref) = outs, scratch
    count, width = mixed_grad.shape
    fill_padded(pad_ref, core[0], twin, conv_grad, other)
    taps32_ref[...] = taps[...].astype(F32)
    mixed_grad.wait()

    def conv(lanes):
        total = mixed_grad[:, lanes]
        for offset, rows in shifted(pad_ref, lanes, count):
            total = total + taps32_ref[KSIZE - offset : KSIZE - offset + 1, lanes] * rows
        out_ref[:, lanes] = total.astype(BF16)

    lane_loop(width, conv)


def chunks(width):
    return [slice(start, start + CHUNK) for start in range(0, width, CHUNK)]


def gather_rows(refs, rows_ref):
    each = refs[0].shape[0]
    for place, ref in enumerate(refs):
        rows_ref[place * each : (place + 1) * each, :] = ref[...]


def gather_pairs(refs, rows_ref):
    each = refs[0].shape[0] // 2
    for place, ref in enumerate(refs):
        for block, start in enumerate((place * each, (len(refs) + place) * each)):
            rows_ref[start : start + each, :] = ref[block * each : (block + 1) * each, :]


def scatter_columns(refs, columns, values):
    each = refs[0].shape[0]
    for place, ref in enumerate(refs):
        ref[:, columns] = values[place * each : (place + 1) * each]


def scatter_pairs(refs, columns, values):
    each = refs[0].shape[0] // 2
    for place, ref in enumerate(refs):
        for block, start in enumerate((place * each, (len(refs) + place) * each)):
            ref[block * each : (block + 1) * each, columns] = values[start : start + each]


def forward_kernel(near, ins, outs, scratch, write):
    chip, rows, (router, near_in, far_in, near_out, far_out) = ins[0], ins[1 : 2 * near + 1], ins[2 * near + 1 :]
    out_refs, (sent, near_slope, far_slope, near_active, gate_ref) = outs[0:near], outs[near:]
    count = near_slope.shape[0]
    rows_part, active_part = slice(0, count), slice(count, 2 * count)
    gather_rows(rows, sent)
    logits = dot_last(sent[rows_part, :], router[...])
    mine = lax.broadcasted_iota(jnp.int32, logits.shape, 1) == chip[0]
    gate = jax.nn.sigmoid(jnp.sum(jnp.where(mine, logits, 0.0), axis=1, keepdims=True))
    gate_ref[...] = jnp.broadcast_to(gate, gate_ref.shape)
    near_in.wait()
    near_out.start()
    far_out.start()
    for weight, slope, active, part in (
        (near_in, near_slope, near_active, slice(None)),
        (far_in, far_slope, sent, active_part),
    ):
        weight.wait()
        for columns in chunks(weight.shape[1]):
            values = dot(sent[rows_part, :], weight[:, columns])
            logistic = jax.nn.sigmoid(values)
            active[part, columns] = (values * logistic).astype(BF16)
            slope[:, columns] = (logistic * (1.0 + values * (1.0 - logistic))).astype(BF16)
    write(near, near + 1, near + 2, near + 3, near + 4)
    near_out.wait()
    far_out.wait()
    for columns in chunks(near_out.shape[1]):
        total = dot(near_active[...], near_out[:, columns])
        total = total + dot(sent[active_part, :], far_out[:, columns])
        scatter_pairs(out_refs, columns, total.astype(BF16))


def backward_kernel(near, ins, outs, scratch, write):
    chip, grads, rest = ins[0], ins[1 : near + 1], ins[near + 1 :]
    gate_ref, near_out, near_slope, near_active, far_out, far_slope, far_active, near_in, far_in, router, rows = rest
    out_refs, (near_grad, sent, router_out) = outs[0 : 2 * near], outs[2 * near :]
    grads_ref, dots_ref = scratch
    count = rows.shape[0]
    grads_part, pre_part = slice(0, count), slice(count, 2 * count)
    gather_pairs(grads, grads_ref)
    gate = gate_ref[...][:, 0:1]
    sent[grads_part, :] = (gate * grads_ref[...].astype(F32)).astype(BF16)
    near_out.wait()
    for later in rest[2:]:
        later.start()
    dots_ref[...] = jnp.zeros_like(dots_ref)
    for weight, slope, active, grad, part in (
        (near_out, near_slope, near_active, near_grad, slice(None)),
        (far_out, far_slope, far_active, sent, pre_part),
    ):
        for ref in (weight, slope, active):
            ref.wait()
        for columns in chunks(weight.shape[0]):
            hidden = dot_last(sent[grads_part, :], weight[columns, :])
            product = hidden * active[:, columns].astype(F32)
            dots_ref[...] += sum(product[:, at : at + LANES] for at in range(0, CHUNK, LANES))
            grad[part, columns] = (hidden * slope[:, columns].astype(F32)).astype(BF16)
    write(2 * near, 2 * near + 1)
    chosen = (jnp.sum(dots_ref[...], axis=1, keepdims=True) * (1.0 - gate)).astype(BF16)
    experts = router_out.shape[0]
    mine = lax.broadcasted_iota(jnp.int32, (count, experts), 1) == chip[0]
    router_out[...] = dot_first(jnp.where(mine, chosen.astype(F32), 0.0).astype(BF16), rows[...])
    own = lax.broadcasted_iota(jnp.int32, router.shape, 0) == chip[0]
    router_row = jnp.sum(jnp.where(own, router[...].astype(F32), 0.0), axis=0, keepdims=True)
    chosen = chosen.astype(F32)
    near_in.wait()
    far_in.wait()
    for columns in chunks(near_in.shape[0]):
        total = dot_last(near_grad[...], near_in[columns, :])
        total = total + dot_last(sent[pre_part, :], far_in[columns, :])
        total = total + chosen * router_row[:, columns]
        scatter_columns(out_refs, columns, total.astype(BF16))


def weights_kernel(ins, outs, scratch, write):
    near_active, near_grads, far_active, far_grads, near_rows, near_grad, far_rows, far_grad = ins
    in_grad, out_grad = outs
    for turn, (a, b, c, d) in ((1, ins[0:4]), (0, ins[4:8])):
        for ref in (a, b, c, d):
            ref.wait()
        for ref in ins[4:8]:
            ref.start()
        for columns in chunks(a.shape[1]):
            total = dot_first(a[:, columns], b[...]) + dot_first(c[:, columns], d[...])
            outs[turn][columns, :] = total.astype(BF16)
        write(turn)


def last_kernel(ins, outs, scratch, write):
    core, mine, other = ins
    taps_ref, gain_ref, router_ref = outs
    width = taps_ref.shape[1]
    for place, half in ((core[0], mine), (1 - core[0], other)):
        lanes = half_lanes(place, width)
        taps_ref[:, lanes] = half[0:KSIZE]
        gain_ref[:, lanes] = half[KSIZE : KSIZE + 1]
        router_ref[:, lanes] = half[KSIZE + 1 :]


def pair_up(values, count):
    pairs = [(i, i + 1) for i in range(1, count - 1, 2)]
    return lax.ppermute(values, "seq", pairs + [(j, i) for i, j in pairs])


def swap(values, count, bit):
    return lax.ppermute(values, "seq", [(i, i ^ bit) for i in range(count)])


def exchange(parts, devices):
    return [parts[0]] + [swap(part, devices, 2 * r) for r, part in enumerate(parts) if r]


def per_device(frames, conv_kernel, norm_gain, router, expert_in, expert_out, expert_ids, out_grad):
    count, width = frames.shape
    devices = lax.axis_size("seq")
    experts = devices // 2
    capacity = 8 * count // devices
    near = experts // 2
    slots = experts * capacity
    gain_at, router_at, router_rows = 2 * RIM, 3 * RIM, -(-experts // RIM) * RIM
    params = jnp.concatenate(
        [
            jnp.pad(conv_kernel, ((0, gain_at - KSIZE), (0, 0))),
            jnp.pad(norm_gain.reshape(1, width), ((0, RIM - 1), (0, 0))),
            jnp.pad(router.T, ((0, router_rows - experts), (0, 0))),
        ]
    )
    taps, gain = Rows(params, 0, gain_at), Rows(params, gain_at, RIM)
    router = Rows(params, router_at, router_rows)
    ids = expert_ids.T
    shape = jax.ShapeDtypeStruct
    pad = pltpu.VMEM((count + 2 * RIM, width), F32)
    taps32 = pltpu.VMEM((KSIZE + 1, width), F32)
    chip = lax.axis_index("seq") // 2
    chips = chip.reshape(1).astype(jnp.int32)
    cross = functools.partial(swap, count=devices, bit=devices // 2)

    core = lax.axis_index("seq") % 2
    cores = core.reshape(1).astype(jnp.int32)
    ends = (frames[count - RIM : count], frames[0:RIM])
    frames, to_twin, to_other = lax.optimization_barrier(
        (frames, jnp.where(core == 0, *ends), jnp.where(core == 0, *ends[::-1]))
    )
    twin, other = swap(to_twin, devices, 1), pair_up(to_other, devices)
    far_frames = cross(frames)
    names = jnp.pad(ids.astype(BF16), ((0, RIM - 2), (0, width - count)))
    weight_in, weight_out = expert_in[0], expert_out[0]
    other_in = swap(weight_in, devices, 1)
    other_out = swap(weight_out, devices, 1)
    twin, other, other_in, other_out = lax.optimization_barrier((twin, other, other_in, other_out))

    model32, model16 = shape((count, width), F32), shape((count, width), BF16)
    part = (shape((capacity, width), BF16),) * near
    pair = (shape((2 * capacity, width), BF16),) * near
    even = jnp.concatenate([twin[: RIM - 1], names[0:1], names[1:2], other[1:]])
    odd = jnp.concatenate([names[0:1], twin[1:], other[: RIM - 1], names[1:2]])
    far_rims = cross(jnp.where(core == 0, even, odd))
    front_scratch = (pltpu.VMEM((count, near * capacity), BF16), pad, taps32)
    front_scratch += (pltpu.VMEM((count, width), F32), pltpu.VMEM((count, LANES), F32))
    conv_out, normed, *parts = kernel_call(
        functools.partial(front_kernel, near, capacity),
        (chips, cores, frames, twin, other, taps, gain, names),
        (model32, model16, *part),
        front_scratch,
        weight=FRONT,
        limit=LARGE,
        scalars=(0, 1),
    )
    rows = exchange(parts, devices)
    far_rims, far_frames, out_grad = lax.optimization_barrier((far_rims, far_frames, out_grad))
    far_grad = cross(out_grad)
    far_names, far_normed, *parts = kernel_call(
        functools.partial(far_front_kernel, near, capacity),
        (chips, cores, far_frames, far_rims, taps, gain),
        (shape((RIM, width), BF16), model16, *part),
        front_scratch,
        limit=LARGE,
        scalars=(0, 1),
    )
    rows, parts = lax.optimization_barrier((rows, parts))
    far_rows = exchange(parts, devices)
    parts = kernel_call(
        functools.partial(pack_both_kernel, near, capacity),
        (chips, names, out_grad, far_names, far_grad),
        pair,
        limit=LARGE,
        scalars=(0,),
    )
    far_rows, parts = lax.optimization_barrier((far_rows, parts))
    rows, grads = rows + far_rows, exchange(parts, devices)

    narrow = shape((slots, weight_in.shape[1]), BF16)
    *parts, sent, near_slope, far_slope, near_active, gate = kernel_call(
        functools.partial(forward_kernel, near),
        (chips, *rows, router, weight_in, other_in, weight_out, other_out),
        pair + (shape((2 * slots, width), BF16), narrow, narrow, narrow, shape((slots, LANES), F32)),
        limit=LARGE,
        scalars=(0,),
    )
    results = exchange(parts, devices)
    all_rows, far_active = Rows(sent, 0, slots), Rows(sent, slots, slots)
    outs = kernel_call(
        functools.partial(backward_kernel, near),
        (chips, *grads, gate, weight_out, near_slope, near_active, other_out, far_slope, far_active)
        + (weight_in, other_in, router, all_rows),
        2 * part + (narrow, shape((2 * slots, width), BF16), shape((experts, width), F32)),
        (pltpu.VMEM((slots, width), BF16), pltpu.VMEM((slots, LANES), F32)),
        limit=LARGE,
        scalars=(0,),
    )
    results, outs, sent = lax.optimization_barrier((results, outs, sent))
    own_in, far_in, (near_grad, sent_grads, router_local) = outs[0:near], outs[near : 2 * near], outs[2 * near :]
    backs = exchange(far_in, devices)
    near_sum, far_sum = kernel_call(
        functools.partial(result_kernel, near, capacity),
        (chips, router, names, normed, far_names, far_normed, *results),
        (model32, model16),
        weight=2.4,
        scalars=(0,),
    )
    come, come_grads = swap(sent, devices, 1), swap(sent_grads, devices, 1)
    backs[1], own_in, come, come_grads = lax.optimization_barrier((backs[1], own_in, come, come_grads))
    own_backs = exchange(own_in, devices)
    backs, near_sum, far_sum = lax.optimization_barrier((backs, near_sum, far_sum))
    (far_back,) = kernel_call(
        functools.partial(back_kernel, near, capacity), (chips, far_names, *backs), (model16,), scalars=(0,)
    )
    far_back = cross(far_back)
    grad = shape(weight_in.shape, BF16)
    first, second = (functools.partial(Rows, start=start, size=slots) for start in (0, slots))
    expert_in_grad, expert_out_grad = kernel_call(
        weights_kernel,
        (near_active, first(sent_grads), second(come), first(come_grads))
        + (first(sent), near_grad, first(come), second(come_grads)),
        (grad, grad),
        weight=4.0,
        limit=WEIGHTS,
    )
    backs, expert_in_grad, expert_out_grad = lax.optimization_barrier(
        (own_backs, expert_in_grad, expert_out_grad)
    )
    (near_back,) = kernel_call(
        functools.partial(back_kernel, near, capacity), (chips, names, *backs), (model32,), scalars=(0,)
    )
    far_back, expert_in_grad, expert_out_grad = lax.optimization_barrier((far_back, expert_in_grad, expert_out_grad))
    far_sum = cross(far_sum)

    rim = shape((RIM, width), BF16)
    lines = KSIZE + 1 + experts
    columns = shape((lines, width // 2), F32)
    mixed, mixed_grad, conv_grad, to_twin, to_other, kept, given = kernel_call(
        final_kernel,
        (cores, frames, twin, other, conv_out, out_grad, gain, router_local, near_back, far_back),
        (model32, model32, model16, rim, rim, columns, columns),
        (pad, pltpu.VMEM((lines, width), F32)),
        weight=0.0,
        scalars=(0,),
    )
    grad_twin, grad_other = swap(to_twin, devices, 1), pair_up(to_other, devices)
    local = kept + swap(given, devices, 1)
    bit = 2
    while bit < devices:
        last = 4 * bit > devices
        others = [swap(local, devices, step) for step in ((bit,) if last else (bit, 2 * bit, 3 * bit))]
        if bit == 2:
            others, grad_twin, grad_other, far_sum = lax.optimization_barrier((others, grad_twin, grad_other, far_sum))
            (block_out,) = kernel_call(block_kernel, (near_sum, mixed, far_sum), (model16,))
            (frames_grad,) = kernel_call(
                frames_kernel,
                (cores, mixed_grad, conv_grad, grad_twin, grad_other, taps),
                (model16,),
                (pad, taps32),
                scalars=(0,),
            )
        bit *= 2 if last else 4
        if bit == devices:
            others, frames_grad = lax.optimization_barrier((others, frames_grad))
        local = local + others[0] if last else (local + others[0]) + (others[1] + others[2])
    kernel_grad, gain_grad, router_grad = kernel_call(
        last_kernel,
        (cores, local, swap(local, devices, 1)),
        (shape((KSIZE, width), F32), shape((1, width), F32), shape((experts, width), F32)),
        weight=0.0,
        scalars=(0,),
    )
    return (
        block_out,
        frames_grad,
        kernel_grad,
        gain_grad[0],
        router_grad.T,
        expert_in_grad[None],
        expert_out_grad[None],
    )


def solution(mesh):
    in_specs = (
        P(("groups", "seq"), None),
        P(),
        P(),
        P(),
        P("seq", None, None),
        P("seq", None, None),
        P(("groups", "seq"), None),
        P(("groups", "seq"), None),
    )
    out_specs = (
        P(("groups", "seq"), None),
        P(("groups", "seq"), None),
        P("groups", None),
        P("groups"),
        P("groups", None),
        P(("groups", "seq"), None, None),
        P(("groups", "seq"), None, None),
    )
    return jax.shard_map(
        per_device, mesh=mesh, in_specs=in_specs, out_specs=out_specs, check_vma=False
    )
```
